256 devices in a mesh: ctx: 64 (over y_hi, x, z), fsdp: 4 (over y_lo, core).
Axes of the slice: x: 4, y: 4 (y_hi: 2, y_lo: 2; y = y_hi * 2 + y_lo), z: 8, core: 2. Of those that a mesh axis runs over, the one named last changes fastest.
Arguments:
- tokens: bfloat16 [1048576, 512], P('ctx', 'fsdp'), may hold values from -6 to 6
- factor_d: bfloat16 [32768, 32, 32], P(('ctx', 'fsdp')), may hold values from -1 to 1
- factor_c: bfloat16 [32768, 32, 32], P(('ctx', 'fsdp')), may hold values from -1 to 1
- factor_b: bfloat16 [32768, 32, 32], P(('ctx', 'fsdp')), may hold values from -1 to 1
- factor_a: bfloat16 [32768, 32, 32], P(('ctx', 'fsdp')), may hold values from -1 to 1
- w_proj: bfloat16 [512, 512], P(None, 'fsdp'), may hold values from -0.25 to 0.25
Outputs:
- output: bfloat16 [1048576, 512], P('ctx', 'fsdp')
The draws below stay inside these ranges and needn't reach their ends.
All inputs are finite; a program needn't handle non-finite values.
Results may differ from the reference program's by a relative error of at most 0.0076.
Values may be sent and summed in bfloat16 or wider, within the bound.
No kernel may reach another device: no remote copies, remote signals or barrier semaphores. Data moves between devices by JAX's collectives and lax.ppermute only.
A program may use at most 128 MiB of HBM per device.

```python
import math
import jax
import jax.numpy as jnp
from jax import lax

BLK = 32
CH = 512
TOKENS = 1048576
NBLOCKS = 32768


def level_of(rng, dims, cuts, low, high):
    gain, own = 1.0, jax.random.fold_in(rng, 6)
    for position, blocks in cuts:
        heights = jnp.exp(jax.random.uniform(jax.random.fold_in(own, position), (blocks,), jnp.float32, low / len(cuts), high / len(cuts)))
        gain = gain * jnp.repeat(heights, dims[position] // blocks).reshape([-1 if axis == position else 1 for axis in range(len(dims))])
    return gain


def centred(key, dims, deviation, reach, split=(), held_as=jnp.bfloat16):
    factor_of = level_of(key, dims, split, -0.22, 0.18) if split else 1.0
    array = jax.random.normal(key, dims, jnp.float32) * deviation * factor_of
    return jnp.minimum(jnp.maximum(array, -reach), reach).astype(held_as)


def setup_inputs(seed: int = 0) -> dict:
    streams_of = jax.random.split(jax.random.key(seed), 7)
    return {
        "tokens": centred(streams_of[0], (TOKENS, CH), 1.0, 6.0, ((0, 64), (1, 4))),
        "factor_d": centred(streams_of[1], (NBLOCKS, BLK, BLK), BLK ** -0.5, 1.0, ((0, 256),)),
        "factor_c": centred(streams_of[2], (NBLOCKS, BLK, BLK), BLK ** -0.5, 1.0, ((0, 256),)),
        "factor_b": centred(streams_of[3], (NBLOCKS, BLK, BLK), BLK ** -0.5, 1.0, ((0, 256),)),
        "factor_a": centred(streams_of[4], (NBLOCKS, BLK, BLK), BLK ** -0.5, 1.0, ((0, 256),)),
        "w_proj": centred(streams_of[5], (CH, CH), CH ** -0.5, 0.25, ((1, 4),)),
    }


def monarch(cols, factor_d, factor_c, factor_b, factor_a):
    width = cols.shape[1]
    square = BLK * BLK
    first = jnp.einsum('gij,gjc->gic', factor_d.astype(jnp.float32), cols.reshape(-1, BLK, width).astype(jnp.float32)).astype(jnp.bfloat16)
    weights_c = factor_c.reshape(square, BLK, BLK, BLK).astype(jnp.float32)
    second = jnp.einsum('pdij,pjdc->pidc', weights_c, first.reshape(square, BLK, BLK, width).astype(jnp.float32)).astype(jnp.bfloat16)
    weights_b = factor_b.reshape(square, BLK, BLK, BLK).astype(jnp.float32)
    third = jnp.einsum('laij,ajlc->ailc', weights_b, second.reshape(BLK, BLK, square, width).astype(jnp.float32)).astype(jnp.bfloat16)
    weights_a = factor_a.reshape(square, BLK, BLK, BLK).astype(jnp.float32)
    fourth = jnp.einsum('lbij,jblc->iblc', weights_a, third.astype(jnp.float32)).astype(jnp.bfloat16)
    return fourth.reshape(-1, width)


def reference(tokens, factor_d, factor_c, factor_b, factor_a, w_proj):
    width = math.gcd(CH, 64)
    count = CH // width
    pieces = tokens.reshape(TOKENS, count, width).transpose(1, 0, 2)
    mixed_pieces = lax.map(lambda cols: monarch(cols, factor_d, factor_c, factor_b, factor_a), pieces)
    mixed = mixed_pieces.transpose(1, 0, 2).reshape(TOKENS, CH)
    gated = (mixed.astype(jnp.float32) * jax.nn.silu(tokens.astype(jnp.float32))).astype(jnp.bfloat16)
    return jnp.dot(gated, w_proj, preferred_element_type=jnp.float32).astype(jnp.bfloat16)
```

```python
import functools

import jax
import jax.numpy as jnp
from jax import lax
from jax.experimental import pallas as pl
from jax.experimental.pallas import tpu as pltpu
from jax.sharding import PartitionSpec as P

BLK = 32
LANES = 128
SUB = 8
WIDE = SUB * BLK
PACK = LANES // BLK
SQUARE = BLK * BLK
RANKS = 4
ALL = RANKS * LANES
BF16 = jnp.bfloat16
F32 = jnp.float32
VMEM_LIMIT = 44 * 1024 * 1024
RETURN_QUADS = (2, 1, 1)

VMEM = pl.BlockSpec(memory_space=pltpu.VMEM)
SMEM = pl.BlockSpec(memory_space=pltpu.SMEM)
ANY = pl.BlockSpec(memory_space=pl.ANY)
FACTOR = pltpu.VMEM((LANES, SQUARE), BF16)
WIDE_SHAPE = pltpu.VMEM((4, SUB, BLK, WIDE), BF16)
SPREAD_SHAPE = pltpu.VMEM((PACK, LANES, WIDE), BF16)


def call(kernel, name, out_shape, in_specs, out_specs, scratch, flops, moved, exps=0, aliases=None):
    return pl.pallas_call(
        kernel,
        name=name,
        out_shape=out_shape,
        in_specs=in_specs,
        out_specs=out_specs,
        scratch_shapes=scratch,
        input_output_aliases=aliases or {},
        compiler_params=pltpu.CompilerParams(vmem_limit_bytes=VMEM_LIMIT),
        cost_estimate=pl.CostEstimate(flops=flops, bytes_accessed=moved, transcendentals=exps),
    )


def aligned(start, size):
    return pl.ds(pl.multiple_of(start, size), size)


def started(copies):
    for copy in copies:
        copy.start()
    return copies


def finish(copies):
    for copy in copies:
        copy.wait()


def iota(shape, axis):
    return lax.broadcasted_iota(jnp.int32, shape, axis)


def ones_where(condition):
    return jnp.where(condition, 1.0, 0.0).astype(BF16)


def reorder(factor_ref, source_of):
    shape = (LANES, LANES)
    order = ones_where(source_of(iota(shape, 0)) == iota(shape, 1))
    factor_ref[...] = jnp.dot(order, factor_ref[...], preferred_element_type=F32).astype(BF16)


def widen_major(factor, wide_ref):
    rows = factor.astype(F32)
    block, row = iota((BLK, LANES), 1) // BLK, iota((BLK, LANES), 0) % SUB
    keeps = (block == row, block == row - PACK)
    for m in range(SUB):
        turned = rows[:, m * LANES : (m + 1) * LANES]
        rolled = [pltpu.roll(turned, turn * BLK, 1) for turn in range(1, PACK)]
        for turn in range(1, PACK):
            turned = jnp.where(row % PACK == turn, rolled[turn - 1], turned)
        for half in range(PACK // 2):
            parts = []
            for q in (2 * half, 2 * half + 1):
                here = turned if q == 0 else pltpu.roll(turned, LANES - q * BLK, 1)
                both = jnp.concatenate([jnp.where(keep, here, 0.0) for keep in keeps], axis=1)
                parts.append(both.reshape(4, SUB, WIDE))
            wide_ref[:, m, half * 16 : half * 16 + 16, :] = jnp.concatenate(parts, axis=1).astype(BF16)


def fill_spread(spread_ref):
    row, want = iota((LANES, WIDE), 0), iota((LANES, WIDE), 1) // 4 % BLK
    for q in range(PACK):
        spread_ref[q] = ones_where(row == want + q * BLK)


def widen_minor(factor, spread_ref, wide_ref):
    rows = factor.astype(F32).reshape(4, SUB, SQUARE)
    tiles = [rows[:, :, m * LANES : (m + 1) * LANES] for m in range(SUB)]
    left = jnp.stack(tiles, axis=1).reshape(WIDE, LANES).astype(BF16)
    shape = (1, SUB, WIDE)
    keep = iota(shape, 1) == iota(shape, 2) // LANES * 4 + iota(shape, 2) % 4
    for half in range(PACK // 2):
        parts = []
        for q in (2 * half, 2 * half + 1):
            part = jnp.dot(left, spread_ref[q], preferred_element_type=F32)
            parts.append(jnp.where(keep, part.reshape(BLK, SUB, WIDE), 0.0))
        both = jnp.concatenate(parts, axis=1).astype(BF16)
        wide_ref[:, :, half * 16 : half * 16 + 16, :] = both.reshape(4, SUB, 16, WIDE)


def apply(wide_ref, group, data):
    left = wide_ref[group].reshape(WIDE, WIDE)
    return jnp.dot(left, data, preferred_element_type=F32).reshape(BLK, SUB, data.shape[1])


def local_kernel(where_ref, tokens_ref, fd_ref, fc_ref, *rest):
    out_ref, tokens_v, fd_v, fc_v, wide_ref, first_ref, out_v, sem, out_sem = rest[-9:]
    quarter = where_ref[0]
    factors = started(
        [pltpu.make_async_copy(fd_ref, fd_v, sem.at[4]), pltpu.make_async_copy(fc_ref, fc_v, sem.at[5])]
    )
    arriving = started(
        [
            pltpu.make_async_copy(tokens_ref.at[aligned((quarter * 4 + p) * SQUARE, SQUARE), :], tokens_v.at[p], sem.at[p])
            for p in range(4)
        ]
    )
    finish(factors)
    reorder(fc_v, lambda r: r // 4 % 4 * BLK + r // 16 * 4 + r % 4)
    for p in range(4):
        widen_major(fd_v[p * BLK : (p + 1) * BLK, :], wide_ref)
        arriving[p].wait()
        for pair in range(2):
            halves = [
                apply(wide_ref, group, tokens_v[p, group * WIDE : (group + 1) * WIDE, :])
                for group in (2 * pair, 2 * pair + 1)
            ]
            first_ref[p, :, pair * 16 : pair * 16 + 16, :] = jnp.concatenate(halves, axis=1).astype(BF16)
    leaving = []
    for step in range(4):
        widen_major(fc_v[step * BLK : (step + 1) * BLK, :], wide_ref)
        for one in range(2):
            quad = 2 * step + one
            halves = []
            for pair in range(2):
                held = first_ref[2 * pair : 2 * pair + 2, 4 * quad : 4 * quad + 4]
                halves.append(apply(wide_ref, 2 * one + pair, held.reshape(WIDE, LANES)))
            out_v[quad] = jnp.concatenate(halves, axis=1).astype(BF16)
            target = out_ref.at[:, quad // 4, quad % 4, quarter]
            leaving += started([pltpu.make_async_copy(out_v.at[quad], target, out_sem.at[quad])])
    finish(leaving)


def local_steps(where, tokens, factor_d, factor_c, base):
    extra = [] if base is None else [base]
    return call(
        local_kernel,
        "steps_d_c",
        jax.ShapeDtypeStruct((BLK, 2, RANKS, RANKS, 16, LANES), BF16),
        [SMEM] + [ANY] * (3 + len(extra)),
        ANY,
        [
            pltpu.VMEM((4, SQUARE, LANES), BF16),
            FACTOR,
            FACTOR,
            WIDE_SHAPE,
            pltpu.VMEM((4, BLK, BLK, LANES), BF16),
            pltpu.VMEM((SUB, BLK, 16, LANES), BF16),
            pltpu.SemaphoreType.DMA((6,)),
            pltpu.SemaphoreType.DMA((SUB,)),
        ],
        flops=2**31,
        moved=3 * 2**20,
        aliases={4: 0} if extra else None,
    )(where, tokens, factor_d, factor_c, *extra)


def d_lo_minor(row):
    return row % 4 * BLK + row // 4


def step_a_quad(quad, third_ref, row_of, fa_v, spread_ref, wide_ref, sent_v, slot):
    rows = [fa_v[high * 64 + quad * 16 : high * 64 + quad * 16 + 16, :] for high in range(2)]
    widen_minor(jnp.concatenate(rows, axis=0), spread_ref, wide_ref)
    for high in range(2):
        halves = []
        for pair in range(2):
            first = row_of(high, quad) + 2 * pair
            halves.append(apply(wide_ref, 2 * high + pair, third_ref[first : first + 2].reshape(WIDE, ALL)))
        sent_v[slot, :, high] = jnp.concatenate(halves, axis=1).astype(BF16)


def middle_kernel(count, held_ref, fb_ref, fa_ref, *rest):
    third_ref, sent_ref, held_v, fb_v, fa_v, wide_ref, spread_ref, third_v, sent_v, sem, out_sem = rest[-11:]
    factors = started(
        [pltpu.make_async_copy(fb_ref, fb_v, sem.at[4]), pltpu.make_async_copy(fa_ref, fa_v, sem.at[5])]
    )
    arriving = started(
        [
            pltpu.make_async_copy(held_ref.at[pl.ds(8 * step, 8)], held_v.at[pl.ds(8 * step, 8)], sem.at[step])
            for step in range(4)
        ]
    )
    fill_spread(spread_ref)
    finish(factors)
    reorder(fb_v, d_lo_minor)
    reorder(fa_v, d_lo_minor)
    for step in range(4):
        widen_minor(fb_v[step * BLK : (step + 1) * BLK, :], spread_ref, wide_ref)
        arriving[step].wait()
        for quad in range(2):
            halves = []
            for pair in range(2):
                a = 8 * step + 4 * quad + 2 * pair
                data = [held_v[a : a + 2, :, rank].reshape(WIDE, LANES) for rank in range(RANKS)]
                halves.append(apply(wide_ref, 2 * quad + pair, jnp.concatenate(data, axis=1)))
            first = step * BLK + quad * 16
            third_v[:, first : first + 16, :] = jnp.concatenate(halves, axis=1).astype(BF16)
    later = 16 - 4 * count
    leaving = started(
        [
            pltpu.make_async_copy(
                third_v.at[pl.ds(high * 16 + 4 * count, later)],
                third_ref.at[pl.ds(high * 16 + 4 * count, later)],
                out_sem.at[high],
            )
            for high in range(2)
        ]
    )
    for quad in range(count):
        step_a_quad(quad, third_v, lambda high, at: high * 16 + at * 4, fa_v, spread_ref, wide_ref, sent_v, quad)
        leaving += started([pltpu.make_async_copy(sent_v.at[quad], sent_ref.at[:, :, quad], out_sem.at[2 + quad])])
    finish(leaving)


def sent_shape(count):
    return jax.ShapeDtypeStruct((BLK, 2, count, 16, ALL), BF16)


def middle(held, factor_b, factor_a, count, after):
    return call(
        functools.partial(middle_kernel, count),
        "steps_b_a",
        (jax.ShapeDtypeStruct((BLK, LANES, ALL), BF16), sent_shape(count)),
        [ANY] * (3 + len(after)),
        (ANY, ANY),
        [
            pltpu.VMEM(held.shape, BF16),
            FACTOR,
            FACTOR,
            WIDE_SHAPE,
            SPREAD_SHAPE,
            pltpu.VMEM((BLK, LANES, ALL), BF16),
            pltpu.VMEM((count, BLK, 2, 16, ALL), BF16),
            pltpu.SemaphoreType.DMA((6,)),
            pltpu.SemaphoreType.DMA((2 + count,)),
        ],
        flops=2**32,
        moved=9 * 2**20,
    )(held, factor_b, factor_a, *after)


def step_a_kernel(first_quad, count, third_ref, fa_ref, *rest):
    sent_ref, third_v, fa_v, wide_ref, spread_ref, sent_v, sem, out_sem = rest[-8:]
    arriving = started(
        [pltpu.make_async_copy(fa_ref, fa_v, sem.at[2])]
        + [
            pltpu.make_async_copy(
                third_ref.at[pl.ds(high * 16 + 4 * first_quad, 4 * count)],
                third_v.at[pl.ds(high * 4 * count, 4 * count)],
                sem.at[high],
            )
            for high in range(2)
        ]
    )
    fill_spread(spread_ref)
    finish(arriving)
    reorder(fa_v, d_lo_minor)
    leaving = []
    for slot in range(count):
        row_of = lambda high, quad: (high * count + quad - first_quad) * 4
        step_a_quad(first_quad + slot, third_v, row_of, fa_v, spread_ref, wide_ref, sent_v, slot)
        leaving += started([pltpu.make_async_copy(sent_v.at[slot], sent_ref.at[:, :, slot], out_sem.at[slot])])
    finish(leaving)


def step_a(third, factor_a, first_quad, count, after):
    return call(
        functools.partial(step_a_kernel, first_quad, count),
        "step_a",
        sent_shape(count),
        [ANY] * (2 + len(after)),
        ANY,
        [
            pltpu.VMEM((8 * count, LANES, ALL), BF16),
            FACTOR,
            WIDE_SHAPE,
            SPREAD_SHAPE,
            pltpu.VMEM((count, BLK, 2, 16, ALL), BF16),
            pltpu.SemaphoreType.DMA((3,)),
            pltpu.SemaphoreType.DMA((count,)),
        ],
        flops=2**29 * count,
        moved=2**21 * count,
    )(third, factor_a, *after)


def place_of(row, f):
    turn, s, p, low = row // 64, row // 16 % 4, row // 4 % 4, row % 4
    return p * 64 + s * 16 + (turn ^ f) * 4 + low


def split_kernel(f_ref, tokens_ref, w_ref, after_ref, *rest):
    out_refs, w_out_ref = rest[:RANKS], rest[RANKS]
    order_ref, tokens_v, out_v, sem, out_sem = rest[RANKS + 1 :]
    leaving = started([pltpu.make_async_copy(w_ref, w_out_ref, sem.at[4])])
    size = 4 * SQUARE
    arriving = started(
        [
            pltpu.make_async_copy(tokens_ref.at[pl.ds(quad * size, size), :], tokens_v.at[quad], sem.at[quad])
            for quad in range(4)
        ]
    )
    order_ref[...] = ones_where(place_of(iota((WIDE, WIDE), 0), f_ref[0]) == iota((WIDE, WIDE), 1))
    for quad in range(4):
        arriving[quad].wait()

        @pl.loop(0, 4)
        def _(step):
            blocks = []
            for one in range(4):
                rows = [tokens_v[quad, aligned(p * SQUARE + step * 256 + one * 64, 64), :] for p in range(4)]
                blocks.append(jnp.concatenate(rows, axis=0))
            held = jnp.concatenate(blocks, axis=1)
            moved = jnp.dot(order_ref[...], held, preferred_element_type=F32).astype(BF16)
            for turn in range(RANKS):
                for one in range(4):
                    block = moved[turn * 64 : turn * 64 + 64, one * LANES : (one + 1) * LANES]
                    out_v[turn, quad, aligned(step * 256 + one * 64, 64), :] = block

        leaving += started(
            [
                pltpu.make_async_copy(
                    out_v.at[turn, quad], out_refs[turn].at[pl.ds(quad * SQUARE, SQUARE), :], out_sem.at[turn, quad]
                )
                for turn in range(RANKS)
            ]
        )
    finish(leaving)


def split(f, tokens, w, after):
    quarter = jax.ShapeDtypeStruct((4 * SQUARE, LANES), BF16)
    *parts, w = call(
        split_kernel,
        "split",
        [quarter] * RANKS + [jax.ShapeDtypeStruct(w.shape, BF16)],
        [SMEM, ANY, ANY, ANY],
        [ANY] * (RANKS + 1),
        [
            pltpu.VMEM((WIDE, WIDE), BF16),
            pltpu.VMEM((4, 4 * SQUARE, LANES), BF16),
            pltpu.VMEM((RANKS, 4, SQUARE, LANES), BF16),
            pltpu.SemaphoreType.DMA((5,)),
            pltpu.SemaphoreType.DMA((RANKS, 4)),
        ],
        flops=2**30,
        moved=8 * 2**20,
    )(f, tokens, w, after)
    return parts, w


def project_kernel(first_quad, f_ref, mixed_ref, *rest):
    token_refs, w_refs, rest = rest[:RANKS], rest[RANKS : 2 * RANKS], rest[2 * RANKS :]
    out_refs = rest[-RANKS - 8 : -8]
    w_all_ref, w_v, mixed_v, tokens_v, out_v, w_sem, sem, out_sem = rest[-8:]
    f = f_ref[0]
    count = mixed_ref.shape[1]
    tile, steps = SQUARE // 4, 4 * count
    weights = started([pltpu.make_async_copy(w_refs[turn], w_v.at[turn], w_sem.at[turn]) for turn in range(RANKS)])
    arriving = []
    for step in range(steps):
        rows = pl.ds((first_quad * 4 + step) * tile, tile)
        source = mixed_ref.at[pl.ds(step % 4 * 16, 16), step // 4]
        arriving.append(
            started(
                [pltpu.make_async_copy(source, mixed_v.at[step], sem.at[step, RANKS])]
                + [
                    pltpu.make_async_copy(token_refs[turn].at[rows, :], tokens_v.at[turn, step], sem.at[step, turn])
                    for turn in range(RANKS)
                ]
            )
        )
    finish(weights)
    for row in range(RANKS):
        for column in range(RANKS):
            block = w_v[column, aligned((f ^ row) * LANES, LANES), :]
            w_all_ref[row * LANES : (row + 1) * LANES, column * LANES : (column + 1) * LANES] = block
    leaving = []
    for step in range(steps):
        finish(arriving[step])
        gated = []
        for turn in range(RANKS):
            mixed = mixed_v[step, :, :, aligned((f ^ turn) * LANES, LANES)].reshape(tile, LANES).astype(F32)
            value = tokens_v[turn, step].astype(F32)
            gated.append((mixed * (value / (1.0 + jnp.exp(-value)))).astype(BF16))
        result = jnp.dot(jnp.concatenate(gated, axis=1), w_all_ref[...], preferred_element_type=F32).astype(BF16)
        for turn in range(RANKS):
            out_v[turn, step] = result[:, turn * LANES : (turn + 1) * LANES]
            target = out_refs[turn].at[pl.ds(step * tile, tile), :]
            leaving += started([pltpu.make_async_copy(out_v.at[turn, step], target, out_sem.at[step, turn])])
    finish(leaving)


def project(f, mixed, tokens, w, first_quad, after):
    steps, tile = mixed.shape[1] * 4, SQUARE // 4
    size = steps * tile * ALL
    return call(
        functools.partial(project_kernel, first_quad),
        "project",
        [jax.ShapeDtypeStruct((steps * tile, LANES), BF16)] * RANKS,
        [SMEM] + [ANY] * (1 + 2 * RANKS + len(after)),
        [ANY] * RANKS,
        [
            pltpu.VMEM((ALL, ALL), BF16),
            pltpu.VMEM((RANKS, ALL, LANES), BF16),
            pltpu.VMEM((steps, 16, 16, ALL), BF16),
            pltpu.VMEM((RANKS, steps, tile, LANES), BF16),
            pltpu.VMEM((RANKS, steps, tile, LANES), BF16),
            pltpu.SemaphoreType.DMA((RANKS,)),
            pltpu.SemaphoreType.DMA((steps, RANKS + 1)),
            pltpu.SemaphoreType.DMA((steps, RANKS)),
        ],
        flops=size * 1024,
        moved=size * 6,
        exps=size,
    )(f, mixed, *tokens, *w, *after)


def merge_kernel(first_row, f_ref, *rest):
    part_refs, (out_ref, done_ref, order_ref, parts_v, held_v, sem, out_sem) = rest[:RANKS], rest[-7:]
    count = part_refs[0].shape[0] // SQUARE
    arriving = [
        started(
            [
                pltpu.make_async_copy(
                    part_refs[turn].at[pl.ds(quad * SQUARE, SQUARE), :], parts_v.at[turn, quad], sem.at[quad, turn]
                )
                for turn in range(RANKS)
            ]
        )
        for quad in range(count)
    ]
    done_ref[...] = jnp.zeros_like(done_ref)
    order_ref[...] = ones_where(place_of(iota((WIDE, WIDE), 1), f_ref[0]) == iota((WIDE, WIDE), 0))
    leaving = []
    for quad in range(count):
        finish(arriving[quad])

        @pl.loop(0, 4)
        def _(step):
            blocks = []
            for one in range(4):
                rows = [parts_v[turn, quad, aligned(step * 256 + one * 64, 64), :] for turn in range(RANKS)]
                blocks.append(jnp.concatenate(rows, axis=0))
            held = jnp.concatenate(blocks, axis=1)
            moved = jnp.dot(order_ref[...], held, preferred_element_type=F32).astype(BF16)
            for p in range(4):
                for one in range(4):
                    block = moved[p * 64 : p * 64 + 64, one * LANES : (one + 1) * LANES]
                    held_v[quad, aligned(p * SQUARE + step * 256 + one * 64, 64), :] = block

        rows = 4 * SQUARE
        target = out_ref.at[pl.ds(first_row + quad * rows, rows), :]
        leaving += started([pltpu.make_async_copy(held_v.at[quad], target, out_sem.at[quad])])
    finish(leaving)


def merge(f, parts, total, first_quad, base):
    rows = parts[0].shape[0]
    count = rows // SQUARE
    extra = [] if base is None else [base]
    return call(
        functools.partial(merge_kernel, first_quad * 4 * SQUARE),
        "merge",
        (jax.ShapeDtypeStruct((total, LANES), BF16), jax.ShapeDtypeStruct((SUB, LANES), F32)),
        [SMEM] + [ANY] * (RANKS + len(extra)),
        (ANY, VMEM),
        [
            pltpu.VMEM((WIDE, WIDE), BF16),
            pltpu.VMEM((RANKS, count, SQUARE, LANES), BF16),
            pltpu.VMEM((count, 4 * SQUARE, LANES), BF16),
            pltpu.SemaphoreType.DMA((count, RANKS)),
            pltpu.SemaphoreType.DMA((count,)),
        ],
        flops=rows * 4 * WIDE * LANES * 2,
        moved=rows * LANES * 16,
        aliases={5: 0} if extra else None,
    )(f, *parts, *extra)


TURNS = [[(rank, rank ^ turn) for rank in range(RANKS)] for turn in range(RANKS)]


def swap(parts):
    return [parts[0]] + [lax.ppermute(parts[turn], "fsdp", TURNS[turn]) for turn in (2, 1, 3)]


def in_turn(got):
    return [got[0], got[2], got[1], got[3]]


def share(x):
    chip = lax.ppermute(x, "fsdp", TURNS[2])
    core = lax.ppermute(x, "fsdp", TURNS[1])
    far = lax.ppermute(chip, "fsdp", TURNS[1])
    return [x, core, chip, far]


def body(tokens, factor_d, factor_c, factor_b, factor_a, w_proj):
    local_rows = tokens.shape[0]
    f = lax.axis_index("fsdp").astype(jnp.int32).reshape(1)

    flat = lambda factor: factor.reshape(-1, SQUARE)
    shared_d, shared_c = share(flat(factor_d)), share(flat(factor_c))

    second = None
    for turn in range(RANKS):
        second = local_steps(f ^ turn, tokens, shared_d[turn], shared_c[turn], second)
    token_parts, w = split(f, tokens, w_proj, second)
    token_parts = in_turn(swap(token_parts))
    w = share(w)
    arrived = lax.all_to_all(
        second.reshape(64 * RANKS, 64, LANES), ("ctx", "fsdp"), split_axis=0, concat_axis=0, tiled=True
    )
    weights_a = flat(factor_a)
    third, first_sent = middle(
        arrived.reshape(BLK, 2, RANKS, 64, LANES), flat(factor_b), weights_a, RETURN_QUADS[0], token_parts[1:] + w[1:]
    )

    out, first_quad = None, 0
    projected, ends = [], []
    for k, count in enumerate(RETURN_QUADS):
        if k == 0:
            sent = first_sent
        else:
            sent = step_a(third, weights_a, first_quad, count, projected[k - 2 : k - 1] if k >= 2 else [])
        mixed = lax.all_to_all(
            sent.reshape(64, count * 16, ALL), "ctx", split_axis=0, concat_axis=0, tiled=True
        ).reshape(64, count, 16, ALL)
        parts = project(f, mixed, token_parts, w, first_quad, ends[k - 2 : k - 1] if k >= 2 else [])
        out, done = merge(f, in_turn(swap(parts)), local_rows, first_quad, out)
        projected.append(parts[0])
        ends.append(done)
        first_quad += count
    return out


def solution(mesh):
    in_specs = (
        P("ctx", "fsdp"),
        P(("ctx", "fsdp"), None, None),
        P(("ctx", "fsdp"), None, None),
        P(("ctx", "fsdp"), None, None),
        P(("ctx", "fsdp"), None, None),
        P(None, "fsdp"),
    )
    out_specs = P("ctx", "fsdp")
    return jax.shard_map(body, mesh=mesh, in_specs=in_specs, out_specs=out_specs, check_vma=False)
```

```python
import functools

import jax
import jax.numpy as jnp
from jax import lax
from jax.experimental import pallas as pl
from jax.experimental.pallas import tpu as pltpu
from jax.sharding import PartitionSpec as P

BLK = 32
LANES = 128
SUB = 8
WIDE = SUB * BLK
PACK = LANES // BLK
SQUARE = BLK * BLK
RANKS = 4
ALL = RANKS * LANES
BF16 = jnp.bfloat16
F32 = jnp.float32
MIB = 1024 * 1024
LARGE, MEDIUM, SMALL = 60 * MIB, 53 * MIB, 24 * MIB
RETURN_QUADS = (2, 2)

VMEM = pl.BlockSpec(memory_space=pltpu.VMEM)
SMEM = pl.BlockSpec(memory_space=pltpu.SMEM)
ANY = pl.BlockSpec(memory_space=pl.ANY)
FACTOR = pltpu.VMEM((LANES, SQUARE), BF16)
DONE = jax.ShapeDtypeStruct((SUB, LANES), F32)
RAW = pltpu.VMEM((SQUARE, LANES), BF16)
WIDE_SHAPE = pltpu.VMEM((4, SUB, BLK, WIDE), BF16)
SPREAD_SHAPE = pltpu.VMEM((PACK, LANES, WIDE), BF16)


def call(kernel, name, out_shape, in_specs, out_specs, scratch, flops, moved, exps=0, aliases=None, grant=LARGE):
    return pl.pallas_call(
        kernel,
        name=name,
        out_shape=out_shape,
        in_specs=in_specs,
        out_specs=out_specs,
        scratch_shapes=scratch,
        input_output_aliases=aliases or {},
        compiler_params=pltpu.CompilerParams(vmem_limit_bytes=grant),
        cost_estimate=pl.CostEstimate(flops=flops, bytes_accessed=moved, transcendentals=exps),
    )


def aligned(start, size):
    return pl.ds(pl.multiple_of(start, size), size)


def started(copies):
    for copy in copies:
        copy.start()
    return copies


def finish(copies):
    for copy in copies:
        copy.wait()


def iota(shape, axis):
    return lax.broadcasted_iota(jnp.int32, shape, axis)


def ones_where(condition):
    return jnp.where(condition, 1.0, 0.0).astype(BF16)


def take(raw, factor_ref, source_of):
    shape = (LANES, LANES)
    order = ones_where(source_of(iota(shape, 0)) == iota(shape, 1))
    factor = lax.dot_general(order, raw, (((1,), (1,)), ((), ())), preferred_element_type=F32)
    factor_ref[...] = factor.astype(BF16)


def widen_major(factor, wide_ref):
    rows = factor.astype(F32)
    block, row = iota((BLK, LANES), 1) // BLK, iota((BLK, LANES), 0) % SUB
    keeps = (block == row, block == row - PACK)
    for m in range(SUB):
        turned = rows[:, m * LANES : (m + 1) * LANES]
        rolled = [pltpu.roll(turned, turn * BLK, 1) for turn in range(1, PACK)]
        for turn in range(1, PACK):
            turned = jnp.where(row % PACK == turn, rolled[turn - 1], turned)
        for half in range(PACK // 2):
            parts = []
            for q in (2 * half, 2 * half + 1):
                here = turned if q == 0 else pltpu.roll(turned, LANES - q * BLK, 1)
                both = jnp.concatenate([jnp.where(keep, here, 0.0) for keep in keeps], axis=1)
                parts.append(both.reshape(4, SUB, WIDE))
            wide_ref[:, m, half * 16 : half * 16 + 16, :] = jnp.concatenate(parts, axis=1).astype(BF16)


def fill_spread(spread_ref):
    row, want = iota((LANES, WIDE), 0), iota((LANES, WIDE), 1) // 4 % BLK
    for q in range(PACK):
        spread_ref[q] = ones_where(row == want + q * BLK)


def widen_minor(factor, spread_ref, wide_ref):
    rows = factor.astype(F32).reshape(4, SUB, SQUARE)
    tiles = [rows[:, :, m * LANES : (m + 1) * LANES] for m in range(SUB)]
    left = jnp.stack(tiles, axis=1).reshape(WIDE, LANES).astype(BF16)
    shape = (1, SUB, WIDE)
    keep = iota(shape, 1) == iota(shape, 2) // LANES * 4 + iota(shape, 2) % 4
    for half in range(PACK // 2):
        parts = []
        for q in (2 * half, 2 * half + 1):
            part = jnp.dot(left, spread_ref[q], preferred_element_type=F32)
            parts.append(jnp.where(keep, part.reshape(BLK, SUB, WIDE), 0.0))
        both = jnp.concatenate(parts, axis=1).astype(BF16)
        wide_ref[:, :, half * 16 : half * 16 + 16, :] = both.reshape(4, SUB, 16, WIDE)


def apply(wide_ref, group, data):
    left = wide_ref[group].reshape(WIDE, WIDE)
    return jnp.dot(left, data, preferred_element_type=F32).reshape(BLK, SUB, data.shape[1])


def local_kernel(fetch, where_ref, tokens_ref, fd_ref, fc_ref, *rest):
    out_ref, done_ref, tokens_v, fd_v, fc_v, wide_ref, first_ref, out_v, sem, out_sem = rest[-10 - 2 * fetch :][:10]
    fetched = []
    if fetch:
        fetched = started(
            [pltpu.make_async_copy(ref, rest[n - 2], sem.at[4 + n]) for n, ref in enumerate((fd_ref, fc_ref))]
        )
        fd_ref, fc_ref = rest[-2:]
    done_ref[...] = jnp.zeros_like(done_ref)
    quarter = where_ref[0]
    arriving = started(
        [
            pltpu.make_async_copy(tokens_ref.at[aligned((quarter * 4 + p) * SQUARE, SQUARE), :], tokens_v.at[p], sem.at[p])
            for p in range(4)
        ]
    )
    finish(fetched)
    take(fd_ref[...], fd_v, lambda r: r)
    take(fc_ref[...], fc_v, lambda r: r // 4 % 4 * BLK + r // 16 * 4 + r % 4)
    for p in range(4):
        widen_major(fd_v[p * BLK : (p + 1) * BLK, :], wide_ref)
        arriving[p].wait()
        for pair in range(2):
            halves = [
                apply(wide_ref, group, tokens_v[p, group * WIDE : (group + 1) * WIDE, :])
                for group in (2 * pair, 2 * pair + 1)
            ]
            first_ref[p, :, pair * 16 : pair * 16 + 16, :] = jnp.concatenate(halves, axis=1).astype(BF16)
    leaving = []
    for step in range(4):
        widen_major(fc_v[step * BLK : (step + 1) * BLK, :], wide_ref)
        for one in range(2):
            quad = 2 * step + one
            halves = []
            for pair in range(2):
                held = first_ref[2 * pair : 2 * pair + 2, 4 * quad : 4 * quad + 4]
                halves.append(apply(wide_ref, 2 * one + pair, held.reshape(WIDE, LANES)))
            out_v[quad] = jnp.concatenate(halves, axis=1).astype(BF16)
            target = out_ref.at[:, quad // 4, quad % 4, quarter]
            leaving += started([pltpu.make_async_copy(out_v.at[quad], target, out_sem.at[quad])])
    finish(leaving)


def local_steps(where, tokens, factor_d, factor_c, base):
    extra = [] if base is None else [base]
    fetch = base is None
    place = ANY if fetch else VMEM
    return call(
        functools.partial(local_kernel, fetch),
        "steps_d_c",
        (jax.ShapeDtypeStruct((BLK, 2, RANKS, RANKS, 16, LANES), BF16), DONE),
        [SMEM, ANY, place, place] + [ANY] * len(extra),
        (ANY, VMEM),
        [
            pltpu.VMEM((4, SQUARE, LANES), BF16),
            FACTOR,
            FACTOR,
            WIDE_SHAPE,
            pltpu.VMEM((4, BLK, BLK, LANES), BF16),
            pltpu.VMEM((SUB, BLK, 16, LANES), BF16),
            pltpu.SemaphoreType.DMA((6,)),
            pltpu.SemaphoreType.DMA((SUB,)),
        ]
        + [RAW, RAW] * fetch,
        flops=2**31,
        moved=3 * 2**20,
        aliases={4: 0} if extra else None,
        grant=LARGE if fetch else MEDIUM,
    )(where, tokens, factor_d, factor_c, *extra)


def d_lo_minor(row):
    return row % 4 * BLK + row // 4


def step_a_quad(quad, third_ref, row_of, fa_v, spread_ref, wide_ref, sent_v, slot):
    rows = [fa_v[high * 64 + quad * 16 : high * 64 + quad * 16 + 16, :] for high in range(2)]
    widen_minor(jnp.concatenate(rows, axis=0), spread_ref, wide_ref)
    for high in range(2):
        halves = []
        for pair in range(2):
            first = row_of(high, quad) + 2 * pair
            halves.append(apply(wide_ref, 2 * high + pair, third_ref[first : first + 2].reshape(WIDE, ALL)))
        sent_v[slot, :, high] = jnp.concatenate(halves, axis=1).astype(BF16)


def middle_kernel(count, held_ref, fb_ref, fa_ref, *rest):
    third_ref, sent_ref, held_v, fb_raw, fa_raw, fb_v, fa_v = rest[-13:-6]
    wide_ref, spread_ref, third_v, sent_v, sem, out_sem = rest[-6:]
    factors = started(
        [pltpu.make_async_copy(fb_ref, fb_raw, sem.at[4]), pltpu.make_async_copy(fa_ref, fa_raw, sem.at[5])]
    )
    arriving = started(
        [
            pltpu.make_async_copy(held_ref.at[pl.ds(8 * step, 8)], held_v.at[pl.ds(8 * step, 8)], sem.at[step])
            for step in range(4)
        ]
    )
    fill_spread(spread_ref)
    finish(factors)
    take(fb_raw[...], fb_v, d_lo_minor)
    take(fa_raw[...], fa_v, d_lo_minor)
    for step in range(4):
        widen_minor(fb_v[step * BLK : (step + 1) * BLK, :], spread_ref, wide_ref)
        arriving[step].wait()
        for quad in range(2):
            halves = []
            for pair in range(2):
                a = 8 * step + 4 * quad + 2 * pair
                data = [held_v[a : a + 2, :, rank].reshape(WIDE, LANES) for rank in range(RANKS)]
                halves.append(apply(wide_ref, 2 * quad + pair, jnp.concatenate(data, axis=1)))
            first = step * BLK + quad * 16
            third_v[:, first : first + 16, :] = jnp.concatenate(halves, axis=1).astype(BF16)
    later = 16 - 4 * count
    leaving = started(
        [
            pltpu.make_async_copy(
                third_v.at[pl.ds(high * 16 + 4 * count, later)],
                third_ref.at[pl.ds(high * 16 + 4 * count, later)],
                out_sem.at[high],
            )
            for high in range(2)
        ]
    )
    for quad in range(count):
        step_a_quad(quad, third_v, lambda high, at: high * 16 + at * 4, fa_v, spread_ref, wide_ref, sent_v, quad)
        leaving += started([pltpu.make_async_copy(sent_v.at[quad], sent_ref.at[:, :, quad], out_sem.at[2 + quad])])
    finish(leaving)


def sent_shape(count):
    return jax.ShapeDtypeStruct((BLK, 2, count, 16, ALL), BF16)


def middle(held, factor_b, factor_a, count, after):
    return call(
        functools.partial(middle_kernel, count),
        "steps_b_a",
        (jax.ShapeDtypeStruct((BLK, LANES, ALL), BF16), sent_shape(count)),
        [ANY] * (3 + len(after)),
        (ANY, ANY),
        [
            pltpu.VMEM(held.shape, BF16),
            RAW,
            RAW,
            FACTOR,
            FACTOR,
            WIDE_SHAPE,
            SPREAD_SHAPE,
            pltpu.VMEM((BLK, LANES, ALL), BF16),
            pltpu.VMEM((count, BLK, 2, 16, ALL), BF16),
            pltpu.SemaphoreType.DMA((6,)),
            pltpu.SemaphoreType.DMA((2 + count,)),
        ],
        flops=2**32,
        moved=9 * 2**20,
    )(held, factor_b, factor_a, *after)


def step_a_kernel(first_quad, count, third_ref, fa_ref, *rest):
    sent_ref, third_v, fa_raw, fa_v, wide_ref, spread_ref, sent_v, sem, out_sem = rest[-9:]
    arriving = started(
        [pltpu.make_async_copy(fa_ref, fa_raw, sem.at[2])]
        + [
            pltpu.make_async_copy(
                third_ref.at[pl.ds(high * 16 + 4 * first_quad, 4 * count)],
                third_v.at[pl.ds(high * 4 * count, 4 * count)],
                sem.at[high],
            )
            for high in range(2)
        ]
    )
    fill_spread(spread_ref)
    finish(arriving)
    take(fa_raw[...], fa_v, d_lo_minor)
    leaving = []
    for slot in range(count):
        row_of = lambda high, quad: (high * count + quad - first_quad) * 4
        step_a_quad(first_quad + slot, third_v, row_of, fa_v, spread_ref, wide_ref, sent_v, slot)
        leaving += started([pltpu.make_async_copy(sent_v.at[slot], sent_ref.at[:, :, slot], out_sem.at[slot])])
    finish(leaving)


def step_a(third, factor_a, first_quad, count, after):
    return call(
        functools.partial(step_a_kernel, first_quad, count),
        "step_a",
        sent_shape(count),
        [ANY] * (2 + len(after)),
        ANY,
        [
            pltpu.VMEM((8 * count, LANES, ALL), BF16),
            RAW,
            FACTOR,
            WIDE_SHAPE,
            SPREAD_SHAPE,
            pltpu.VMEM((count, BLK, 2, 16, ALL), BF16),
            pltpu.SemaphoreType.DMA((3,)),
            pltpu.SemaphoreType.DMA((count,)),
        ],
        flops=2**29 * count,
        moved=2**21 * count,
    )(third, factor_a, *after)


def place_of(row, f):
    turn, s, p, low = row // 64, row // 16 % 4, row // 4 % 4, row % 4
    return p * 64 + s * 16 + (turn ^ f) * 4 + low


def split_kernel(f_ref, tokens_ref, w_ref, after_ref, *rest):
    halves, w_out_ref = (rest[:RANKS], rest[RANKS : 2 * RANKS]), rest[2 * RANKS]
    order_ref, tokens_v, out_v, sem, out_sem = rest[2 * RANKS + 1 :]
    leaving = started([pltpu.make_async_copy(w_ref, w_out_ref, sem.at[4])])
    size = 4 * SQUARE
    arriving = started(
        [
            pltpu.make_async_copy(tokens_ref.at[pl.ds(quad * size, size), :], tokens_v.at[quad], sem.at[quad])
            for quad in range(4)
        ]
    )
    order_ref[...] = ones_where(place_of(iota((WIDE, WIDE), 0), f_ref[0]) == iota((WIDE, WIDE), 1))
    for quad in range(4):
        arriving[quad].wait()

        for step in range(4):
            blocks = []
            for one in range(4):
                start = step * 256 + one * 64
                rows = [tokens_v[quad, p * SQUARE + start : p * SQUARE + start + 64, :] for p in range(4)]
                blocks.append(jnp.concatenate(rows, axis=0))
            held = jnp.concatenate(blocks, axis=1)
            moved = jnp.dot(order_ref[...], held, preferred_element_type=F32).astype(BF16)
            for turn in range(RANKS):
                for one in range(4):
                    block = moved[turn * 64 : turn * 64 + 64, one * LANES : (one + 1) * LANES]
                    start = step * 256 + one * 64
                    out_v[turn, quad, start : start + 64, :] = block

        leaving += started(
            [
                pltpu.make_async_copy(
                    out_v.at[turn, quad],
                    halves[quad // 2][turn].at[pl.ds(quad % 2 * SQUARE, SQUARE), :],
                    out_sem.at[turn, quad],
                )
                for turn in range(RANKS)
            ]
        )
    finish(leaving)


def split(f, tokens, w, after):
    half = jax.ShapeDtypeStruct((2 * SQUARE, LANES), BF16)
    *parts, w = call(
        split_kernel,
        "split",
        [half] * (2 * RANKS) + [jax.ShapeDtypeStruct(w.shape, BF16)],
        [SMEM, ANY, ANY, ANY],
        [ANY] * (2 * RANKS + 1),
        [
            pltpu.VMEM((WIDE, WIDE), BF16),
            pltpu.VMEM((4, 4 * SQUARE, LANES), BF16),
            pltpu.VMEM((RANKS, 4, SQUARE, LANES), BF16),
            pltpu.SemaphoreType.DMA((5,)),
            pltpu.SemaphoreType.DMA((RANKS, 4)),
        ],
        flops=2**30,
        moved=8 * 2**20,
    )(f, tokens, w, after)
    return (parts[:RANKS], parts[RANKS:]), w


def project_kernel(f_ref, mixed_ref, *rest):
    token_refs, w_refs, rest = rest[:RANKS], rest[RANKS : 2 * RANKS], rest[2 * RANKS :]
    out_refs = rest[: -8][-RANKS * mixed_ref.shape[1] :]
    w_all_ref, w_v, mixed_v, tokens_v, out_v, w_sem, sem, out_sem = rest[-8:]
    f = f_ref[0]
    steps, blocks, tile = mixed_v.shape[0], mixed_v.shape[1], tokens_v.shape[2]
    per_quad = SQUARE // tile
    weights = started([pltpu.make_async_copy(w_refs[turn], w_v.at[turn], w_sem.at[turn]) for turn in range(RANKS)])
    arriving = []
    for step in range(steps):
        rows = pl.ds(step * tile, tile)
        source = mixed_ref.at[pl.ds(step % per_quad * blocks, blocks), step // per_quad]
        arriving.append(
            started(
                [pltpu.make_async_copy(source, mixed_v.at[step], sem.at[step, RANKS])]
                + [
                    pltpu.make_async_copy(token_refs[turn].at[rows, :], tokens_v.at[turn, step], sem.at[step, turn])
                    for turn in range(RANKS)
                ]
            )
        )
    finish(weights)
    for row in range(RANKS):
        for column in range(RANKS):
            block = w_v[column, aligned((f ^ row) * LANES, LANES), :]
            w_all_ref[row * LANES : (row + 1) * LANES, column * LANES : (column + 1) * LANES] = block
    leaving = []
    for step in range(steps):
        finish(arriving[step])
        gated = []
        for turn in range(RANKS):
            mixed = mixed_v[step, :, :, aligned((f ^ turn) * LANES, LANES)].reshape(tile, LANES).astype(F32)
            value = tokens_v[turn, step].astype(F32)
            gated.append((mixed * (value / (1.0 + jnp.exp(-value)))).astype(BF16))
        result = jnp.dot(jnp.concatenate(gated, axis=1), w_all_ref[...], preferred_element_type=F32).astype(BF16)
        for turn in range(RANKS):
            out_v[turn, step] = result[:, turn * LANES : (turn + 1) * LANES]
            target = out_refs[step // per_quad * RANKS + turn].at[pl.ds(step % per_quad * tile, tile), :]
            leaving += started([pltpu.make_async_copy(out_v.at[turn, step], target, out_sem.at[step, turn])])
    finish(leaving)


def project(f, mixed, tokens, w, after):
    count = mixed.shape[1]
    tile = SQUARE // 2
    steps = count * SQUARE // tile
    size = steps * tile * ALL
    parts = call(
        project_kernel,
        "project",
        [jax.ShapeDtypeStruct((SQUARE, LANES), BF16)] * (RANKS * count),
        [SMEM] + [ANY] * (1 + 2 * RANKS + len(after)),
        [ANY] * (RANKS * count),
        [
            pltpu.VMEM((ALL, ALL), BF16),
            pltpu.VMEM((RANKS, ALL, LANES), BF16),
            pltpu.VMEM((steps, tile // 16, 16, ALL), BF16),
            pltpu.VMEM((RANKS, steps, tile, LANES), BF16),
            pltpu.VMEM((RANKS, steps, tile, LANES), BF16),
            pltpu.SemaphoreType.DMA((RANKS,)),
            pltpu.SemaphoreType.DMA((steps, RANKS + 1)),
            pltpu.SemaphoreType.DMA((steps, RANKS)),
        ],
        flops=size * 1024,
        moved=size * 6,
        exps=size,
    )(f, mixed, *tokens, *w, *after)
    return [parts[RANKS * quad : RANKS * (quad + 1)] for quad in range(count)]


def merge_kernel(first_row, f_ref, *rest):
    part_refs, (out_ref, done_ref, order_ref, held_v, out_sem) = rest[:RANKS], rest[-5:]
    count = part_refs[0].shape[0] // SQUARE
    done_ref[...] = jnp.zeros_like(done_ref)
    order_ref[...] = ones_where(place_of(iota((WIDE, WIDE), 1), f_ref[0]) == iota((WIDE, WIDE), 0))
    leaving = []
    for quad in range(count):
        for step in range(4):
            blocks = []
            for one in range(4):
                start = quad * SQUARE + step * 256 + one * 64
                rows = [ref[start : start + 64, :] for ref in part_refs]
                blocks.append(jnp.concatenate(rows, axis=0))
            held = jnp.concatenate(blocks, axis=1)
            moved = jnp.dot(order_ref[...], held, preferred_element_type=F32).astype(BF16)
            for p in range(4):
                for one in range(4):
                    block = moved[p * 64 : p * 64 + 64, one * LANES : (one + 1) * LANES]
                    start = p * SQUARE + step * 256 + one * 64
                    held_v[quad, start : start + 64, :] = block

        rows = 4 * SQUARE
        target = out_ref.at[pl.ds(first_row + quad * rows, rows), :]
        leaving += started([pltpu.make_async_copy(held_v.at[quad], target, out_sem.at[quad])])
    finish(leaving)


def merge(f, parts, total, first_quad, base):
    rows = parts[0].shape[0]
    count = rows // SQUARE
    extra = [] if base is None else [base]
    return call(
        functools.partial(merge_kernel, first_quad * 4 * SQUARE),
        "merge",
        (jax.ShapeDtypeStruct((total, LANES), BF16), DONE),
        [SMEM] + [VMEM] * RANKS + [ANY] * len(extra),
        (ANY, VMEM),
        [
            pltpu.VMEM((WIDE, WIDE), BF16),
            pltpu.VMEM((count, 4 * SQUARE, LANES), BF16),
            pltpu.SemaphoreType.DMA((count,)),
        ],
        flops=rows * 4 * WIDE * LANES * 2,
        moved=rows * LANES * 16,
        aliases={5: 0} if extra else None,
        grant=SMALL,
    )(f, *parts, *extra)


TURNS = [[(rank, rank ^ turn) for rank in range(RANKS)] for turn in range(RANKS)]


def swap(parts):
    return [parts[0]] + [lax.ppermute(parts[turn], "fsdp", TURNS[turn]) for turn in (2, 1, 3)]


def in_turn(got):
    return [got[0], got[2], got[1], got[3]]


def hold_kernel(x_ref, after_ref, out_ref):
    pass


def hold(x, after):
    return call(
        hold_kernel,
        "hold",
        jax.ShapeDtypeStruct(x.shape, x.dtype),
        [ANY, ANY],
        ANY,
        [],
        flops=0,
        moved=0,
        aliases={0: 0},
        grant=SMALL,
    )(x, after)


def share(x):
    chip = lax.ppermute(x, "fsdp", TURNS[2])
    core = lax.ppermute(x, "fsdp", TURNS[1])
    far = lax.ppermute(chip, "fsdp", TURNS[1])
    return [x, core, chip, far]


def body(tokens, factor_d, factor_c, factor_b, factor_a, w_proj):
    local_rows = tokens.shape[0]
    f = lax.axis_index("fsdp").astype(jnp.int32).reshape(1)

    raw = lambda factor: factor.transpose(1, 2, 0).reshape(SQUARE, LANES)

    own = (raw(factor_d), raw(factor_c))
    chip = [lax.ppermute(x, "fsdp", TURNS[2]) for x in own]
    core = [lax.ppermute(x, "fsdp", TURNS[1]) for x in own]
    second, _ = local_steps(f, tokens, *own, None)
    second, done = local_steps(f ^ 1, tokens, *core, second)
    chip = [hold(x, done) for x in chip]
    far = [lax.ppermute(x, "fsdp", TURNS[1]) for x in chip]
    second, _ = local_steps(f ^ 2, tokens, *chip, second)
    second, done = local_steps(f ^ 3, tokens, *far, second)
    token_parts, w = split(f, tokens, w_proj, done)
    w = share(w)
    token_parts = [in_turn(swap(half)) for half in token_parts]
    arrived = lax.all_to_all(
        second.reshape(64 * RANKS, 64, LANES), ("ctx", "fsdp"), split_axis=0, concat_axis=0, tiled=True
    )
    weights_a = raw(factor_a)
    third, first_sent = middle(
        arrived.reshape(BLK, 2, RANKS, 64, LANES), raw(factor_b), weights_a, RETURN_QUADS[0], token_parts[0][1:] + w[1:]
    )

    out, first_quad, after = None, 0, []
    for k, count in enumerate(RETURN_QUADS):
        sent = step_a(third, weights_a, first_quad, count, token_parts[1][1:]) if k else first_sent
        mixed = lax.all_to_all(
            sent.reshape(64, count * 16, ALL), "ctx", split_axis=0, concat_axis=0, tiled=True
        ).reshape(64, count, 16, ALL)
        parts = [in_turn(swap(part)) for part in project(f, mixed, token_parts[k], w, after)]
        for part in parts:
            out, done = merge(f, part, local_rows, first_quad, out)
            first_quad += 1
        after = [done]
    return out


def solution(mesh):
    in_specs = (
        P("ctx", "fsdp"),
        P(("ctx", "fsdp"), None, None),
        P(("ctx", "fsdp"), None, None),
        P(("ctx", "fsdp"), None, None),
        P(("ctx", "fsdp"), None, None),
        P(None, "fsdp"),
    )
    out_specs = P("ctx", "fsdp")
    return jax.shard_map(body, mesh=mesh, in_specs=in_specs, out_specs=out_specs, check_vma=False)
```

```python
import functools

import jax
import jax.numpy as jnp
from jax import lax
from jax.experimental import pallas as pl
from jax.experimental.pallas import tpu as pltpu
from jax.sharding import PartitionSpec as P

BLK = 32
LANES = 128
SUB = 8
WIDE = SUB * BLK
PACK = LANES // BLK
SQUARE = BLK * BLK
RANKS = 4
ALL = RANKS * LANES
BF16 = jnp.bfloat16
F32 = jnp.float32
MIB = 1024 * 1024
LARGE, MEDIUM, SMALL = 60 * MIB, 53 * MIB, 24 * MIB
RETURN_QUADS = (2, 2)

VMEM = pl.BlockSpec(memory_space=pltpu.VMEM)
SMEM = pl.BlockSpec(memory_space=pltpu.SMEM)
ANY = pl.BlockSpec(memory_space=pl.ANY)
FACTOR = pltpu.VMEM((LANES, SQUARE), BF16)
DONE = jax.ShapeDtypeStruct((SUB, LANES), F32)
RAW = pltpu.VMEM((SQUARE, LANES), BF16)
WIDE_SHAPE = pltpu.VMEM((4, SUB, BLK, WIDE), BF16)
SPREAD_SHAPE = pltpu.VMEM((PACK, LANES, WIDE), BF16)


def call(kernel, name, out_shape, in_specs, out_specs, scratch, flops, moved, exps=0, aliases=None, grant=LARGE):
    return pl.pallas_call(
        kernel,
        name=name,
        out_shape=out_shape,
        in_specs=in_specs,
        out_specs=out_specs,
        scratch_shapes=scratch,
        input_output_aliases=aliases or {},
        compiler_params=pltpu.CompilerParams(vmem_limit_bytes=grant),
        cost_estimate=pl.CostEstimate(flops=flops, bytes_accessed=moved, transcendentals=exps),
    )


def aligned(start, size):
    return pl.ds(pl.multiple_of(start, size), size)


def started(copies):
    for copy in copies:
        copy.start()
    return copies


def finish(copies):
    for copy in copies:
        copy.wait()


def iota(shape, axis):
    return lax.broadcasted_iota(jnp.int32, shape, axis)


def ones_where(condition):
    return jnp.where(condition, 1.0, 0.0).astype(BF16)


def take(raw, factor_ref, source_of):
    shape = (LANES, LANES)
    order = ones_where(source_of(iota(shape, 0)) == iota(shape, 1))
    factor = lax.dot_general(order, raw, (((1,), (1,)), ((), ())), preferred_element_type=F32)
    factor_ref[...] = factor.astype(BF16)


def widen_major(factor, wide_ref):
    rows = factor.astype(F32)
    block, row = iota((BLK, LANES), 1) // BLK, iota((BLK, LANES), 0) % SUB
    keeps = (block == row, block == row - PACK)
    for m in range(SUB):
        turned = rows[:, m * LANES : (m + 1) * LANES]
        rolled = [pltpu.roll(turned, turn * BLK, 1) for turn in range(1, PACK)]
        for turn in range(1, PACK):
            turned = jnp.where(row % PACK == turn, rolled[turn - 1], turned)
        for half in range(PACK // 2):
            parts = []
            for q in (2 * half, 2 * half + 1):
                here = turned if q == 0 else pltpu.roll(turned, LANES - q * BLK, 1)
                both = jnp.concatenate([jnp.where(keep, here, 0.0) for keep in keeps], axis=1)
                parts.append(both.reshape(4, SUB, WIDE))
            wide_ref[:, m, half * 16 : half * 16 + 16, :] = jnp.concatenate(parts, axis=1).astype(BF16)


def fill_spread(spread_ref):
    row, want = iota((LANES, WIDE), 0), iota((LANES, WIDE), 1) // 4 % BLK
    for q in range(PACK):
        spread_ref[q] = ones_where(row == want + q * BLK)


def widen_minor(factor, spread_ref, wide_ref):
    rows = factor.astype(F32).reshape(4, SUB, SQUARE)
    tiles = [rows[:, :, m * LANES : (m + 1) * LANES] for m in range(SUB)]
    left = jnp.stack(tiles, axis=1).reshape(WIDE, LANES).astype(BF16)
    shape = (1, SUB, WIDE)
    keep = iota(shape, 1) == iota(shape, 2) // LANES * 4 + iota(shape, 2) % 4
    for half in range(PACK // 2):
        parts = []
        for q in (2 * half, 2 * half + 1):
            part = jnp.dot(left, spread_ref[q], preferred_element_type=F32)
            parts.append(jnp.where(keep, part.reshape(BLK, SUB, WIDE), 0.0))
        both = jnp.concatenate(parts, axis=1).astype(BF16)
        wide_ref[:, :, half * 16 : half * 16 + 16, :] = both.reshape(4, SUB, 16, WIDE)


def apply(wide_ref, group, data):
    left = wide_ref[group].reshape(WIDE, WIDE)
    return jnp.dot(left, data, preferred_element_type=F32).reshape(BLK, SUB, data.shape[1])


def local_kernel(fetch, where_ref, tokens_ref, fd_ref, fc_ref, *rest):
    out_ref, done_ref, tokens_v, fd_v, fc_v, wide_ref, first_ref, out_v, sem, out_sem = rest[-10 - 2 * fetch :][:10]
    fetched = []
    if fetch:
        fetched = started(
            [pltpu.make_async_copy(ref, rest[n - 2], sem.at[4 + n]) for n, ref in enumerate((fd_ref, fc_ref))]
        )
        fd_ref, fc_ref = rest[-2:]
    done_ref[...] = jnp.zeros_like(done_ref)
    quarter = where_ref[0]
    arriving = started(
        [
            pltpu.make_async_copy(tokens_ref.at[aligned((quarter * 4 + p) * SQUARE, SQUARE), :], tokens_v.at[p], sem.at[p])
            for p in range(4)
        ]
    )
    finish(fetched)
    take(fd_ref[...], fd_v, lambda r: r)
    take(fc_ref[...], fc_v, lambda r: r // 4 % 4 * BLK + r // 16 * 4 + r % 4)
    for p in range(4):
        widen_major(fd_v[p * BLK : (p + 1) * BLK, :], wide_ref)
        arriving[p].wait()
        for pair in range(2):
            halves = [
                apply(wide_ref, group, tokens_v[p, group * WIDE : (group + 1) * WIDE, :])
                for group in (2 * pair, 2 * pair + 1)
            ]
            first_ref[p, :, pair * 16 : pair * 16 + 16, :] = jnp.concatenate(halves, axis=1).astype(BF16)
    leaving = []
    for step in range(4):
        widen_major(fc_v[step * BLK : (step + 1) * BLK, :], wide_ref)
        for one in range(2):
            quad = 2 * step + one
            halves = []
            for pair in range(2):
                held = first_ref[2 * pair : 2 * pair + 2, 4 * quad : 4 * quad + 4]
                halves.append(apply(wide_ref, 2 * one + pair, held.reshape(WIDE, LANES)))
            out_v[quad] = jnp.concatenate(halves, axis=1).astype(BF16)
            target = out_ref.at[:, quad // 4, quad % 4, quarter]
            leaving += started([pltpu.make_async_copy(out_v.at[quad], target, out_sem.at[quad])])
    finish(leaving)


def local_steps(where, tokens, factor_d, factor_c, base):
    extra = [] if base is None else [base]
    fetch = base is None
    place = ANY if fetch else VMEM
    return call(
        functools.partial(local_kernel, fetch),
        "steps_d_c",
        (jax.ShapeDtypeStruct((BLK, 2, RANKS, RANKS, 16, LANES), BF16), DONE),
        [SMEM, ANY, place, place] + [ANY] * len(extra),
        (ANY, VMEM),
        [
            pltpu.VMEM((4, SQUARE, LANES), BF16),
            FACTOR,
            FACTOR,
            WIDE_SHAPE,
            pltpu.VMEM((4, BLK, BLK, LANES), BF16),
            pltpu.VMEM((SUB, BLK, 16, LANES), BF16),
            pltpu.SemaphoreType.DMA((6,)),
            pltpu.SemaphoreType.DMA((SUB,)),
        ]
        + [RAW, RAW] * fetch,
        flops=2**31,
        moved=3 * 2**20,
        aliases={4: 0} if extra else None,
        grant=LARGE if fetch else MEDIUM,
    )(where, tokens, factor_d, factor_c, *extra)


def d_lo_minor(row):
    return row % 4 * BLK + row // 4


GROUPS = 16
WEIGHTS = jax.ShapeDtypeStruct((GROUPS, SUB, BLK, WIDE), BF16)


def weights_kernel(fb_ref, fa_ref, after_ref, *rest):
    out_refs, (fb_raw, fa_raw, factor_ref, spread_ref, wide_v, sem, out_sem) = rest[:2], rest[2:]
    arriving = started(
        [
            pltpu.make_async_copy(ref, raw, sem.at[n])
            for n, (ref, raw) in enumerate(((fb_ref, fb_raw), (fa_ref, fa_raw)))
        ]
    )
    fill_spread(spread_ref)
    leaving = []
    for n, raw in enumerate((fb_raw, fa_raw)):
        arriving[n].wait()
        take(raw[...], factor_ref, d_lo_minor)
        for step in range(4):
            if n == 0:
                rows = factor_ref[step * BLK : (step + 1) * BLK, :]
            else:
                rows = [factor_ref[high * 64 + step * 16 : high * 64 + step * 16 + 16, :] for high in range(2)]
                rows = jnp.concatenate(rows, axis=0)
            groups = pl.ds(4 * step, 4)
            widen_minor(rows, spread_ref, wide_v.at[n, groups])
            leaving += started(
                [pltpu.make_async_copy(wide_v.at[n, groups], out_refs[n].at[groups], out_sem.at[n, step])]
            )
    finish(leaving)


def weights(factor_b, factor_a, after):
    return call(
        weights_kernel,
        "weights",
        (WEIGHTS, WEIGHTS),
        [ANY, ANY, ANY],
        (ANY, ANY),
        [
            RAW,
            RAW,
            FACTOR,
            SPREAD_SHAPE,
            pltpu.VMEM((2,) + WEIGHTS.shape, BF16),
            pltpu.SemaphoreType.DMA((2,)),
            pltpu.SemaphoreType.DMA((2, 4)),
        ],
        flops=2**31,
        moved=5 * 2**20,
    )(factor_b, factor_a, after)


def step_a_quad(slot, third_ref, row_of, wide_ref, sent_v):
    for high in range(2):
        halves = []
        for pair in range(2):
            first = row_of(high) + 2 * pair
            data = third_ref[first : first + 2].reshape(WIDE, ALL)
            halves.append(apply(wide_ref, 4 * slot + 2 * high + pair, data))
        sent_v[slot, :, high] = jnp.concatenate(halves, axis=1).astype(BF16)


def middle_kernel(count, held_ref, wb_ref, wa_ref, *rest):
    third_ref, sent_ref, held_v, wb_v, wa_v, third_v, sent_v, sem, out_sem = rest[-9:]
    arriving = []
    for step in range(4):
        groups, rows = pl.ds(4 * step, 4), pl.ds(8 * step, 8)
        arriving.append(
            started(
                [
                    pltpu.make_async_copy(wb_ref.at[groups], wb_v.at[groups], sem.at[step, 0]),
                    pltpu.make_async_copy(held_ref.at[rows], held_v.at[rows], sem.at[step, 1]),
                ]
            )
        )
    last = started([pltpu.make_async_copy(wa_ref.at[pl.ds(0, 4 * count)], wa_v, sem.at[4, 0])])
    for step in range(4):
        finish(arriving[step])
        for quad in range(2):
            halves = []
            for pair in range(2):
                a = 8 * step + 4 * quad + 2 * pair
                data = [held_v[a : a + 2, :, rank].reshape(WIDE, LANES) for rank in range(RANKS)]
                halves.append(apply(wb_v, 4 * step + 2 * quad + pair, jnp.concatenate(data, axis=1)))
            first = step * BLK + quad * 16
            third_v[:, first : first + 16, :] = jnp.concatenate(halves, axis=1).astype(BF16)
    finish(last)
    leaving = []
    for quad in range(count):
        step_a_quad(quad, third_v, lambda high: high * 16 + quad * 4, wa_v, sent_v)
        leaving += started([pltpu.make_async_copy(sent_v.at[quad], sent_ref.at[:, :, quad], out_sem.at[2 + quad])])
    later = 16 - 4 * count
    leaving += started(
        [
            pltpu.make_async_copy(
                third_v.at[pl.ds(high * 16 + 4 * count, later)],
                third_ref.at[pl.ds(high * 16 + 4 * count, later)],
                out_sem.at[high],
            )
            for high in range(2)
        ]
    )
    finish(leaving)


def sent_shape(count):
    return jax.ShapeDtypeStruct((BLK, 2, count, 16, ALL), BF16)


def middle(held, weights_b, weights_a, count, after):
    return call(
        functools.partial(middle_kernel, count),
        "steps_b_a",
        (jax.ShapeDtypeStruct((BLK, LANES, ALL), BF16), sent_shape(count)),
        [ANY] * (3 + len(after)),
        (ANY, ANY),
        [
            pltpu.VMEM(held.shape, BF16),
            pltpu.VMEM(WEIGHTS.shape, BF16),
            pltpu.VMEM((4 * count,) + WEIGHTS.shape[1:], BF16),
            pltpu.VMEM((BLK, LANES, ALL), BF16),
            pltpu.VMEM((count, BLK, 2, 16, ALL), BF16),
            pltpu.SemaphoreType.DMA((5, 2)),
            pltpu.SemaphoreType.DMA((2 + count,)),
        ],
        flops=2**32,
        moved=9 * 2**20,
    )(held, weights_b, weights_a, *after)


def step_a_kernel(first_quad, count, third_ref, wa_ref, *rest):
    sent_ref, third_v, wa_v, sent_v, sem, out_sem = rest[-6:]
    arriving = started(
        [pltpu.make_async_copy(wa_ref.at[pl.ds(4 * first_quad, 4 * count)], wa_v, sem.at[2])]
        + [
            pltpu.make_async_copy(
                third_ref.at[pl.ds(high * 16 + 4 * first_quad, 4 * count)],
                third_v.at[pl.ds(high * 4 * count, 4 * count)],
                sem.at[high],
            )
            for high in range(2)
        ]
    )
    finish(arriving)
    leaving = []
    for slot in range(count):
        step_a_quad(slot, third_v, lambda high: (high * count + slot) * 4, wa_v, sent_v)
        leaving += started([pltpu.make_async_copy(sent_v.at[slot], sent_ref.at[:, :, slot], out_sem.at[slot])])
    finish(leaving)


def step_a(third, weights_a, first_quad, count, after):
    return call(
        functools.partial(step_a_kernel, first_quad, count),
        "step_a",
        sent_shape(count),
        [ANY] * (2 + len(after)),
        ANY,
        [
            pltpu.VMEM((8 * count, LANES, ALL), BF16),
            pltpu.VMEM((4 * count,) + WEIGHTS.shape[1:], BF16),
            pltpu.VMEM((count, BLK, 2, 16, ALL), BF16),
            pltpu.SemaphoreType.DMA((3,)),
            pltpu.SemaphoreType.DMA((count,)),
        ],
        flops=2**29 * count,
        moved=2**21 * count,
    )(third, weights_a, *after)


def place_of(row, f):
    turn, s, p, low = row // 64, row // 16 % 4, row // 4 % 4, row % 4
    return p * 64 + s * 16 + (turn ^ f) * 4 + low


def split_kernel(f_ref, tokens_ref, w_ref, after_ref, *rest):
    out_refs, w_out_ref = rest[: 4 * RANKS], rest[4 * RANKS]
    order_ref, tokens_v, out_v, sem, out_sem = rest[4 * RANKS + 1 :]
    leaving = started([pltpu.make_async_copy(w_ref, w_out_ref, sem.at[4])])
    size = 4 * SQUARE
    arriving = started(
        [
            pltpu.make_async_copy(tokens_ref.at[pl.ds(quad * size, size), :], tokens_v.at[quad], sem.at[quad])
            for quad in range(4)
        ]
    )
    order_ref[...] = ones_where(place_of(iota((WIDE, WIDE), 0), f_ref[0]) == iota((WIDE, WIDE), 1))
    for quad in range(4):
        arriving[quad].wait()

        for step in range(4):
            blocks = []
            for one in range(4):
                start = step * 256 + one * 64
                rows = [tokens_v[quad, p * SQUARE + start : p * SQUARE + start + 64, :] for p in range(4)]
                blocks.append(jnp.concatenate(rows, axis=0))
            held = jnp.concatenate(blocks, axis=1)
            moved = jnp.dot(order_ref[...], held, preferred_element_type=F32)
            moved = (moved / (1.0 + jnp.exp(-moved))).astype(BF16)
            for turn in range(RANKS):
                for one in range(4):
                    block = moved[turn * 64 : turn * 64 + 64, one * LANES : (one + 1) * LANES]
                    start = step * 256 + one * 64
                    out_v[turn, quad, start : start + 64, :] = block

        leaving += started(
            [
                pltpu.make_async_copy(out_v.at[turn, quad], out_refs[quad * RANKS + turn], out_sem.at[turn, quad])
                for turn in range(RANKS)
            ]
        )
    finish(leaving)


def split(f, tokens, w, after):
    *parts, w = call(
        split_kernel,
        "split",
        [jax.ShapeDtypeStruct((SQUARE, LANES), BF16)] * (4 * RANKS) + [jax.ShapeDtypeStruct(w.shape, BF16)],
        [SMEM, ANY, ANY, ANY],
        [ANY] * (4 * RANKS + 1),
        [
            pltpu.VMEM((WIDE, WIDE), BF16),
            pltpu.VMEM((4, 4 * SQUARE, LANES), BF16),
            pltpu.VMEM((RANKS, 4, SQUARE, LANES), BF16),
            pltpu.SemaphoreType.DMA((5,)),
            pltpu.SemaphoreType.DMA((RANKS, 4)),
        ],
        flops=2**30,
        moved=8 * 2**20,
    )(f, tokens, w, after)
    return [parts[RANKS * quad : RANKS * (quad + 1)] for quad in range(4)], w


def project_kernel(f_ref, mixed_ref, *rest):
    count = mixed_ref.shape[1]
    token_refs, w_refs = rest[: RANKS * count], rest[RANKS * count : RANKS * (count + 1)]
    out_refs = rest[:-8][-RANKS * count :]
    w_all_ref, w_v, mixed_v, tokens_v, out_v, w_sem, sem, out_sem = rest[-8:]
    f = f_ref[0]
    steps, blocks, tile = mixed_v.shape[0], mixed_v.shape[1], tokens_v.shape[2]
    per_quad = SQUARE // tile
    weights = started([pltpu.make_async_copy(w_refs[turn], w_v.at[turn], w_sem.at[turn]) for turn in range(RANKS)])
    arriving = []
    for step in range(steps):
        rows = pl.ds(step % per_quad * tile, tile)
        source = mixed_ref.at[pl.ds(step % per_quad * blocks, blocks), step // per_quad]
        arriving.append(
            started(
                [pltpu.make_async_copy(source, mixed_v.at[step], sem.at[step, RANKS])]
                + [
                    pltpu.make_async_copy(
                        token_refs[step // per_quad * RANKS + turn].at[rows, :], tokens_v.at[turn, step], sem.at[step, turn]
                    )
                    for turn in range(RANKS)
                ]
            )
        )
    finish(weights)
    for row in range(RANKS):
        for column in range(RANKS):
            block = w_v[column, aligned((f ^ row) * LANES, LANES), :]
            w_all_ref[row * LANES : (row + 1) * LANES, column * LANES : (column + 1) * LANES] = block
    leaving = []
    for step in range(steps):
        finish(arriving[step])
        gated = []
        for turn in range(RANKS):
            mixed = mixed_v[step, :, :, aligned((f ^ turn) * LANES, LANES)].reshape(tile, LANES).astype(F32)
            gated.append((mixed * tokens_v[turn, step].astype(F32)).astype(BF16))
        result = jnp.dot(jnp.concatenate(gated, axis=1), w_all_ref[...], preferred_element_type=F32).astype(BF16)
        for turn in range(RANKS):
            out_v[turn, step] = result[:, turn * LANES : (turn + 1) * LANES]
            target = out_refs[step // per_quad * RANKS + turn].at[pl.ds(step % per_quad * tile, tile), :]
            leaving += started([pltpu.make_async_copy(out_v.at[turn, step], target, out_sem.at[step, turn])])
    finish(leaving)


def project(f, mixed, tokens, w, after):
    count = mixed.shape[1]
    tile = SQUARE // 2
    steps = count * SQUARE // tile
    size = steps * tile * ALL
    parts = call(
        project_kernel,
        "project",
        [jax.ShapeDtypeStruct((SQUARE, LANES), BF16)] * (RANKS * count),
        [SMEM] + [ANY] * (1 + RANKS * (count + 1) + len(after)),
        [ANY] * (RANKS * count),
        [
            pltpu.VMEM((ALL, ALL), BF16),
            pltpu.VMEM((RANKS, ALL, LANES), BF16),
            pltpu.VMEM((steps, tile // 16, 16, ALL), BF16),
            pltpu.VMEM((RANKS, steps, tile, LANES), BF16),
            pltpu.VMEM((RANKS, steps, tile, LANES), BF16),
            pltpu.SemaphoreType.DMA((RANKS,)),
            pltpu.SemaphoreType.DMA((steps, RANKS + 1)),
            pltpu.SemaphoreType.DMA((steps, RANKS)),
        ],
        flops=size * 1024,
        moved=size * 6,
    )(f, mixed, *sum(tokens, []), *w, *after)
    return [parts[RANKS * quad : RANKS * (quad + 1)] for quad in range(count)]


def merge_kernel(first_row, f_ref, *rest):
    part_refs, (out_ref, done_ref, order_ref, held_v, out_sem) = rest[:RANKS], rest[-5:]
    count = part_refs[0].shape[0] // SQUARE
    done_ref[...] = jnp.zeros_like(done_ref)
    order_ref[...] = ones_where(place_of(iota((WIDE, WIDE), 1), f_ref[0]) == iota((WIDE, WIDE), 0))
    leaving = []
    for quad in range(count):
        for step in range(4):
            blocks = []
            for one in range(4):
                start = quad * SQUARE + step * 256 + one * 64
                rows = [ref[start : start + 64, :] for ref in part_refs]
                blocks.append(jnp.concatenate(rows, axis=0))
            held = jnp.concatenate(blocks, axis=1)
            moved = jnp.dot(order_ref[...], held, preferred_element_type=F32).astype(BF16)
            for p in range(4):
                for one in range(4):
                    block = moved[p * 64 : p * 64 + 64, one * LANES : (one + 1) * LANES]
                    start = p * SQUARE + step * 256 + one * 64
                    held_v[quad, start : start + 64, :] = block

        rows = 4 * SQUARE
        target = out_ref.at[pl.ds(first_row + quad * rows, rows), :]
        leaving += started([pltpu.make_async_copy(held_v.at[quad], target, out_sem.at[quad])])
    finish(leaving)


def merge(f, parts, total, first_quad, base):
    rows = parts[0].shape[0]
    count = rows // SQUARE
    extra = [] if base is None else [base]
    return call(
        functools.partial(merge_kernel, first_quad * 4 * SQUARE),
        "merge",
        (jax.ShapeDtypeStruct((total, LANES), BF16), DONE),
        [SMEM] + [VMEM] * RANKS + [ANY] * len(extra),
        (ANY, VMEM),
        [
            pltpu.VMEM((WIDE, WIDE), BF16),
            pltpu.VMEM((count, 4 * SQUARE, LANES), BF16),
            pltpu.SemaphoreType.DMA((count,)),
        ],
        flops=rows * 4 * WIDE * LANES * 2,
        moved=rows * LANES * 16,
        aliases={5: 0} if extra else None,
        grant=SMALL,
    )(f, *parts, *extra)


TURNS = [[(rank, rank ^ turn) for rank in range(RANKS)] for turn in range(RANKS)]


def swap(parts):
    return [parts[0]] + [lax.ppermute(parts[turn], "fsdp", TURNS[turn]) for turn in (2, 1, 3)]


def in_turn(got):
    return [got[0], got[2], got[1], got[3]]


def hold_kernel(x_ref, after_ref, out_ref):
    pass


def hold(x, after):
    return call(
        hold_kernel,
        "hold",
        jax.ShapeDtypeStruct(x.shape, x.dtype),
        [ANY, ANY],
        ANY,
        [],
        flops=0,
        moved=0,
        aliases={0: 0},
        grant=SMALL,
    )(x, after)


def share(x):
    chip = lax.ppermute(x, "fsdp", TURNS[2])
    core = lax.ppermute(x, "fsdp", TURNS[1])
    far = lax.ppermute(chip, "fsdp", TURNS[1])
    return [x, core, chip, far]


def body(tokens, factor_d, factor_c, factor_b, factor_a, w_proj):
    local_rows = tokens.shape[0]
    f = lax.axis_index("fsdp").astype(jnp.int32).reshape(1)

    raw = lambda factor: factor.transpose(1, 2, 0).reshape(SQUARE, LANES)

    own = (raw(factor_d), raw(factor_c))
    chip = [lax.ppermute(x, "fsdp", TURNS[2]) for x in own]
    core = [lax.ppermute(x, "fsdp", TURNS[1]) for x in own]
    second, _ = local_steps(f, tokens, *own, None)
    second, done = local_steps(f ^ 1, tokens, *core, second)
    chip = [hold(x, done) for x in chip]
    far = [lax.ppermute(x, "fsdp", TURNS[1]) for x in chip]
    second, _ = local_steps(f ^ 2, tokens, *chip, second)
    second, done = local_steps(f ^ 3, tokens, *far, second)
    token_parts, w = split(f, tokens, w_proj, done)
    w = share(w)
    token_parts = [in_turn(swap(quad)) for quad in token_parts]
    weights_b, weights_a = weights(raw(factor_b), raw(factor_a), done)
    arrived = lax.all_to_all(
        second.reshape(64 * RANKS, 64, LANES), ("ctx", "fsdp"), split_axis=0, concat_axis=0, tiled=True
    )
    early = [part for quad in token_parts[:3] for part in quad[1:]]
    third, first_sent = middle(
        arrived.reshape(BLK, 2, RANKS, 64, LANES), weights_b, weights_a, RETURN_QUADS[0], early + w[1:]
    )

    out, first_quad, after = None, 0, []
    for k, count in enumerate(RETURN_QUADS):
        sent = step_a(third, weights_a, first_quad, count, token_parts[3][1:]) if k else first_sent
        mixed = lax.all_to_all(
            sent.reshape(64, count * 16, ALL), "ctx", split_axis=0, concat_axis=0, tiled=True
        ).reshape(64, count, 16, ALL)
        tokens_here = token_parts[first_quad : first_quad + count]
        parts = [in_turn(swap(part)) for part in project(f, mixed, tokens_here, w, after)]
        ends = []
        for part in parts:
            out, done = merge(f, part, local_rows, first_quad, out)
            first_quad += 1
            ends.append(done)
        after = ends[:1]
    return out


def solution(mesh):
    in_specs = (
        P("ctx", "fsdp"),
        P(("ctx", "fsdp"), None, None),
        P(("ctx", "fsdp"), None, None),
        P(("ctx", "fsdp"), None, None),
        P(("ctx", "fsdp"), None, None),
        P(None, "fsdp"),
    )
    out_specs = P("ctx", "fsdp")
    return jax.shard_map(body, mesh=mesh, in_specs=in_specs, out_specs=out_specs, check_vma=False)
```

```python
import functools

import jax
import jax.numpy as jnp
from jax import lax
from jax.experimental import pallas as pl
from jax.experimental.pallas import tpu as pltpu
from jax.sharding import PartitionSpec as P

BLK = 32
LANES = 128
SUB = 8
WIDE = SUB * BLK
PACK = LANES // BLK
SQUARE = BLK * BLK
RANKS = 4
ALL = RANKS * LANES
BF16 = jnp.bfloat16
F32 = jnp.float32
MIB = 1024 * 1024
LARGE, MEDIUM, SMALL = 60 * MIB, 53 * MIB, 24 * MIB
RETURN_QUADS = (2, 2)

VMEM = pl.BlockSpec(memory_space=pltpu.VMEM)
SMEM = pl.BlockSpec(memory_space=pltpu.SMEM)
HBM = pl.BlockSpec(memory_space=pltpu.HBM)
ANY = pl.BlockSpec(memory_space=pl.ANY)
FACTOR = pltpu.VMEM((LANES, SQUARE), BF16)
DONE = jax.ShapeDtypeStruct((SUB, LANES), F32)
RAW = pltpu.VMEM((SQUARE, LANES), BF16)
WIDE_SHAPE = pltpu.VMEM((4, SUB, BLK, WIDE), BF16)
SPREAD_SHAPE = pltpu.VMEM((PACK, LANES, WIDE), BF16)


def call(kernel, name, out_shape, in_specs, out_specs, scratch, flops, moved, exps=0, aliases=None, grant=SMALL):
    return pl.pallas_call(
        kernel,
        name=name,
        out_shape=out_shape,
        in_specs=in_specs,
        out_specs=out_specs,
        scratch_shapes=scratch,
        input_output_aliases=aliases or {},
        compiler_params=pltpu.CompilerParams(vmem_limit_bytes=grant),
        cost_estimate=pl.CostEstimate(flops=flops, bytes_accessed=moved, transcendentals=exps),
    )


def aligned(start, size):
    return pl.ds(pl.multiple_of(start, size), size)


def started(copies):
    for copy in copies:
        copy.start()
    return copies


def finish(copies):
    for copy in copies:
        copy.wait()


def iota(shape, axis):
    return lax.broadcasted_iota(jnp.int32, shape, axis)


def ones_where(condition):
    return jnp.where(condition, 1.0, 0.0).astype(BF16)


def take(raw, factor_ref, source_of):
    shape = (LANES, LANES)
    order = ones_where(source_of(iota(shape, 0)) == iota(shape, 1))
    factor = lax.dot_general(order, raw, (((1,), (1,)), ((), ())), preferred_element_type=F32)
    factor_ref[...] = factor.astype(BF16)


def widen_major(factor, wide_ref):
    rows = factor.astype(F32)
    block, row = iota((BLK, LANES), 1) // BLK, iota((BLK, LANES), 0) % SUB
    keeps = (block == row, block == row - PACK)
    for m in range(SUB):
        turned = rows[:, m * LANES : (m + 1) * LANES]
        rolled = [pltpu.roll(turned, turn * BLK, 1) for turn in range(1, PACK)]
        for turn in range(1, PACK):
            turned = jnp.where(row % PACK == turn, rolled[turn - 1], turned)
        for half in range(PACK // 2):
            parts = []
            for q in (2 * half, 2 * half + 1):
                here = turned if q == 0 else pltpu.roll(turned, LANES - q * BLK, 1)
                both = jnp.concatenate([jnp.where(keep, here, 0.0) for keep in keeps], axis=1)
                parts.append(both.reshape(4, SUB, WIDE))
            wide_ref[:, m, half * 16 : half * 16 + 16, :] = jnp.concatenate(parts, axis=1).astype(BF16)


def fill_spread(spread_ref):
    row, want = iota((LANES, WIDE), 0), iota((LANES, WIDE), 1) // 4 % BLK
    for q in range(PACK):
        spread_ref[q] = ones_where(row == want + q * BLK)


def widen_minor(factor, spread_ref, wide_ref):
    rows = factor.astype(F32).reshape(4, SUB, SQUARE)
    tiles = [rows[:, :, m * LANES : (m + 1) * LANES] for m in range(SUB)]
    left = jnp.stack(tiles, axis=1).reshape(WIDE, LANES).astype(BF16)
    shape = (1, SUB, WIDE)
    keep = iota(shape, 1) == iota(shape, 2) // LANES * 4 + iota(shape, 2) % 4
    for half in range(PACK // 2):
        parts = []
        for q in (2 * half, 2 * half + 1):
            part = jnp.dot(left, spread_ref[q], preferred_element_type=F32)
            parts.append(jnp.where(keep, part.reshape(BLK, SUB, WIDE), 0.0))
        both = jnp.concatenate(parts, axis=1).astype(BF16)
        wide_ref[:, :, half * 16 : half * 16 + 16, :] = both.reshape(4, SUB, 16, WIDE)


def apply(wide_ref, group, data):
    left = wide_ref[group].reshape(WIDE, WIDE)
    return jnp.dot(left, data, preferred_element_type=F32).reshape(BLK, SUB, data.shape[1])


def local_kernel(fetch, where_ref, tokens_ref, fd_ref, fc_ref, *rest):
    out_ref, done_ref, tokens_v, fd_v, fc_v, wide_ref, first_ref, out_v, sem, out_sem = rest[-10 - 2 * fetch :][:10]
    fetched = []
    if fetch:
        fetched = started(
            [pltpu.make_async_copy(ref, rest[n - 2], sem.at[4 + n]) for n, ref in enumerate((fd_ref, fc_ref))]
        )
        fd_ref, fc_ref = rest[-2:]
    done_ref[...] = jnp.zeros_like(done_ref)
    quarter = where_ref[0]
    arriving = started(
        [
            pltpu.make_async_copy(tokens_ref.at[aligned((quarter * 4 + p) * SQUARE, SQUARE), :], tokens_v.at[p], sem.at[p])
            for p in range(4)
        ]
    )
    finish(fetched)
    take(fd_ref[...], fd_v, lambda r: r)
    take(fc_ref[...], fc_v, lambda r: r // 4 % 4 * BLK + r // 16 * 4 + r % 4)
    for p in range(4):
        widen_major(fd_v[p * BLK : (p + 1) * BLK, :], wide_ref)
        arriving[p].wait()
        for pair in range(2):
            halves = [
                apply(wide_ref, group, tokens_v[p, group * WIDE : (group + 1) * WIDE, :])
                for group in (2 * pair, 2 * pair + 1)
            ]
            first_ref[p, :, pair * 16 : pair * 16 + 16, :] = jnp.concatenate(halves, axis=1).astype(BF16)
    leaving = []
    for step in range(4):
        widen_major(fc_v[step * BLK : (step + 1) * BLK, :], wide_ref)
        for one in range(2):
            quad = 2 * step + one
            halves = []
            for pair in range(2):
                held = first_ref[2 * pair : 2 * pair + 2, 4 * quad : 4 * quad + 4]
                halves.append(apply(wide_ref, 2 * one + pair, held.reshape(WIDE, LANES)))
            out_v[quad] = jnp.concatenate(halves, axis=1).astype(BF16)
            target = out_ref.at[:, quad // 4, quad % 4, quarter]
            leaving += started([pltpu.make_async_copy(out_v.at[quad], target, out_sem.at[quad])])
    finish(leaving)


def local_steps(where, tokens, factor_d, factor_c, base):
    extra = [] if base is None else [base]
    fetch = base is None
    place = HBM if fetch else VMEM
    return call(
        functools.partial(local_kernel, fetch),
        "steps_d_c",
        (jax.ShapeDtypeStruct((BLK, 2, RANKS, RANKS, 16, LANES), BF16), DONE),
        [SMEM, HBM, place, place] + [HBM] * len(extra),
        (HBM, VMEM),
        [
            pltpu.VMEM((4, SQUARE, LANES), BF16),
            FACTOR,
            FACTOR,
            WIDE_SHAPE,
            pltpu.VMEM((4, BLK, BLK, LANES), BF16),
            pltpu.VMEM((SUB, BLK, 16, LANES), BF16),
            pltpu.SemaphoreType.DMA((6,)),
            pltpu.SemaphoreType.DMA((SUB,)),
        ]
        + [RAW, RAW] * fetch,
        flops=2**31,
        moved=3 * 2**20,
        aliases={4: 0} if extra else None,
        grant=LARGE if fetch else MEDIUM,
    )(where, tokens, factor_d, factor_c, *extra)


def d_lo_minor(row):
    return row % 4 * BLK + row // 4


GROUPS = 16
WEIGHTS = jax.ShapeDtypeStruct((GROUPS, SUB, BLK, WIDE), BF16)


def weights_kernel(fb_ref, fa_ref, after_ref, *rest):
    out_refs, (fb_raw, fa_raw, factor_ref, spread_ref, sem) = rest[:2], rest[2:]
    arriving = started(
        [
            pltpu.make_async_copy(ref, raw, sem.at[n])
            for n, (ref, raw) in enumerate(((fb_ref, fb_raw), (fa_ref, fa_raw)))
        ]
    )
    fill_spread(spread_ref)
    for n, raw in enumerate((fb_raw, fa_raw)):
        arriving[n].wait()
        take(raw[...], factor_ref, d_lo_minor)
        for step in range(4):
            if n == 0:
                rows = factor_ref[step * BLK : (step + 1) * BLK, :]
            else:
                rows = [factor_ref[high * 64 + step * 16 : high * 64 + step * 16 + 16, :] for high in range(2)]
                rows = jnp.concatenate(rows, axis=0)
            widen_minor(rows, spread_ref, out_refs[n].at[pl.ds(4 * step, 4)])


def weights(factor_b, factor_a, after):
    return call(
        weights_kernel,
        "weights",
        (WEIGHTS, WEIGHTS),
        [HBM, HBM, ANY],
        (VMEM, VMEM),
        [
            RAW,
            RAW,
            FACTOR,
            SPREAD_SHAPE,
            pltpu.SemaphoreType.DMA((2,)),
        ],
        flops=2**31,
        moved=5 * 2**20,
    )(factor_b, factor_a, after)


def step_a_quad(slot, group, third_ref, row_of, wide_ref, sent_v):
    for high in range(2):
        halves = []
        for pair in range(2):
            first = row_of(high) + 2 * pair
            data = third_ref[first : first + 2].reshape(WIDE, ALL)
            halves.append(apply(wide_ref, group + 2 * high + pair, data))
        sent_v[slot, :, high] = jnp.concatenate(halves, axis=1).astype(BF16)


def middle_kernel(count, held_ref, wb_ref, wa_ref, *rest):
    third_ref, sent_ref, held_v, third_v, sent_v, sem, out_sem = rest[-7:]
    arriving = started(
        [
            pltpu.make_async_copy(held_ref.at[pl.ds(8 * step, 8)], held_v.at[pl.ds(8 * step, 8)], sem.at[step])
            for step in range(4)
        ]
    )
    leaving = []
    later = 16 - 4 * count
    for step in range(4):
        arriving[step].wait()
        for quad in range(2):
            halves = []
            for pair in range(2):
                a = 8 * step + 4 * quad + 2 * pair
                data = [held_v[a : a + 2, :, rank].reshape(WIDE, LANES) for rank in range(RANKS)]
                halves.append(apply(wb_ref, 4 * step + 2 * quad + pair, jnp.concatenate(data, axis=1)))
            first = step * BLK + quad * 16
            third_v[:, first : first + 16, :] = jnp.concatenate(halves, axis=1).astype(BF16)
        for high in range(2):
            block = (pl.ds(high * 16 + 4 * count, later), pl.ds(step * BLK, BLK))
            leaving += started(
                [pltpu.make_async_copy(third_v.at[block], third_ref.at[block], out_sem.at[step, high])]
            )
    for quad in range(count):
        step_a_quad(quad, 4 * quad, third_v, lambda high: high * 16 + quad * 4, wa_ref, sent_v)
        leaving += started([pltpu.make_async_copy(sent_v.at[quad], sent_ref.at[:, :, quad], out_sem.at[4, quad])])
    finish(leaving)


def sent_shape(count):
    return jax.ShapeDtypeStruct((BLK, 2, count, 16, ALL), BF16)


def middle(held, weights_b, weights_a, count, after):
    return call(
        functools.partial(middle_kernel, count),
        "steps_b_a",
        (jax.ShapeDtypeStruct((BLK, LANES, ALL), BF16), sent_shape(count)),
        [HBM, VMEM, VMEM] + [ANY] * len(after),
        (HBM, HBM),
        [
            pltpu.VMEM(held.shape, BF16),
            pltpu.VMEM((BLK, LANES, ALL), BF16),
            pltpu.VMEM((count, BLK, 2, 16, ALL), BF16),
            pltpu.SemaphoreType.DMA((4,)),
            pltpu.SemaphoreType.DMA((5, max(2, count))),
        ],
        flops=2**32,
        moved=9 * 2**20,
    )(held, weights_b, weights_a, *after)


def step_a_kernel(first_quad, count, third_ref, wa_ref, *rest):
    sent_ref, third_v, sent_v, sem, out_sem = rest[-5:]
    arriving = started(
        [
            pltpu.make_async_copy(
                third_ref.at[pl.ds(high * 16 + 4 * first_quad, 4 * count)],
                third_v.at[pl.ds(high * 4 * count, 4 * count)],
                sem.at[high],
            )
            for high in range(2)
        ]
    )
    finish(arriving)
    leaving = []
    for slot in range(count):
        step_a_quad(slot, 4 * (first_quad + slot), third_v, lambda high: (high * count + slot) * 4, wa_ref, sent_v)
        leaving += started([pltpu.make_async_copy(sent_v.at[slot], sent_ref.at[:, :, slot], out_sem.at[slot])])
    finish(leaving)


def step_a(third, weights_a, first_quad, count, after):
    return call(
        functools.partial(step_a_kernel, first_quad, count),
        "step_a",
        sent_shape(count),
        [HBM, VMEM] + [ANY] * len(after),
        HBM,
        [
            pltpu.VMEM((8 * count, LANES, ALL), BF16),
            pltpu.VMEM((count, BLK, 2, 16, ALL), BF16),
            pltpu.SemaphoreType.DMA((2,)),
            pltpu.SemaphoreType.DMA((count,)),
        ],
        flops=2**29 * count,
        moved=2**21 * count,
    )(third, weights_a, *after)


def place_of(row, f):
    turn, s, p, low = row // 64, row // 16 % 4, row // 4 % 4, row % 4
    return p * 64 + s * 16 + (turn ^ f) * 4 + low


def split_kernel(f_ref, tokens_ref, w_ref, after_ref, *rest):
    out_refs, w_out_ref = rest[: 4 * RANKS], rest[4 * RANKS]
    order_ref, tokens_v, out_v, sem, out_sem = rest[4 * RANKS + 1 :]
    leaving = started([pltpu.make_async_copy(w_ref, w_out_ref, sem.at[4])])
    size = 4 * SQUARE
    arriving = started(
        [
            pltpu.make_async_copy(tokens_ref.at[pl.ds(quad * size, size), :], tokens_v.at[quad], sem.at[quad])
            for quad in range(4)
        ]
    )
    order_ref[...] = ones_where(place_of(iota((WIDE, WIDE), 0), f_ref[0]) == iota((WIDE, WIDE), 1))
    for quad in range(4):
        arriving[quad].wait()

        for step in range(4):
            blocks = []
            for one in range(4):
                start = step * 256 + one * 64
                rows = [tokens_v[quad, p * SQUARE + start : p * SQUARE + start + 64, :] for p in range(4)]
                blocks.append(jnp.concatenate(rows, axis=0))
            held = jnp.concatenate(blocks, axis=1)
            moved = jnp.dot(order_ref[...], held, preferred_element_type=F32).astype(BF16)
            for turn in range(RANKS):
                for one in range(4):
                    block = moved[turn * 64 : turn * 64 + 64, one * LANES : (one + 1) * LANES]
                    start = step * 256 + one * 64
                    out_v[turn, quad, start : start + 64, :] = block

        leaving += started(
            [
                pltpu.make_async_copy(out_v.at[turn, quad], out_refs[quad * RANKS + turn], out_sem.at[turn, quad])
                for turn in range(RANKS)
            ]
        )
    finish(leaving)


def split(f, tokens, w, after):
    *parts, w = call(
        split_kernel,
        "split",
        [jax.ShapeDtypeStruct((SQUARE, LANES), BF16)] * (4 * RANKS) + [jax.ShapeDtypeStruct(w.shape, BF16)],
        [SMEM, HBM, HBM, ANY],
        [HBM] * (4 * RANKS + 1),
        [
            pltpu.VMEM((WIDE, WIDE), BF16),
            pltpu.VMEM((4, 4 * SQUARE, LANES), BF16),
            pltpu.VMEM((RANKS, 4, SQUARE, LANES), BF16),
            pltpu.SemaphoreType.DMA((5,)),
            pltpu.SemaphoreType.DMA((RANKS, 4)),
        ],
        flops=2**30,
        moved=8 * 2**20,
        grant=LARGE,
    )(f, tokens, w, after)
    return [parts[RANKS * quad : RANKS * (quad + 1)] for quad in range(4)], w


def project_kernel(f_ref, mixed_ref, *rest):
    count = mixed_ref.shape[1]
    token_refs, w_refs = rest[: RANKS * count], rest[RANKS * count : RANKS * (count + 1)]
    out_refs, w_all_ref = rest[:-1][-RANKS * count :], rest[-1]
    f = f_ref[0]
    for row in range(RANKS):
        for column in range(RANKS):
            block = w_refs[column][aligned((f ^ row) * LANES, LANES), :]
            w_all_ref[row * LANES : (row + 1) * LANES, column * LANES : (column + 1) * LANES] = block
    tile = SQUARE // 2
    for quad in range(count):
        for half in range(2):
            rows, blocks = slice(half * tile, (half + 1) * tile), slice(half * 32, (half + 1) * 32)
            gated = []
            for turn in range(RANKS):
                mixed = mixed_ref[blocks, quad, :, aligned((f ^ turn) * LANES, LANES)].reshape(tile, LANES)
                value = token_refs[RANKS * quad + turn][rows, :].astype(F32)
                gated.append((mixed.astype(F32) * (value / (1.0 + jnp.exp(-value)))).astype(BF16))
            result = jnp.dot(jnp.concatenate(gated, axis=1), w_all_ref[...], preferred_element_type=F32).astype(BF16)
            for turn in range(RANKS):
                out_refs[RANKS * quad + turn][rows, :] = result[:, turn * LANES : (turn + 1) * LANES]


def project(f, mixed, tokens, w, after):
    count = mixed.shape[1]
    size = count * SQUARE * ALL
    parts = call(
        project_kernel,
        "project",
        [jax.ShapeDtypeStruct((SQUARE, LANES), BF16)] * (RANKS * count),
        [SMEM] + [VMEM] * (1 + RANKS * (count + 1)) + [ANY] * len(after),
        [VMEM] * (RANKS * count),
        [pltpu.VMEM((ALL, ALL), BF16)],
        flops=size * 1024,
        moved=size * 6,
        exps=size,
    )(f, mixed, *sum(tokens, []), *w, *after)
    return [parts[RANKS * quad : RANKS * (quad + 1)] for quad in range(count)]


def merge_kernel(first_row, f_ref, *rest):
    part_refs, (out_ref, done_ref, order_ref, held_v, out_sem) = rest[:RANKS], rest[-5:]
    count = part_refs[0].shape[0] // SQUARE
    done_ref[...] = jnp.zeros_like(done_ref)
    order_ref[...] = ones_where(place_of(iota((WIDE, WIDE), 1), f_ref[0]) == iota((WIDE, WIDE), 0))
    leaving = []
    for quad in range(count):
        for step in range(4):
            blocks = []
            for one in range(4):
                start = quad * SQUARE + step * 256 + one * 64
                rows = [ref[start : start + 64, :] for ref in part_refs]
                blocks.append(jnp.concatenate(rows, axis=0))
            held = jnp.concatenate(blocks, axis=1)
            moved = jnp.dot(order_ref[...], held, preferred_element_type=F32).astype(BF16)
            for p in range(4):
                for one in range(4):
                    block = moved[p * 64 : p * 64 + 64, one * LANES : (one + 1) * LANES]
                    start = p * SQUARE + step * 256 + one * 64
                    held_v[quad, start : start + 64, :] = block

        rows = 4 * SQUARE
        target = out_ref.at[pl.ds(first_row + quad * rows, rows), :]
        leaving += started([pltpu.make_async_copy(held_v.at[quad], target, out_sem.at[quad])])
    finish(leaving)


def merge(f, parts, total, first_quad, base):
    rows = parts[0].shape[0]
    count = rows // SQUARE
    extra = [] if base is None else [base]
    return call(
        functools.partial(merge_kernel, first_quad * 4 * SQUARE),
        "merge",
        (jax.ShapeDtypeStruct((total, LANES), BF16), DONE),
        [SMEM] + [VMEM] * RANKS + [HBM] * len(extra),
        (HBM, VMEM),
        [
            pltpu.VMEM((WIDE, WIDE), BF16),
            pltpu.VMEM((count, 4 * SQUARE, LANES), BF16),
            pltpu.SemaphoreType.DMA((count,)),
        ],
        flops=rows * 4 * WIDE * LANES * 2,
        moved=rows * LANES * 16,
        aliases={5: 0} if extra else None,
    )(f, *parts, *extra)


TURNS = [[(rank, rank ^ turn) for rank in range(RANKS)] for turn in range(RANKS)]


def swap(parts):
    return [parts[0]] + [lax.ppermute(parts[turn], "fsdp", TURNS[turn]) for turn in (2, 1, 3)]


def in_turn(got):
    return [got[0], got[2], got[1], got[3]]


def hold_kernel(x_ref, after_ref, out_ref):
    pass


def hold(x, after):
    return call(
        hold_kernel,
        "hold",
        jax.ShapeDtypeStruct(x.shape, x.dtype),
        [ANY, ANY],
        ANY,
        [],
        flops=0,
        moved=0,
        aliases={0: 0},
    )(x, after)


def share(x):
    chip = lax.ppermute(x, "fsdp", TURNS[2])
    core = lax.ppermute(x, "fsdp", TURNS[1])
    far = lax.ppermute(chip, "fsdp", TURNS[1])
    return [x, core, chip, far]


def body(tokens, factor_d, factor_c, factor_b, factor_a, w_proj):
    local_rows = tokens.shape[0]
    f = lax.axis_index("fsdp").astype(jnp.int32).reshape(1)

    raw = lambda factor: factor.transpose(1, 2, 0).reshape(SQUARE, LANES)

    own = (raw(factor_d), raw(factor_c))
    chip = [lax.ppermute(x, "fsdp", TURNS[2]) for x in own]
    core = [lax.ppermute(x, "fsdp", TURNS[1]) for x in own]
    second, _ = local_steps(f, tokens, *own, None)
    second, done = local_steps(f ^ 1, tokens, *core, second)
    chip = [hold(x, done) for x in chip]
    far = [lax.ppermute(x, "fsdp", TURNS[1]) for x in chip]
    second, _ = local_steps(f ^ 2, tokens, *chip, second)
    second, done = local_steps(f ^ 3, tokens, *far, second)
    token_parts, w = split(f, tokens, w_proj, done)
    w = share(w)
    token_parts = [in_turn(swap(quad)) for quad in token_parts]
    weights_b, weights_a = weights(raw(factor_b), raw(factor_a), done)
    arrived = lax.all_to_all(
        second.reshape(64 * RANKS, 64, LANES), ("ctx", "fsdp"), split_axis=0, concat_axis=0, tiled=True
    )
    early = [part for quad in token_parts[:3] for part in quad[1:]]
    third, first_sent = middle(
        arrived.reshape(BLK, 2, RANKS, 64, LANES), weights_b, weights_a, RETURN_QUADS[0], early + w[1:]
    )

    out, first_quad, after = None, 0, []
    for k, count in enumerate(RETURN_QUADS):
        sent = step_a(third, weights_a, first_quad, count, token_parts[3][1:]) if k else first_sent
        mixed = lax.all_to_all(
            sent.reshape(64, count * 16, ALL), "ctx", split_axis=0, concat_axis=0, tiled=True
        ).reshape(64, count, 16, ALL)
        tokens_here = token_parts[first_quad : first_quad + count]
        parts = [in_turn(swap(part)) for part in project(f, mixed, tokens_here, w, after)]
        ends = []
        for part in parts:
            out, done = merge(f, part, local_rows, first_quad, out)
            first_quad += 1
            ends.append(done)
        after = ends[:1]
    return out


def solution(mesh):
    in_specs = (
        P("ctx", "fsdp"),
        P(("ctx", "fsdp"), None, None),
        P(("ctx", "fsdp"), None, None),
        P(("ctx", "fsdp"), None, None),
        P(("ctx", "fsdp"), None, None),
        P(None, "fsdp"),
    )
    out_specs = P("ctx", "fsdp")
    return jax.shard_map(body, mesh=mesh, in_specs=in_specs, out_specs=out_specs, check_vma=False)
```

```python
import functools

import jax
import jax.numpy as jnp
from jax import lax
from jax.experimental import pallas as pl
from jax.experimental.pallas import tpu as pltpu
from jax.sharding import PartitionSpec as P

BLK = 32
LANES = 128
SUB = 8
WIDE = SUB * BLK
PACK = LANES // BLK
SQUARE = BLK * BLK
RANKS = 4
ALL = RANKS * LANES
BF16 = jnp.bfloat16
F32 = jnp.float32
MIB = 1024 * 1024
LARGE, MEDIUM, SMALL = 60 * MIB, 53 * MIB, 24 * MIB
RETURN_QUADS = (2, 2)

VMEM = pl.BlockSpec(memory_space=pltpu.VMEM)
SMEM = pl.BlockSpec(memory_space=pltpu.SMEM)
ANY = pl.BlockSpec(memory_space=pl.ANY)
FACTOR = pltpu.VMEM((LANES, SQUARE), BF16)
DONE = jax.ShapeDtypeStruct((SUB, LANES), F32)
RAW = pltpu.VMEM((SQUARE, LANES), BF16)
WIDE_SHAPE = pltpu.VMEM((4, SUB, BLK, WIDE), BF16)
SPREAD_SHAPE = pltpu.VMEM((PACK, LANES, WIDE), BF16)


def call(kernel, name, out_shape, in_specs, out_specs, scratch, flops, moved, exps=0, aliases=None, grant=LARGE):
    return pl.pallas_call(
        kernel,
        name=name,
        out_shape=out_shape,
        in_specs=in_specs,
        out_specs=out_specs,
        scratch_shapes=scratch,
        input_output_aliases=aliases or {},
        compiler_params=pltpu.CompilerParams(vmem_limit_bytes=grant),
        cost_estimate=pl.CostEstimate(flops=flops, bytes_accessed=moved, transcendentals=exps),
    )


def aligned(start, size):
    return pl.ds(pl.multiple_of(start, size), size)


def started(copies):
    for copy in copies:
        copy.start()
    return copies


def finish(copies):
    for copy in copies:
        copy.wait()


def iota(shape, axis):
    return lax.broadcasted_iota(jnp.int32, shape, axis)


def ones_where(condition):
    return jnp.where(condition, 1.0, 0.0).astype(BF16)


def take(raw, factor_ref, source_of):
    shape = (LANES, LANES)
    order = ones_where(source_of(iota(shape, 0)) == iota(shape, 1))
    factor = lax.dot_general(order, raw, (((1,), (1,)), ((), ())), preferred_element_type=F32)
    factor_ref[...] = factor.astype(BF16)


def widen_major(factor, wide_ref):
    rows = factor.astype(F32)
    block, row = iota((BLK, LANES), 1) // BLK, iota((BLK, LANES), 0) % SUB
    keeps = (block == row, block == row - PACK)
    for m in range(SUB):
        turned = rows[:, m * LANES : (m + 1) * LANES]
        rolled = [pltpu.roll(turned, turn * BLK, 1) for turn in range(1, PACK)]
        for turn in range(1, PACK):
            turned = jnp.where(row % PACK == turn, rolled[turn - 1], turned)
        for half in range(PACK // 2):
            parts = []
            for q in (2 * half, 2 * half + 1):
                here = turned if q == 0 else pltpu.roll(turned, LANES - q * BLK, 1)
                both = jnp.concatenate([jnp.where(keep, here, 0.0) for keep in keeps], axis=1)
                parts.append(both.reshape(4, SUB, WIDE))
            wide_ref[:, m, half * 16 : half * 16 + 16, :] = jnp.concatenate(parts, axis=1).astype(BF16)


def fill_spread(spread_ref):
    row, want = iota((LANES, WIDE), 0), iota((LANES, WIDE), 1) // 4 % BLK
    for q in range(PACK):
        spread_ref[q] = ones_where(row == want + q * BLK)


def widen_minor(factor, spread_ref, wide_ref):
    rows = factor.astype(F32).reshape(4, SUB, SQUARE)
    tiles = [rows[:, :, m * LANES : (m + 1) * LANES] for m in range(SUB)]
    left = jnp.stack(tiles, axis=1).reshape(WIDE, LANES).astype(BF16)
    shape = (1, SUB, WIDE)
    keep = iota(shape, 1) == iota(shape, 2) // LANES * 4 + iota(shape, 2) % 4
    for half in range(PACK // 2):
        parts = []
        for q in (2 * half, 2 * half + 1):
            part = jnp.dot(left, spread_ref[q], preferred_element_type=F32)
            parts.append(jnp.where(keep, part.reshape(BLK, SUB, WIDE), 0.0))
        both = jnp.concatenate(parts, axis=1).astype(BF16)
        wide_ref[:, :, half * 16 : half * 16 + 16, :] = both.reshape(4, SUB, 16, WIDE)


def apply(wide_ref, group, data):
    left = wide_ref[group].reshape(WIDE, WIDE)
    return jnp.dot(left, data, preferred_element_type=F32).reshape(BLK, SUB, data.shape[1])


def local_kernel(fetch, where_ref, tokens_ref, fd_ref, fc_ref, *rest):
    out_ref, done_ref, tokens_v, fd_v, fc_v, wide_ref, first_ref, out_v, sem, out_sem = rest[-10 - 2 * fetch :][:10]
    fetched = []
    if fetch:
        fetched = started(
            [pltpu.make_async_copy(ref, rest[n - 2], sem.at[4 + n]) for n, ref in enumerate((fd_ref, fc_ref))]
        )
        fd_ref, fc_ref = rest[-2:]
    done_ref[...] = jnp.zeros_like(done_ref)
    quarter = where_ref[0]
    arriving = started(
        [
            pltpu.make_async_copy(tokens_ref.at[aligned((quarter * 4 + p) * SQUARE, SQUARE), :], tokens_v.at[p], sem.at[p])
            for p in range(4)
        ]
    )
    finish(fetched)
    take(fd_ref[...], fd_v, lambda r: r)
    take(fc_ref[...], fc_v, lambda r: r // 4 % 4 * BLK + r // 16 * 4 + r % 4)
    for p in range(4):
        widen_major(fd_v[p * BLK : (p + 1) * BLK, :], wide_ref)
        arriving[p].wait()
        for pair in range(2):
            halves = [
                apply(wide_ref, group, tokens_v[p, group * WIDE : (group + 1) * WIDE, :])
                for group in (2 * pair, 2 * pair + 1)
            ]
            first_ref[p, :, pair * 16 : pair * 16 + 16, :] = jnp.concatenate(halves, axis=1).astype(BF16)
    leaving = []
    for step in range(4):
        widen_major(fc_v[step * BLK : (step + 1) * BLK, :], wide_ref)
        for one in range(2):
            quad = 2 * step + one
            halves = []
            for pair in range(2):
                held = first_ref[2 * pair : 2 * pair + 2, 4 * quad : 4 * quad + 4]
                halves.append(apply(wide_ref, 2 * one + pair, held.reshape(WIDE, LANES)))
            out_v[quad] = jnp.concatenate(halves, axis=1).astype(BF16)
            target = out_ref.at[:, quad // 4, quad % 4, quarter]
            leaving += started([pltpu.make_async_copy(out_v.at[quad], target, out_sem.at[quad])])
    finish(leaving)


def local_steps(where, tokens, factor_d, factor_c, base):
    extra = [] if base is None else [base]
    fetch = base is None
    place = ANY if fetch else VMEM
    return call(
        functools.partial(local_kernel, fetch),
        "steps_d_c",
        (jax.ShapeDtypeStruct((BLK, 2, RANKS, RANKS, 16, LANES), BF16), DONE),
        [SMEM, ANY, place, place] + [ANY] * len(extra),
        (ANY, VMEM),
        [
            pltpu.VMEM((4, SQUARE, LANES), BF16),
            FACTOR,
            FACTOR,
            WIDE_SHAPE,
            pltpu.VMEM((4, BLK, BLK, LANES), BF16),
            pltpu.VMEM((SUB, BLK, 16, LANES), BF16),
            pltpu.SemaphoreType.DMA((6,)),
            pltpu.SemaphoreType.DMA((SUB,)),
        ]
        + [RAW, RAW] * fetch,
        flops=2**31,
        moved=3 * 2**20,
        aliases={4: 0} if extra else None,
        grant=LARGE if fetch else MEDIUM,
    )(where, tokens, factor_d, factor_c, *extra)


def d_lo_minor(row):
    return row % 4 * BLK + row // 4


def quad_rows(factor_ref, quad):
    rows = [factor_ref[high * 64 + quad * 16 : high * 64 + quad * 16 + 16, :] for high in range(2)]
    return jnp.concatenate(rows, axis=0)


def step_a_quad(slot, factor, third_ref, row_of, spread_ref, wide_ref, sent_v):
    widen_minor(factor, spread_ref, wide_ref)
    for high in range(2):
        halves = []
        for pair in range(2):
            first = row_of(high) + 2 * pair
            data = third_ref[first : first + 2].reshape(WIDE, ALL)
            halves.append(apply(wide_ref, 2 * high + pair, data))
        sent_v[slot, :, high] = jnp.concatenate(halves, axis=1).astype(BF16)


def middle_kernel(count, held_ref, fb_ref, fa_ref, *rest):
    third_ref, sent_ref, held_v, fb_raw, fa_raw, fb_v, fa_v = rest[-14:-7]
    wide_b, wide_a, spread_ref, third_v, sent_v, sem, out_sem = rest[-7:]
    factors = started(
        [pltpu.make_async_copy(fb_ref, fb_raw, sem.at[4]), pltpu.make_async_copy(fa_ref, fa_raw, sem.at[5])]
    )
    arriving = started(
        [
            pltpu.make_async_copy(held_ref.at[pl.ds(8 * step, 8)], held_v.at[pl.ds(8 * step, 8)], sem.at[step])
            for step in range(4)
        ]
    )
    fill_spread(spread_ref)
    finish(factors)
    take(fb_raw[...], fb_v, d_lo_minor)
    take(fa_raw[...], fa_v, d_lo_minor)
    leaving = []
    later = 16 - 4 * count
    for step in range(4):
        widen_minor(fb_v[step * BLK : (step + 1) * BLK, :], spread_ref, wide_b.at[step])
        arriving[step].wait()
        for quad in range(2):
            halves = []
            for pair in range(2):
                a = 8 * step + 4 * quad + 2 * pair
                data = [held_v[a : a + 2, :, rank].reshape(WIDE, LANES) for rank in range(RANKS)]
                halves.append(apply(wide_b.at[step], 2 * quad + pair, jnp.concatenate(data, axis=1)))
            first = step * BLK + quad * 16
            third_v[:, first : first + 16, :] = jnp.concatenate(halves, axis=1).astype(BF16)
        for high in range(2):
            block = (pl.ds(high * 16 + 4 * count, later), pl.ds(step * BLK, BLK))
            leaving += started(
                [pltpu.make_async_copy(third_v.at[block], third_ref.at[block], out_sem.at[step, high])]
            )
    for quad in range(count):
        row_of = lambda high: high * 16 + quad * 4
        step_a_quad(quad, quad_rows(fa_v, quad), third_v, row_of, spread_ref, wide_a.at[quad], sent_v)
        leaving += started([pltpu.make_async_copy(sent_v.at[quad], sent_ref.at[:, :, quad], out_sem.at[4, quad])])
    finish(leaving)


def sent_shape(count):
    return jax.ShapeDtypeStruct((BLK, 2, count, 16, ALL), BF16)


def middle(held, factor_b, factor_a, count, after):
    return call(
        functools.partial(middle_kernel, count),
        "steps_b_a",
        (jax.ShapeDtypeStruct((BLK, LANES, ALL), BF16), sent_shape(count)),
        [ANY] * (3 + len(after)),
        (ANY, ANY),
        [
            pltpu.VMEM(held.shape, BF16),
            RAW,
            RAW,
            FACTOR,
            FACTOR,
            pltpu.VMEM((4, 4, SUB, BLK, WIDE), BF16),
            pltpu.VMEM((count, 4, SUB, BLK, WIDE), BF16),
            SPREAD_SHAPE,
            pltpu.VMEM((BLK, LANES, ALL), BF16),
            pltpu.VMEM((count, BLK, 2, 16, ALL), BF16),
            pltpu.SemaphoreType.DMA((6,)),
            pltpu.SemaphoreType.DMA((5, max(2, count))),
        ],
        flops=2**32,
        moved=9 * 2**20,
    )(held, factor_b, factor_a, *after)


def step_a_kernel(first_quad, count, third_ref, fa_ref, *rest):
    sent_ref, third_v, fa_raw, fa_v, wide_ref, spread_ref, sent_v, sem, out_sem = rest[-9:]
    arriving = started(
        [pltpu.make_async_copy(fa_ref, fa_raw, sem.at[2])]
        + [
            pltpu.make_async_copy(
                third_ref.at[pl.ds(high * 16 + 4 * first_quad, 4 * count)],
                third_v.at[pl.ds(high * 4 * count, 4 * count)],
                sem.at[high],
            )
            for high in range(2)
        ]
    )
    fill_spread(spread_ref)
    finish(arriving)
    take(fa_raw[...], fa_v, d_lo_minor)
    leaving = []
    for slot in range(count):
        row_of = lambda high: (high * count + slot) * 4
        step_a_quad(slot, quad_rows(fa_v, first_quad + slot), third_v, row_of, spread_ref, wide_ref, sent_v)
        leaving += started([pltpu.make_async_copy(sent_v.at[slot], sent_ref.at[:, :, slot], out_sem.at[slot])])
    finish(leaving)


def step_a(third, factor_a, first_quad, count, after):
    return call(
        functools.partial(step_a_kernel, first_quad, count),
        "step_a",
        sent_shape(count),
        [ANY] * (2 + len(after)),
        ANY,
        [
            pltpu.VMEM((8 * count, LANES, ALL), BF16),
            RAW,
            FACTOR,
            WIDE_SHAPE,
            SPREAD_SHAPE,
            pltpu.VMEM((count, BLK, 2, 16, ALL), BF16),
            pltpu.SemaphoreType.DMA((3,)),
            pltpu.SemaphoreType.DMA((count,)),
        ],
        flops=2**29 * count,
        moved=2**21 * count,
    )(third, factor_a, *after)


def place_of(row, f):
    turn, s, p, low = row // 64, row // 16 % 4, row // 4 % 4, row % 4
    return p * 64 + s * 16 + (turn ^ f) * 4 + low


def split_kernel(f_ref, tokens_ref, w_ref, after_ref, *rest):
    out_refs, w_out_ref = rest[: 4 * RANKS], rest[4 * RANKS]
    order_ref, tokens_v, out_v, sem, out_sem = rest[4 * RANKS + 1 :]
    leaving = started([pltpu.make_async_copy(w_ref, w_out_ref, sem.at[4])])
    size = 4 * SQUARE
    arriving = started(
        [
            pltpu.make_async_copy(tokens_ref.at[pl.ds(quad * size, size), :], tokens_v.at[quad], sem.at[quad])
            for quad in range(4)
        ]
    )
    order_ref[...] = ones_where(place_of(iota((WIDE, WIDE), 0), f_ref[0]) == iota((WIDE, WIDE), 1))
    for quad in range(4):
        arriving[quad].wait()

        for step in range(4):
            blocks = []
            for one in range(4):
                start = step * 256 + one * 64
                rows = [tokens_v[quad, p * SQUARE + start : p * SQUARE + start + 64, :] for p in range(4)]
                blocks.append(jnp.concatenate(rows, axis=0))
            held = jnp.concatenate(blocks, axis=1)
            moved = jnp.dot(order_ref[...], held, preferred_element_type=F32).astype(BF16)
            for turn in range(RANKS):
                for one in range(4):
                    block = moved[turn * 64 : turn * 64 + 64, one * LANES : (one + 1) * LANES]
                    start = step * 256 + one * 64
                    out_v[turn, quad, start : start + 64, :] = block

        leaving += started(
            [
                pltpu.make_async_copy(out_v.at[turn, quad], out_refs[quad * RANKS + turn], out_sem.at[turn, quad])
                for turn in range(RANKS)
            ]
        )
    finish(leaving)


def split(f, tokens, w, after):
    *parts, w = call(
        split_kernel,
        "split",
        [jax.ShapeDtypeStruct((SQUARE, LANES), BF16)] * (4 * RANKS) + [jax.ShapeDtypeStruct(w.shape, BF16)],
        [SMEM, ANY, ANY, ANY],
        [ANY] * (4 * RANKS + 1),
        [
            pltpu.VMEM((WIDE, WIDE), BF16),
            pltpu.VMEM((4, 4 * SQUARE, LANES), BF16),
            pltpu.VMEM((RANKS, 4, SQUARE, LANES), BF16),
            pltpu.SemaphoreType.DMA((5,)),
            pltpu.SemaphoreType.DMA((RANKS, 4)),
        ],
        flops=2**30,
        moved=8 * 2**20,
    )(f, tokens, w, after)
    return [parts[RANKS * quad : RANKS * (quad + 1)] for quad in range(4)], w


def project_kernel(first, count, f_ref, mixed_ref, *rest):
    token_refs, w_refs = rest[: RANKS * count], rest[RANKS * count : RANKS * (count + 1)]
    out_refs = rest[:-8][-RANKS * count :]
    w_all_ref, w_v, mixed_v, tokens_v, out_v, w_sem, sem, out_sem = rest[-8:]
    f = f_ref[0]
    steps, blocks, tile = mixed_v.shape[0], mixed_v.shape[1], tokens_v.shape[2]
    per_quad = SQUARE // tile
    weights = started([pltpu.make_async_copy(w_refs[turn], w_v.at[turn], w_sem.at[turn]) for turn in range(RANKS)])
    arriving = []
    for step in range(steps):
        rows = pl.ds(step % per_quad * tile, tile)
        source = mixed_ref.at[pl.ds(step % per_quad * blocks, blocks), first + step // per_quad]
        arriving.append(
            started(
                [pltpu.make_async_copy(source, mixed_v.at[step], sem.at[step, RANKS])]
                + [
                    pltpu.make_async_copy(
                        token_refs[step // per_quad * RANKS + turn].at[rows, :], tokens_v.at[turn, step], sem.at[step, turn]
                    )
                    for turn in range(RANKS)
                ]
            )
        )
    finish(weights)
    for row in range(RANKS):
        for column in range(RANKS):
            block = w_v[column, aligned((f ^ row) * LANES, LANES), :]
            w_all_ref[row * LANES : (row + 1) * LANES, column * LANES : (column + 1) * LANES] = block
    leaving = []
    for step in range(steps):
        finish(arriving[step])
        gated = []
        for turn in range(RANKS):
            mixed = mixed_v[step, :, :, aligned((f ^ turn) * LANES, LANES)].reshape(tile, LANES).astype(F32)
            value = tokens_v[turn, step].astype(F32)
            gated.append((mixed * (value / (1.0 + jnp.exp(-value)))).astype(BF16))
        result = jnp.dot(jnp.concatenate(gated, axis=1), w_all_ref[...], preferred_element_type=F32).astype(BF16)
        for turn in range(RANKS):
            out_v[turn, step] = result[:, turn * LANES : (turn + 1) * LANES]
            target = out_refs[step // per_quad * RANKS + turn].at[pl.ds(step % per_quad * tile, tile), :]
            leaving += started([pltpu.make_async_copy(out_v.at[turn, step], target, out_sem.at[step, turn])])
    finish(leaving)


def project(f, mixed, tokens, w, first, count, after):
    tile = SQUARE // 2
    steps = count * SQUARE // tile
    size = steps * tile * ALL
    parts = call(
        functools.partial(project_kernel, first, count),
        "project",
        [jax.ShapeDtypeStruct((SQUARE, LANES), BF16)] * (RANKS * count),
        [SMEM] + [ANY] * (1 + RANKS * (count + 1) + len(after)),
        [ANY] * (RANKS * count),
        [
            pltpu.VMEM((ALL, ALL), BF16),
            pltpu.VMEM((RANKS, ALL, LANES), BF16),
            pltpu.VMEM((steps, tile // 16, 16, ALL), BF16),
            pltpu.VMEM((RANKS, steps, tile, LANES), BF16),
            pltpu.VMEM((RANKS, steps, tile, LANES), BF16),
            pltpu.SemaphoreType.DMA((RANKS,)),
            pltpu.SemaphoreType.DMA((steps, RANKS + 1)),
            pltpu.SemaphoreType.DMA((steps, RANKS)),
        ],
        flops=size * 1024,
        moved=size * 6,
    )(f, mixed, *sum(tokens, []), *w, *after)
    return [parts[RANKS * quad : RANKS * (quad + 1)] for quad in range(count)]


def merge_kernel(first_row, f_ref, *rest):
    part_refs, (out_ref, done_ref, order_ref, held_v, out_sem) = rest[:RANKS], rest[-5:]
    count = part_refs[0].shape[0] // SQUARE
    done_ref[...] = jnp.zeros_like(done_ref)
    order_ref[...] = ones_where(place_of(iota((WIDE, WIDE), 1), f_ref[0]) == iota((WIDE, WIDE), 0))
    leaving = []
    for quad in range(count):
        for step in range(4):
            blocks = []
            for one in range(4):
                start = quad * SQUARE + step * 256 + one * 64
                rows = [ref[start : start + 64, :] for ref in part_refs]
                blocks.append(jnp.concatenate(rows, axis=0))
            held = jnp.concatenate(blocks, axis=1)
            moved = jnp.dot(order_ref[...], held, preferred_element_type=F32).astype(BF16)
            for p in range(4):
                for one in range(4):
                    block = moved[p * 64 : p * 64 + 64, one * LANES : (one + 1) * LANES]
                    start = p * SQUARE + step * 256 + one * 64
                    held_v[quad, start : start + 64, :] = block

        rows = 4 * SQUARE
        target = out_ref.at[pl.ds(first_row + quad * rows, rows), :]
        leaving += started([pltpu.make_async_copy(held_v.at[quad], target, out_sem.at[quad])])
    finish(leaving)


def merge(f, parts, total, first_quad, base):
    rows = parts[0].shape[0]
    count = rows // SQUARE
    extra = [] if base is None else [base]
    return call(
        functools.partial(merge_kernel, first_quad * 4 * SQUARE),
        "merge",
        (jax.ShapeDtypeStruct((total, LANES), BF16), DONE),
        [SMEM] + [VMEM] * RANKS + [ANY] * len(extra),
        (ANY, VMEM),
        [
            pltpu.VMEM((WIDE, WIDE), BF16),
            pltpu.VMEM((count, 4 * SQUARE, LANES), BF16),
            pltpu.SemaphoreType.DMA((count,)),
        ],
        flops=rows * 4 * WIDE * LANES * 2,
        moved=rows * LANES * 16,
        aliases={5: 0} if extra else None,
        grant=SMALL,
    )(f, *parts, *extra)


TURNS = [[(rank, rank ^ turn) for rank in range(RANKS)] for turn in range(RANKS)]


def swap(parts):
    return [parts[0]] + [lax.ppermute(parts[turn], "fsdp", TURNS[turn]) for turn in (2, 1, 3)]


def in_turn(got):
    return [got[0], got[2], got[1], got[3]]


def hold_kernel(x_ref, after_ref, out_ref):
    pass


def hold(x, after):
    return call(
        hold_kernel,
        "hold",
        jax.ShapeDtypeStruct(x.shape, x.dtype),
        [ANY, ANY],
        ANY,
        [],
        flops=0,
        moved=0,
        aliases={0: 0},
        grant=SMALL,
    )(x, after)


def share(x):
    chip = lax.ppermute(x, "fsdp", TURNS[2])
    core = lax.ppermute(x, "fsdp", TURNS[1])
    far = lax.ppermute(chip, "fsdp", TURNS[1])
    return [x, core, chip, far]


def body(tokens, factor_d, factor_c, factor_b, factor_a, w_proj):
    local_rows = tokens.shape[0]
    f = lax.axis_index("fsdp").astype(jnp.int32).reshape(1)

    raw = lambda factor: factor.transpose(1, 2, 0).reshape(SQUARE, LANES)

    own = (raw(factor_d), raw(factor_c))
    chip = [lax.ppermute(x, "fsdp", TURNS[2]) for x in own]
    core = [lax.ppermute(x, "fsdp", TURNS[1]) for x in own]
    second, _ = local_steps(f, tokens, *own, None)
    second, done = local_steps(f ^ 1, tokens, *core, second)
    chip = [hold(x, done) for x in chip]
    far = [lax.ppermute(x, "fsdp", TURNS[1]) for x in chip]
    second, _ = local_steps(f ^ 2, tokens, *chip, second)
    second, _ = local_steps(f ^ 3, tokens, *far, second)
    token_parts, w = split(f, tokens, w_proj, second)
    w = share(w)
    token_parts = [in_turn(swap(quad)) for quad in token_parts]
    arrived = lax.all_to_all(
        second.reshape(64 * RANKS, 64, LANES), ("ctx", "fsdp"), split_axis=0, concat_axis=0, tiled=True
    )
    early = [part for quad in token_parts[:3] for part in quad[1:]]
    third, first_sent = middle(
        arrived.reshape(BLK, 2, RANKS, 64, LANES), raw(factor_b), raw(factor_a), RETURN_QUADS[0], early + w[1:]
    )

    out, first_quad, after = None, 0, []
    for k, count in enumerate(RETURN_QUADS):
        sent = step_a(third, raw(factor_a), first_quad, count, token_parts[3][1:]) if k else first_sent
        mixed = lax.all_to_all(
            sent.reshape(64, count * 16, ALL), "ctx", split_axis=0, concat_axis=0, tiled=True
        ).reshape(64, count, 16, ALL)
        parts = []
        size = 1 if k == len(RETURN_QUADS) - 1 else count
        for slot in range(0, count, size):
            tokens_here = token_parts[first_quad + slot : first_quad + slot + size]
            parts += [in_turn(swap(part)) for part in project(f, mixed, tokens_here, w, slot, size, after)]
        ends = []
        for part in parts:
            out, done = merge(f, part, local_rows, first_quad, out)
            first_quad += 1
            ends.append(done)
        after = ends[:1]
    return out


def solution(mesh):
    in_specs = (
        P("ctx", "fsdp"),
        P(("ctx", "fsdp"), None, None),
        P(("ctx", "fsdp"), None, None),
        P(("ctx", "fsdp"), None, None),
        P(("ctx", "fsdp"), None, None),
        P(None, "fsdp"),
    )
    out_specs = P("ctx", "fsdp")
    return jax.shard_map(body, mesh=mesh, in_specs=in_specs, out_specs=out_specs, check_vma=False)
```

```python
import functools

import jax
import jax.numpy as jnp
from jax import lax
from jax.experimental import pallas as pl
from jax.experimental.pallas import tpu as pltpu
from jax.sharding import PartitionSpec as P

BLK = 32
LANES = 128
SUB = 8
WIDE = SUB * BLK
PACK = LANES // BLK
SQUARE = BLK * BLK
RANKS = 4
ALL = RANKS * LANES
BF16 = jnp.bfloat16
F32 = jnp.float32
MIB = 1024 * 1024
LARGE, MEDIUM, SMALL = 60 * MIB, 53 * MIB, 24 * MIB
RETURN_QUADS = (2, 2)

VMEM = pl.BlockSpec(memory_space=pltpu.VMEM)
SMEM = pl.BlockSpec(memory_space=pltpu.SMEM)
ANY = pl.BlockSpec(memory_space=pl.ANY)
FACTOR = pltpu.VMEM((LANES, SQUARE), BF16)
DONE = jax.ShapeDtypeStruct((SUB, LANES), F32)
RAW = pltpu.VMEM((SQUARE, LANES), BF16)
WIDE_SHAPE = pltpu.VMEM((4, SUB, BLK, WIDE), BF16)
SPREAD_SHAPE = pltpu.VMEM((PACK, LANES, WIDE), BF16)


def call(kernel, name, out_shape, in_specs, out_specs, scratch, flops, moved, exps=0, aliases=None, grant=LARGE):
    return pl.pallas_call(
        kernel,
        name=name,
        out_shape=out_shape,
        in_specs=in_specs,
        out_specs=out_specs,
        scratch_shapes=scratch,
        input_output_aliases=aliases or {},
        compiler_params=pltpu.CompilerParams(vmem_limit_bytes=grant),
        cost_estimate=pl.CostEstimate(flops=flops, bytes_accessed=moved, transcendentals=exps),
    )


def aligned(start, size):
    return pl.ds(pl.multiple_of(start, size), size)


def started(copies):
    for copy in copies:
        copy.start()
    return copies


def finish(copies):
    for copy in copies:
        copy.wait()


def iota(shape, axis):
    return lax.broadcasted_iota(jnp.int32, shape, axis)


def ones_where(condition):
    return jnp.where(condition, 1.0, 0.0).astype(BF16)


def take(raw, factor_ref, source_of):
    shape = (LANES, LANES)
    order = ones_where(source_of(iota(shape, 0)) == iota(shape, 1))
    factor = lax.dot_general(order, raw, (((1,), (1,)), ((), ())), preferred_element_type=F32)
    factor_ref[...] = factor.astype(BF16)


def widen_major(factor, wide_ref):
    rows = factor.astype(F32)
    block, row = iota((BLK, LANES), 1) // BLK, iota((BLK, LANES), 0) % SUB
    keeps = (block == row, block == row - PACK)
    for m in range(SUB):
        turned = rows[:, m * LANES : (m + 1) * LANES]
        rolled = [pltpu.roll(turned, turn * BLK, 1) for turn in range(1, PACK)]
        for turn in range(1, PACK):
            turned = jnp.where(row % PACK == turn, rolled[turn - 1], turned)
        for half in range(PACK // 2):
            parts = []
            for q in (2 * half, 2 * half + 1):
                here = turned if q == 0 else pltpu.roll(turned, LANES - q * BLK, 1)
                both = jnp.concatenate([jnp.where(keep, here, 0.0) for keep in keeps], axis=1)
                parts.append(both.reshape(4, SUB, WIDE))
            wide_ref[:, m, half * 16 : half * 16 + 16, :] = jnp.concatenate(parts, axis=1).astype(BF16)


def fill_spread(spread_ref):
    row, want = iota((LANES, WIDE), 0), iota((LANES, WIDE), 1) // 4 % BLK
    for q in range(PACK):
        spread_ref[q] = ones_where(row == want + q * BLK)


def widen_minor(factor, spread_ref, wide_ref):
    rows = factor.astype(F32).reshape(4, SUB, SQUARE)
    tiles = [rows[:, :, m * LANES : (m + 1) * LANES] for m in range(SUB)]
    left = jnp.stack(tiles, axis=1).reshape(WIDE, LANES).astype(BF16)
    shape = (1, SUB, WIDE)
    keep = iota(shape, 1) == iota(shape, 2) // LANES * 4 + iota(shape, 2) % 4
    for half in range(PACK // 2):
        parts = []
        for q in (2 * half, 2 * half + 1):
            part = jnp.dot(left, spread_ref[q], preferred_element_type=F32)
            parts.append(jnp.where(keep, part.reshape(BLK, SUB, WIDE), 0.0))
        both = jnp.concatenate(parts, axis=1).astype(BF16)
        wide_ref[:, :, half * 16 : half * 16 + 16, :] = both.reshape(4, SUB, 16, WIDE)


def apply(wide_ref, group, data):
    left = wide_ref[group].reshape(WIDE, WIDE)
    return jnp.dot(left, data, preferred_element_type=F32).reshape(BLK, SUB, data.shape[1])


def local_kernel(fetch, where_ref, tokens_ref, fd_ref, fc_ref, *rest):
    out_ref, done_ref, tokens_v, fd_v, fc_v, wide_ref, first_ref, out_v, sem, out_sem = rest[-10 - 2 * fetch :][:10]
    fetched = []
    if fetch:
        fetched = started(
            [pltpu.make_async_copy(ref, rest[n - 2], sem.at[4 + n]) for n, ref in enumerate((fd_ref, fc_ref))]
        )
        fd_ref, fc_ref = rest[-2:]
    done_ref[...] = jnp.zeros_like(done_ref)
    quarter = where_ref[0]
    arriving = started(
        [
            pltpu.make_async_copy(tokens_ref.at[aligned((quarter * 4 + p) * SQUARE, SQUARE), :], tokens_v.at[p], sem.at[p])
            for p in range(4)
        ]
    )
    finish(fetched)
    take(fd_ref[...], fd_v, lambda r: r)
    take(fc_ref[...], fc_v, lambda r: r // 4 % 4 * BLK + r // 16 * 4 + r % 4)
    for p in range(4):
        widen_major(fd_v[p * BLK : (p + 1) * BLK, :], wide_ref)
        arriving[p].wait()
        for pair in range(2):
            halves = [
                apply(wide_ref, group, tokens_v[p, group * WIDE : (group + 1) * WIDE, :])
                for group in (2 * pair, 2 * pair + 1)
            ]
            first_ref[p, :, pair * 16 : pair * 16 + 16, :] = jnp.concatenate(halves, axis=1).astype(BF16)
    leaving = []
    for step in range(4):
        widen_major(fc_v[step * BLK : (step + 1) * BLK, :], wide_ref)
        for one in range(2):
            quad = 2 * step + one
            halves = []
            for pair in range(2):
                held = first_ref[2 * pair : 2 * pair + 2, 4 * quad : 4 * quad + 4]
                halves.append(apply(wide_ref, 2 * one + pair, held.reshape(WIDE, LANES)))
            out_v[quad] = jnp.concatenate(halves, axis=1).astype(BF16)
            target = out_ref.at[:, quad // 4, quad % 4, quarter]
            leaving += started([pltpu.make_async_copy(out_v.at[quad], target, out_sem.at[quad])])
    finish(leaving)


def local_steps(where, tokens, factor_d, factor_c, base):
    extra = [] if base is None else [base]
    fetch = base is None
    place = ANY if fetch else VMEM
    return call(
        functools.partial(local_kernel, fetch),
        "steps_d_c",
        (jax.ShapeDtypeStruct((BLK, 2, RANKS, RANKS, 16, LANES), BF16), DONE),
        [SMEM, ANY, place, place] + [ANY] * len(extra),
        (ANY, VMEM),
        [
            pltpu.VMEM((4, SQUARE, LANES), BF16),
            FACTOR,
            FACTOR,
            WIDE_SHAPE,
            pltpu.VMEM((4, BLK, BLK, LANES), BF16),
            pltpu.VMEM((SUB, BLK, 16, LANES), BF16),
            pltpu.SemaphoreType.DMA((6,)),
            pltpu.SemaphoreType.DMA((SUB,)),
        ]
        + [RAW, RAW] * fetch,
        flops=2**31,
        moved=3 * 2**20,
        aliases={4: 0} if extra else None,
        grant=LARGE if fetch else MEDIUM,
    )(where, tokens, factor_d, factor_c, *extra)


def d_lo_minor(row):
    return row % 4 * BLK + row // 4


def quad_rows(factor_ref, quad):
    rows = [factor_ref[high * 64 + quad * 16 : high * 64 + quad * 16 + 16, :] for high in range(2)]
    return jnp.concatenate(rows, axis=0)


def step_a_quad(slot, factor, third_ref, row_of, spread_ref, wide_ref, sent_v):
    widen_minor(factor, spread_ref, wide_ref)
    for high in range(2):
        halves = []
        for pair in range(2):
            first = row_of(high) + 2 * pair
            data = third_ref[first : first + 2].reshape(WIDE, ALL)
            halves.append(apply(wide_ref, 2 * high + pair, data))
        sent_v[slot, :, high] = jnp.concatenate(halves, axis=1).astype(BF16)


def middle_kernel(count, held_ref, fb_ref, fa_ref, *rest):
    third_ref, sent_ref, held_v, fb_raw, fa_raw, fb_v, fa_v = rest[-14:-7]
    wide_b, wide_a, spread_ref, third_v, sent_v, sem, out_sem = rest[-7:]
    factors = started(
        [pltpu.make_async_copy(fb_ref, fb_raw, sem.at[4]), pltpu.make_async_copy(fa_ref, fa_raw, sem.at[5])]
    )
    arriving = started(
        [
            pltpu.make_async_copy(held_ref.at[pl.ds(8 * step, 8)], held_v.at[pl.ds(8 * step, 8)], sem.at[step])
            for step in range(4)
        ]
    )
    fill_spread(spread_ref)
    finish(factors)
    take(fb_raw[...], fb_v, d_lo_minor)
    take(fa_raw[...], fa_v, d_lo_minor)
    leaving = []
    later = 16 - 4 * count
    for step in range(4):
        widen_minor(fb_v[step * BLK : (step + 1) * BLK, :], spread_ref, wide_b.at[step])
        arriving[step].wait()
        for quad in range(2):
            halves = []
            for pair in range(2):
                a = 8 * step + 4 * quad + 2 * pair
                data = [held_v[a : a + 2, :, rank].reshape(WIDE, LANES) for rank in range(RANKS)]
                halves.append(apply(wide_b.at[step], 2 * quad + pair, jnp.concatenate(data, axis=1)))
            first = step * BLK + quad * 16
            third_v[:, first : first + 16, :] = jnp.concatenate(halves, axis=1).astype(BF16)
        for high in range(2):
            block = (pl.ds(high * 16 + 4 * count, later), pl.ds(step * BLK, BLK))
            leaving += started(
                [pltpu.make_async_copy(third_v.at[block], third_ref.at[block], out_sem.at[step, high])]
            )
    for quad in range(count):
        row_of = lambda high: high * 16 + quad * 4
        step_a_quad(quad, quad_rows(fa_v, quad), third_v, row_of, spread_ref, wide_a.at[quad], sent_v)
        leaving += started([pltpu.make_async_copy(sent_v.at[quad], sent_ref.at[:, :, quad], out_sem.at[4, quad])])
    finish(leaving)


def sent_shape(count):
    return jax.ShapeDtypeStruct((BLK, 2, count, 16, ALL), BF16)


def middle(held, factor_b, factor_a, count, after):
    return call(
        functools.partial(middle_kernel, count),
        "steps_b_a",
        (jax.ShapeDtypeStruct((BLK, LANES, ALL), BF16), sent_shape(count)),
        [ANY] * (3 + len(after)),
        (ANY, ANY),
        [
            pltpu.VMEM(held.shape, BF16),
            RAW,
            RAW,
            FACTOR,
            FACTOR,
            pltpu.VMEM((4, 4, SUB, BLK, WIDE), BF16),
            pltpu.VMEM((count, 4, SUB, BLK, WIDE), BF16),
            SPREAD_SHAPE,
            pltpu.VMEM((BLK, LANES, ALL), BF16),
            pltpu.VMEM((count, BLK, 2, 16, ALL), BF16),
            pltpu.SemaphoreType.DMA((6,)),
            pltpu.SemaphoreType.DMA((5, max(2, count))),
        ],
        flops=2**32,
        moved=9 * 2**20,
    )(held, factor_b, factor_a, *after)


def step_a_kernel(first_quad, count, third_ref, fa_ref, *rest):
    sent_ref, third_v, fa_raw, fa_v, wide_ref, spread_ref, sent_v, sem, out_sem = rest[-9:]
    arriving = started(
        [pltpu.make_async_copy(fa_ref, fa_raw, sem.at[2])]
        + [
            pltpu.make_async_copy(
                third_ref.at[pl.ds(high * 16 + 4 * first_quad, 4 * count)],
                third_v.at[pl.ds(high * 4 * count, 4 * count)],
                sem.at[high],
            )
            for high in range(2)
        ]
    )
    fill_spread(spread_ref)
    finish(arriving)
    take(fa_raw[...], fa_v, d_lo_minor)
    leaving = []
    for slot in range(count):
        row_of = lambda high: (high * count + slot) * 4
        step_a_quad(slot, quad_rows(fa_v, first_quad + slot), third_v, row_of, spread_ref, wide_ref, sent_v)
        leaving += started([pltpu.make_async_copy(sent_v.at[slot], sent_ref.at[:, :, slot], out_sem.at[slot])])
    finish(leaving)


def step_a(third, factor_a, first_quad, count, after):
    return call(
        functools.partial(step_a_kernel, first_quad, count),
        "step_a",
        sent_shape(count),
        [ANY] * (2 + len(after)),
        ANY,
        [
            pltpu.VMEM((8 * count, LANES, ALL), BF16),
            RAW,
            FACTOR,
            WIDE_SHAPE,
            SPREAD_SHAPE,
            pltpu.VMEM((count, BLK, 2, 16, ALL), BF16),
            pltpu.SemaphoreType.DMA((3,)),
            pltpu.SemaphoreType.DMA((count,)),
        ],
        flops=2**29 * count,
        moved=2**21 * count,
        grant=SMALL,
    )(third, factor_a, *after)


def place_of(row, f):
    turn, s, p, low = row // 64, row // 16 % 4, row // 4 % 4, row % 4
    return p * 64 + s * 16 + (turn ^ f) * 4 + low


def split_kernel(f_ref, tokens_ref, w_ref, after_ref, *rest):
    out_refs, w_out_ref = rest[: 4 * RANKS], rest[4 * RANKS]
    order_ref, tokens_v, out_v, sem, out_sem = rest[4 * RANKS + 1 :]
    leaving = started([pltpu.make_async_copy(w_ref, w_out_ref, sem.at[4])])
    size = 4 * SQUARE
    arriving = started(
        [
            pltpu.make_async_copy(tokens_ref.at[pl.ds(quad * size, size), :], tokens_v.at[quad], sem.at[quad])
            for quad in range(4)
        ]
    )
    order_ref[...] = ones_where(place_of(iota((WIDE, WIDE), 0), f_ref[0]) == iota((WIDE, WIDE), 1))
    for quad in range(4):
        arriving[quad].wait()

        for step in range(4):
            blocks = []
            for one in range(4):
                start = step * 256 + one * 64
                rows = [tokens_v[quad, p * SQUARE + start : p * SQUARE + start + 64, :] for p in range(4)]
                blocks.append(jnp.concatenate(rows, axis=0))
            held = jnp.concatenate(blocks, axis=1)
            moved = jnp.dot(order_ref[...], held, preferred_element_type=F32).astype(BF16)
            for turn in range(RANKS):
                for one in range(4):
                    block = moved[turn * 64 : turn * 64 + 64, one * LANES : (one + 1) * LANES]
                    start = step * 256 + one * 64
                    out_v[turn, quad, start : start + 64, :] = block

        leaving += started(
            [
                pltpu.make_async_copy(out_v.at[turn, quad], out_refs[quad * RANKS + turn], out_sem.at[turn, quad])
                for turn in range(RANKS)
            ]
        )
    finish(leaving)


def split(f, tokens, w, after):
    *parts, w = call(
        split_kernel,
        "split",
        [jax.ShapeDtypeStruct((SQUARE, LANES), BF16)] * (4 * RANKS) + [jax.ShapeDtypeStruct(w.shape, BF16)],
        [SMEM, ANY, ANY, ANY],
        [ANY] * (4 * RANKS + 1),
        [
            pltpu.VMEM((WIDE, WIDE), BF16),
            pltpu.VMEM((4, 4 * SQUARE, LANES), BF16),
            pltpu.VMEM((RANKS, 4, SQUARE, LANES), BF16),
            pltpu.SemaphoreType.DMA((5,)),
            pltpu.SemaphoreType.DMA((RANKS, 4)),
        ],
        flops=2**30,
        moved=8 * 2**20,
    )(f, tokens, w, after)
    return [parts[RANKS * quad : RANKS * (quad + 1)] for quad in range(4)], w


def gather_kernel(count, f_ref, *rest):
    token_refs, w_refs = rest[: RANKS * count], rest[RANKS * count : RANKS * (count + 1)]
    tokens_ref, w_ref, w_v, sem = rest[-4:]
    f = f_ref[0]
    weights = started([pltpu.make_async_copy(w_refs[turn], w_v.at[turn], sem.at[turn]) for turn in range(RANKS)])
    arriving = started(
        [
            pltpu.make_async_copy(ref, tokens_ref.at[n // RANKS, n % RANKS], sem.at[RANKS + n])
            for n, ref in enumerate(token_refs)
        ]
    )
    finish(weights)
    for row in range(RANKS):
        for column in range(RANKS):
            block = w_v[column, aligned((f ^ row) * LANES, LANES), :]
            w_ref[row * LANES : (row + 1) * LANES, column * LANES : (column + 1) * LANES] = block
    finish(arriving)


def gather(f, tokens, w):
    count = len(tokens)
    return call(
        functools.partial(gather_kernel, count),
        "gather",
        (jax.ShapeDtypeStruct((count, RANKS, SQUARE, LANES), BF16), jax.ShapeDtypeStruct((ALL, ALL), BF16)),
        [SMEM] + [ANY] * (RANKS * (count + 1)),
        (VMEM, VMEM),
        [pltpu.VMEM((RANKS, ALL, LANES), BF16), pltpu.SemaphoreType.DMA((RANKS * (count + 1),))],
        flops=0,
        moved=count * 2**21 + 2**20,
        grant=SMALL,
    )(f, *sum(tokens, []), *w)


def project_kernel(f_ref, mixed_ref, tokens_ref, w_ref, *rest):
    count = mixed_ref.shape[1]
    out_refs = rest[-RANKS * count :]
    f = f_ref[0]
    tile = SQUARE // 2
    for quad in range(count):
        for half in range(2):
            rows, blocks = slice(half * tile, (half + 1) * tile), slice(half * 32, (half + 1) * 32)
            gated = []
            for turn in range(RANKS):
                mixed = mixed_ref[blocks, quad, :, aligned((f ^ turn) * LANES, LANES)].reshape(tile, LANES)
                value = tokens_ref[quad, turn, rows, :].astype(F32)
                gated.append((mixed.astype(F32) * (value / (1.0 + jnp.exp(-value)))).astype(BF16))
            result = jnp.dot(jnp.concatenate(gated, axis=1), w_ref[...], preferred_element_type=F32).astype(BF16)
            for turn in range(RANKS):
                out_refs[RANKS * quad + turn][rows, :] = result[:, turn * LANES : (turn + 1) * LANES]


def project(f, mixed, tokens, w, after):
    count = mixed.shape[1]
    size = count * SQUARE * ALL
    parts = call(
        project_kernel,
        "project",
        [jax.ShapeDtypeStruct((SQUARE, LANES), BF16)] * (RANKS * count),
        [SMEM] + [VMEM] * 3 + [ANY] * len(after),
        [VMEM] * (RANKS * count),
        [],
        flops=size * 1024,
        moved=size * 6,
        exps=size,
        grant=SMALL,
    )(f, mixed, tokens, w, *after)
    return [parts[RANKS * quad : RANKS * (quad + 1)] for quad in range(count)]


def merge_kernel(first_row, f_ref, *rest):
    part_refs, (out_ref, done_ref, order_ref, held_v, out_sem) = rest[:RANKS], rest[-5:]
    count = part_refs[0].shape[0] // SQUARE
    done_ref[...] = jnp.zeros_like(done_ref)
    order_ref[...] = ones_where(place_of(iota((WIDE, WIDE), 1), f_ref[0]) == iota((WIDE, WIDE), 0))
    leaving = []
    for quad in range(count):
        for step in range(4):
            blocks = []
            for one in range(4):
                start = quad * SQUARE + step * 256 + one * 64
                rows = [ref[start : start + 64, :] for ref in part_refs]
                blocks.append(jnp.concatenate(rows, axis=0))
            held = jnp.concatenate(blocks, axis=1)
            moved = jnp.dot(order_ref[...], held, preferred_element_type=F32).astype(BF16)
            for p in range(4):
                for one in range(4):
                    block = moved[p * 64 : p * 64 + 64, one * LANES : (one + 1) * LANES]
                    start = p * SQUARE + step * 256 + one * 64
                    held_v[quad, start : start + 64, :] = block
                rows = pl.ds(p * SQUARE + step * 256, 256)
                target = out_ref.at[pl.ds(first_row + (quad * 4 + p) * SQUARE + step * 256, 256), :]
                leaving += started(
                    [pltpu.make_async_copy(held_v.at[quad, rows, :], target, out_sem.at[quad, step * 4 + p])]
                )
    finish(leaving)


def merge(f, parts, total, first_quad, base, after):
    rows = parts[0].shape[0]
    count = rows // SQUARE
    extra = [] if base is None else [base]
    return call(
        functools.partial(merge_kernel, first_quad * 4 * SQUARE),
        "merge",
        (jax.ShapeDtypeStruct((total, LANES), BF16), DONE),
        [SMEM] + [VMEM] * RANKS + [ANY] * (len(extra) + len(after)),
        (ANY, VMEM),
        [
            pltpu.VMEM((WIDE, WIDE), BF16),
            pltpu.VMEM((count, 4 * SQUARE, LANES), BF16),
            pltpu.SemaphoreType.DMA((count, 16)),
        ],
        flops=rows * 4 * WIDE * LANES * 2,
        moved=rows * LANES * 16,
        aliases={5: 0} if extra else None,
        grant=SMALL,
    )(f, *parts, *extra, *after)


TURNS = [[(rank, rank ^ turn) for rank in range(RANKS)] for turn in range(RANKS)]


def swap(parts):
    return [parts[0]] + [lax.ppermute(parts[turn], "fsdp", TURNS[turn]) for turn in (2, 1, 3)]


def in_turn(got):
    return [got[0], got[2], got[1], got[3]]


def hold_kernel(x_ref, after_ref, out_ref):
    pass


def hold(x, after):
    return call(
        hold_kernel,
        "hold",
        jax.ShapeDtypeStruct(x.shape, x.dtype),
        [ANY, ANY],
        ANY,
        [],
        flops=0,
        moved=0,
        aliases={0: 0},
        grant=SMALL,
    )(x, after)


def share(x):
    chip = lax.ppermute(x, "fsdp", TURNS[2])
    core = lax.ppermute(x, "fsdp", TURNS[1])
    far = lax.ppermute(chip, "fsdp", TURNS[1])
    return [x, core, chip, far]


def body(tokens, factor_d, factor_c, factor_b, factor_a, w_proj):
    local_rows = tokens.shape[0]
    f = lax.axis_index("fsdp").astype(jnp.int32).reshape(1)

    raw = lambda factor: factor.transpose(1, 2, 0).reshape(SQUARE, LANES)

    own = (raw(factor_d), raw(factor_c))
    core = [lax.ppermute(x, "fsdp", TURNS[1]) for x in own]
    chip = [lax.ppermute(x, "fsdp", TURNS[2]) for x in own]
    second, _ = local_steps(f, tokens, *own, None)
    second, done = local_steps(f ^ 1, tokens, *core, second)
    chip = [hold(x, done) for x in chip]
    far = [lax.ppermute(x, "fsdp", TURNS[1]) for x in chip]
    second, _ = local_steps(f ^ 2, tokens, *chip, second)
    second, _ = local_steps(f ^ 3, tokens, *far, second)
    token_parts, w = split(f, tokens, w_proj, second)
    w = share(w)
    token_parts = [in_turn(swap(quad)) for quad in token_parts]
    arrived = lax.all_to_all(
        second.reshape(64 * RANKS, 64, LANES), ("ctx", "fsdp"), split_axis=0, concat_axis=0, tiled=True
    )
    early = [part for quad in token_parts[:3] for part in quad[1:]]
    third, first_sent = middle(
        arrived.reshape(BLK, 2, RANKS, 64, LANES), raw(factor_b), raw(factor_a), RETURN_QUADS[0], early + w[1:]
    )

    out, first_quad, after = None, 0, []
    gathered = [gather(f, token_parts[:2], w), gather(f, token_parts[2:], w)]
    for k, count in enumerate(RETURN_QUADS):
        sent = step_a(third, raw(factor_a), first_quad, count, token_parts[3][1:] + [gathered[0][1]]) if k else first_sent
        mixed = lax.all_to_all(
            sent.reshape(64, count * 16, ALL), "ctx", split_axis=0, concat_axis=0, tiled=True
        ).reshape(64, count, 16, ALL)
        tokens_here, w_here = gathered[k]
        parts = [in_turn(swap(part)) for part in project(f, mixed, tokens_here, w_here, after)]
        ends = []
        for part in parts:
            out, done = merge(f, part, local_rows, first_quad, out, [] if first_quad else [gathered[1][1]])
            first_quad += 1
            ends.append(done)
        after = ends[:1]
    return out


def solution(mesh):
    in_specs = (
        P("ctx", "fsdp"),
        P(("ctx", "fsdp"), None, None),
        P(("ctx", "fsdp"), None, None),
        P(("ctx", "fsdp"), None, None),
        P(("ctx", "fsdp"), None, None),
        P(None, "fsdp"),
    )
    out_specs = P("ctx", "fsdp")
    return jax.shard_map(body, mesh=mesh, in_specs=in_specs, out_specs=out_specs, check_vma=False)
```

```python
import functools

import jax
import jax.numpy as jnp
from jax import lax
from jax.experimental import pallas as pl
from jax.experimental.pallas import tpu as pltpu
from jax.sharding import PartitionSpec as P

BLK = 32
LANES = 128
SUB = 8
WIDE = SUB * BLK
PACK = LANES // BLK
SQUARE = BLK * BLK
RANKS = 4
ALL = RANKS * LANES
BF16 = jnp.bfloat16
F32 = jnp.float32
MIB = 1024 * 1024
LARGE, MEDIUM, SMALL = 60 * MIB, 53 * MIB, 24 * MIB
RETURN_QUADS = (2, 2)

VMEM = pl.BlockSpec(memory_space=pltpu.VMEM)
SMEM = pl.BlockSpec(memory_space=pltpu.SMEM)
ANY = pl.BlockSpec(memory_space=pl.ANY)
FACTOR = pltpu.VMEM((LANES, SQUARE), BF16)
DONE = jax.ShapeDtypeStruct((SUB, LANES), F32)
RAW = pltpu.VMEM((SQUARE, LANES), BF16)
WIDE_SHAPE = pltpu.VMEM((4, SUB, BLK, WIDE), BF16)
SPREAD_SHAPE = pltpu.VMEM((PACK, LANES, WIDE), BF16)


def call(kernel, name, out_shape, in_specs, out_specs, scratch, flops, moved, exps=0, aliases=None, grant=LARGE):
    return pl.pallas_call(
        kernel,
        name=name,
        out_shape=out_shape,
        in_specs=in_specs,
        out_specs=out_specs,
        scratch_shapes=scratch,
        input_output_aliases=aliases or {},
        compiler_params=pltpu.CompilerParams(vmem_limit_bytes=grant),
        cost_estimate=pl.CostEstimate(flops=flops, bytes_accessed=moved, transcendentals=exps),
    )


def aligned(start, size):
    return pl.ds(pl.multiple_of(start, size), size)


def started(copies):
    for copy in copies:
        copy.start()
    return copies


def finish(copies):
    for copy in copies:
        copy.wait()


def iota(shape, axis):
    return lax.broadcasted_iota(jnp.int32, shape, axis)


def ones_where(condition):
    return jnp.where(condition, 1.0, 0.0).astype(BF16)


def take(raw, factor_ref, source_of):
    shape = (LANES, LANES)
    order = ones_where(source_of(iota(shape, 0)) == iota(shape, 1))
    factor = lax.dot_general(order, raw, (((1,), (1,)), ((), ())), preferred_element_type=F32)
    factor_ref[...] = factor.astype(BF16)


def widen_major(factor, wide_ref):
    rows = factor.astype(F32)
    block, row = iota((BLK, LANES), 1) // BLK, iota((BLK, LANES), 0) % SUB
    keeps = (block == row, block == row - PACK)
    for m in range(SUB):
        turned = rows[:, m * LANES : (m + 1) * LANES]
        rolled = [pltpu.roll(turned, turn * BLK, 1) for turn in range(1, PACK)]
        for turn in range(1, PACK):
            turned = jnp.where(row % PACK == turn, rolled[turn - 1], turned)
        for half in range(PACK // 2):
            parts = []
            for q in (2 * half, 2 * half + 1):
                here = turned if q == 0 else pltpu.roll(turned, LANES - q * BLK, 1)
                both = jnp.concatenate([jnp.where(keep, here, 0.0) for keep in keeps], axis=1)
                parts.append(both.reshape(4, SUB, WIDE))
            wide_ref[:, m, half * 16 : half * 16 + 16, :] = jnp.concatenate(parts, axis=1).astype(BF16)


def fill_spread(spread_ref):
    row, want = iota((LANES, WIDE), 0), iota((LANES, WIDE), 1) // 4 % BLK
    for q in range(PACK):
        spread_ref[q] = ones_where(row == want + q * BLK)


def widen_minor(factor, spread_ref, wide_ref):
    rows = factor.astype(F32).reshape(4, SUB, SQUARE)
    tiles = [rows[:, :, m * LANES : (m + 1) * LANES] for m in range(SUB)]
    left = jnp.stack(tiles, axis=1).reshape(WIDE, LANES).astype(BF16)
    shape = (1, SUB, WIDE)
    keep = iota(shape, 1) == iota(shape, 2) // LANES * 4 + iota(shape, 2) % 4
    for half in range(PACK // 2):
        parts = []
        for q in (2 * half, 2 * half + 1):
            part = jnp.dot(left, spread_ref[q], preferred_element_type=F32)
            parts.append(jnp.where(keep, part.reshape(BLK, SUB, WIDE), 0.0))
        both = jnp.concatenate(parts, axis=1).astype(BF16)
        wide_ref[:, :, half * 16 : half * 16 + 16, :] = both.reshape(4, SUB, 16, WIDE)


def apply(wide_ref, group, data):
    left = wide_ref[group].reshape(WIDE, WIDE)
    return jnp.dot(left, data, preferred_element_type=F32).reshape(BLK, SUB, data.shape[1])


def local_kernel(fetch, where_ref, tokens_ref, fd_ref, fc_ref, *rest):
    out_ref, done_ref, tokens_v, fd_v, fc_v, wide_ref, first_ref, out_v, sem, out_sem = rest[-10 - 2 * fetch :][:10]
    fetched = []
    if fetch:
        fetched = started(
            [pltpu.make_async_copy(ref, rest[n - 2], sem.at[4 + n]) for n, ref in enumerate((fd_ref, fc_ref))]
        )
        fd_ref, fc_ref = rest[-2:]
    done_ref[...] = jnp.zeros_like(done_ref)
    quarter = where_ref[0]
    arriving = started(
        [
            pltpu.make_async_copy(tokens_ref.at[aligned((quarter * 4 + p) * SQUARE, SQUARE), :], tokens_v.at[p], sem.at[p])
            for p in range(4)
        ]
    )
    finish(fetched)
    take(fd_ref[...], fd_v, lambda r: r)
    take(fc_ref[...], fc_v, lambda r: r // 4 % 4 * BLK + r // 16 * 4 + r % 4)
    for p in range(4):
        widen_major(fd_v[p * BLK : (p + 1) * BLK, :], wide_ref)
        arriving[p].wait()
        for pair in range(2):
            halves = [
                apply(wide_ref, group, tokens_v[p, group * WIDE : (group + 1) * WIDE, :])
                for group in (2 * pair, 2 * pair + 1)
            ]
            first_ref[p, :, pair * 16 : pair * 16 + 16, :] = jnp.concatenate(halves, axis=1).astype(BF16)
    leaving = []
    for step in range(4):
        widen_major(fc_v[step * BLK : (step + 1) * BLK, :], wide_ref)
        for one in range(2):
            quad = 2 * step + one
            halves = []
            for pair in range(2):
                held = first_ref[2 * pair : 2 * pair + 2, 4 * quad : 4 * quad + 4]
                halves.append(apply(wide_ref, 2 * one + pair, held.reshape(WIDE, LANES)))
            out_v[quad] = jnp.concatenate(halves, axis=1).astype(BF16)
            target = out_ref.at[:, quad // 4, quad % 4, quarter]
            leaving += started([pltpu.make_async_copy(out_v.at[quad], target, out_sem.at[quad])])
    finish(leaving)


def local_steps(where, tokens, factor_d, factor_c, base):
    extra = [] if base is None else [base]
    fetch = base is None
    place = ANY if fetch else VMEM
    return call(
        functools.partial(local_kernel, fetch),
        "steps_d_c",
        (jax.ShapeDtypeStruct((BLK, 2, RANKS, RANKS, 16, LANES), BF16), DONE),
        [SMEM, ANY, place, place] + [ANY] * len(extra),
        (ANY, VMEM),
        [
            pltpu.VMEM((4, SQUARE, LANES), BF16),
            FACTOR,
            FACTOR,
            WIDE_SHAPE,
            pltpu.VMEM((4, BLK, BLK, LANES), BF16),
            pltpu.VMEM((SUB, BLK, 16, LANES), BF16),
            pltpu.SemaphoreType.DMA((6,)),
            pltpu.SemaphoreType.DMA((SUB,)),
        ]
        + [RAW, RAW] * fetch,
        flops=2**31,
        moved=3 * 2**20,
        aliases={4: 0} if extra else None,
        grant=LARGE if fetch else MEDIUM,
    )(where, tokens, factor_d, factor_c, *extra)


def d_lo_minor(row):
    return row % 4 * BLK + row // 4


def quad_rows(factor_ref, quad):
    rows = [factor_ref[high * 64 + quad * 16 : high * 64 + quad * 16 + 16, :] for high in range(2)]
    return jnp.concatenate(rows, axis=0)


READY = jax.ShapeDtypeStruct((4, 4, SUB, BLK, WIDE), BF16)


def weights_kernel(fb_ref, fa_ref, after_ref, out_ref, fb_raw, fa_raw, factor_ref, spread_ref, wide_v, sem, out_sem):
    arriving = started(
        [
            pltpu.make_async_copy(ref, raw, sem.at[n])
            for n, (ref, raw) in enumerate(((fb_ref, fb_raw), (fa_ref, fa_raw)))
        ]
    )
    fill_spread(spread_ref)
    leaving = []
    for n, raw in enumerate((fb_raw, fa_raw)):
        arriving[n].wait()
        take(raw[...], factor_ref, d_lo_minor)
        for step in range(2):
            slot = 2 * n + step
            rows = quad_rows(factor_ref, step) if n else factor_ref[(2 + step) * BLK : (3 + step) * BLK, :]
            widen_minor(rows, spread_ref, wide_v.at[slot])
            leaving += started([pltpu.make_async_copy(wide_v.at[slot], out_ref.at[slot], out_sem.at[slot])])
    finish(leaving)


def weights(factor_b, factor_a, after):
    return call(
        weights_kernel,
        "weights",
        READY,
        [ANY, ANY, ANY],
        ANY,
        [
            RAW,
            RAW,
            FACTOR,
            SPREAD_SHAPE,
            pltpu.VMEM(READY.shape, BF16),
            pltpu.SemaphoreType.DMA((2,)),
            pltpu.SemaphoreType.DMA((4,)),
        ],
        flops=2**30,
        moved=3 * 2**20,
    )(factor_b, factor_a, after)


def step_a_quad(slot, factor, third_ref, row_of, spread_ref, wide_ref, sent_v):
    if factor is not None:
        widen_minor(factor, spread_ref, wide_ref)
    for high in range(2):
        halves = []
        for pair in range(2):
            first = row_of(high) + 2 * pair
            data = third_ref[first : first + 2].reshape(WIDE, ALL)
            halves.append(apply(wide_ref, 2 * high + pair, data))
        sent_v[slot, :, high] = jnp.concatenate(halves, axis=1).astype(BF16)


def middle_kernel(count, held_ref, fb_ref, ready_ref, *rest):
    third_ref, sent_ref, held_v, fb_raw, fb_v, wide_b, wide_a = rest[-12:-5]
    spread_ref, third_v, sent_v, sem, out_sem = rest[-5:]
    factor = started([pltpu.make_async_copy(fb_ref, fb_raw, sem.at[4])])
    rows = [pl.ds(8 * step, 8) for step in range(4)]
    arriving = [pltpu.make_async_copy(held_ref.at[rows[n]], held_v.at[rows[n]], sem.at[n]) for n in range(4)]
    ready_b = pltpu.make_async_copy(ready_ref.at[pl.ds(0, 2)], wide_b.at[pl.ds(2, 2)], sem.at[5])
    ready_a = pltpu.make_async_copy(ready_ref.at[pl.ds(2, 2)], wide_a, sem.at[6])
    started(arriving[:2] + [ready_b] + arriving[2:] + [ready_a])
    fill_spread(spread_ref)
    finish(factor)
    take(fb_raw[...], fb_v, d_lo_minor)
    leaving = []
    later = 16 - 4 * count
    for step in range(4):
        if step < 2:
            widen_minor(fb_v[step * BLK : (step + 1) * BLK, :], spread_ref, wide_b.at[step])
        elif step == 2:
            ready_b.wait()
        arriving[step].wait()
        for quad in range(2):
            halves = []
            for pair in range(2):
                a = 8 * step + 4 * quad + 2 * pair
                data = [held_v[a : a + 2, :, rank].reshape(WIDE, LANES) for rank in range(RANKS)]
                halves.append(apply(wide_b.at[step], 2 * quad + pair, jnp.concatenate(data, axis=1)))
            first = step * BLK + quad * 16
            third_v[:, first : first + 16, :] = jnp.concatenate(halves, axis=1).astype(BF16)
        for high in range(2):
            block = (pl.ds(high * 16 + 4 * count, later), pl.ds(step * BLK, BLK))
            leaving += started(
                [pltpu.make_async_copy(third_v.at[block], third_ref.at[block], out_sem.at[step, high])]
            )
    ready_a.wait()
    for quad in range(count):
        row_of = lambda high: high * 16 + quad * 4
        step_a_quad(quad, None, third_v, row_of, None, wide_a.at[quad], sent_v)
        leaving += started([pltpu.make_async_copy(sent_v.at[quad], sent_ref.at[:, :, quad], out_sem.at[4, quad])])
    finish(leaving)


def sent_shape(count):
    return jax.ShapeDtypeStruct((BLK, 2, count, 16, ALL), BF16)


def middle(held, factor_b, ready, count, after):
    return call(
        functools.partial(middle_kernel, count),
        "steps_b_a",
        (jax.ShapeDtypeStruct((BLK, LANES, ALL), BF16), sent_shape(count)),
        [ANY] * (3 + len(after)),
        (ANY, ANY),
        [
            pltpu.VMEM(held.shape, BF16),
            RAW,
            FACTOR,
            pltpu.VMEM((4, 4, SUB, BLK, WIDE), BF16),
            pltpu.VMEM((count, 4, SUB, BLK, WIDE), BF16),
            SPREAD_SHAPE,
            pltpu.VMEM((BLK, LANES, ALL), BF16),
            pltpu.VMEM((count, BLK, 2, 16, ALL), BF16),
            pltpu.SemaphoreType.DMA((7,)),
            pltpu.SemaphoreType.DMA((5, max(2, count))),
        ],
        flops=2**32,
        moved=9 * 2**20,
    )(held, factor_b, ready, *after)


def step_a_kernel(first_quad, count, third_ref, fa_ref, *rest):
    sent_ref, third_v, fa_raw, fa_v, wide_ref, spread_ref, sent_v, sem, out_sem = rest[-9:]
    arriving = started(
        [pltpu.make_async_copy(fa_ref, fa_raw, sem.at[2])]
        + [
            pltpu.make_async_copy(
                third_ref.at[pl.ds(high * 16 + 4 * first_quad, 4 * count)],
                third_v.at[pl.ds(high * 4 * count, 4 * count)],
                sem.at[high],
            )
            for high in range(2)
        ]
    )
    fill_spread(spread_ref)
    finish(arriving)
    take(fa_raw[...], fa_v, d_lo_minor)
    leaving = []
    for slot in range(count):
        row_of = lambda high: (high * count + slot) * 4
        step_a_quad(slot, quad_rows(fa_v, first_quad + slot), third_v, row_of, spread_ref, wide_ref, sent_v)
        leaving += started([pltpu.make_async_copy(sent_v.at[slot], sent_ref.at[:, :, slot], out_sem.at[slot])])
    finish(leaving)


def step_a(third, factor_a, first_quad, count, after):
    return call(
        functools.partial(step_a_kernel, first_quad, count),
        "step_a",
        sent_shape(count),
        [ANY] * (2 + len(after)),
        ANY,
        [
            pltpu.VMEM((8 * count, LANES, ALL), BF16),
            RAW,
            FACTOR,
            WIDE_SHAPE,
            SPREAD_SHAPE,
            pltpu.VMEM((count, BLK, 2, 16, ALL), BF16),
            pltpu.SemaphoreType.DMA((3,)),
            pltpu.SemaphoreType.DMA((count,)),
        ],
        flops=2**29 * count,
        moved=2**21 * count,
        grant=SMALL,
    )(third, factor_a, *after)


def place_of(row, f):
    turn, s, p, low = row // 64, row // 16 % 4, row // 4 % 4, row % 4
    return p * 64 + s * 16 + (turn ^ f) * 4 + low


def split_kernel(f_ref, tokens_ref, w_ref, after_ref, *rest):
    out_refs, w_out_ref = rest[: 4 * RANKS], rest[4 * RANKS]
    order_ref, tokens_v, out_v, sem, out_sem = rest[4 * RANKS + 1 :]
    leaving = started([pltpu.make_async_copy(w_ref, w_out_ref, sem.at[4])])
    size = 4 * SQUARE
    arriving = started(
        [
            pltpu.make_async_copy(tokens_ref.at[pl.ds(quad * size, size), :], tokens_v.at[quad], sem.at[quad])
            for quad in range(4)
        ]
    )
    order_ref[...] = ones_where(place_of(iota((WIDE, WIDE), 0), f_ref[0]) == iota((WIDE, WIDE), 1))
    for quad in range(4):
        arriving[quad].wait()

        for step in range(4):
            blocks = []
            for one in range(4):
                start = step * 256 + one * 64
                rows = [tokens_v[quad, p * SQUARE + start : p * SQUARE + start + 64, :] for p in range(4)]
                blocks.append(jnp.concatenate(rows, axis=0))
            held = jnp.concatenate(blocks, axis=1)
            moved = jnp.dot(order_ref[...], held, preferred_element_type=F32).astype(BF16)
            for turn in range(RANKS):
                for one in range(4):
                    block = moved[turn * 64 : turn * 64 + 64, one * LANES : (one + 1) * LANES]
                    start = step * 256 + one * 64
                    out_v[turn, quad, start : start + 64, :] = block

        leaving += started(
            [
                pltpu.make_async_copy(out_v.at[turn, quad], out_refs[quad * RANKS + turn], out_sem.at[turn, quad])
                for turn in range(RANKS)
            ]
        )
    finish(leaving)


def split(f, tokens, w, after):
    *parts, w = call(
        split_kernel,
        "split",
        [jax.ShapeDtypeStruct((SQUARE, LANES), BF16)] * (4 * RANKS) + [jax.ShapeDtypeStruct(w.shape, BF16)],
        [SMEM, ANY, ANY, ANY],
        [ANY] * (4 * RANKS + 1),
        [
            pltpu.VMEM((WIDE, WIDE), BF16),
            pltpu.VMEM((4, 4 * SQUARE, LANES), BF16),
            pltpu.VMEM((RANKS, 4, SQUARE, LANES), BF16),
            pltpu.SemaphoreType.DMA((5,)),
            pltpu.SemaphoreType.DMA((RANKS, 4)),
        ],
        flops=2**30,
        moved=8 * 2**20,
    )(f, tokens, w, after)
    return [parts[RANKS * quad : RANKS * (quad + 1)] for quad in range(4)], w


def gather_kernel(count, f_ref, *rest):
    token_refs, w_refs = rest[: RANKS * count], rest[RANKS * count : RANKS * (count + 1)]
    tokens_ref, w_ref, w_v, sem = rest[-4:]
    f = f_ref[0]
    weights = started([pltpu.make_async_copy(w_refs[turn], w_v.at[turn], sem.at[turn]) for turn in range(RANKS)])
    arriving = started(
        [
            pltpu.make_async_copy(ref, tokens_ref.at[n // RANKS, n % RANKS], sem.at[RANKS + n])
            for n, ref in enumerate(token_refs)
        ]
    )
    finish(weights)
    for row in range(RANKS):
        for column in range(RANKS):
            block = w_v[column, aligned((f ^ row) * LANES, LANES), :]
            w_ref[row * LANES : (row + 1) * LANES, column * LANES : (column + 1) * LANES] = block
    finish(arriving)


def gather(f, tokens, w):
    count = len(tokens)
    return call(
        functools.partial(gather_kernel, count),
        "gather",
        (jax.ShapeDtypeStruct((count, RANKS, SQUARE, LANES), BF16), jax.ShapeDtypeStruct((ALL, ALL), BF16)),
        [SMEM] + [ANY] * (RANKS * (count + 1)),
        (VMEM, VMEM),
        [pltpu.VMEM((RANKS, ALL, LANES), BF16), pltpu.SemaphoreType.DMA((RANKS * (count + 1),))],
        flops=0,
        moved=count * 2**21 + 2**20,
        grant=SMALL,
    )(f, *sum(tokens, []), *w)


def project_kernel(first, count, f_ref, mixed_ref, tokens_ref, w_ref, *rest):
    out_refs = rest[-RANKS * count :]
    f = f_ref[0]
    tile = SQUARE // 2
    for quad in range(count):
        for half in range(2):
            rows, blocks = slice(half * tile, (half + 1) * tile), slice(half * 32, (half + 1) * 32)
            gated = []
            for turn in range(RANKS):
                mixed = mixed_ref[blocks, first + quad, :, aligned((f ^ turn) * LANES, LANES)].reshape(tile, LANES)
                value = tokens_ref[first + quad, turn, rows, :].astype(F32)
                gated.append((mixed.astype(F32) * (value / (1.0 + jnp.exp(-value)))).astype(BF16))
            result = jnp.dot(jnp.concatenate(gated, axis=1), w_ref[...], preferred_element_type=F32).astype(BF16)
            for turn in range(RANKS):
                out_refs[RANKS * quad + turn][rows, :] = result[:, turn * LANES : (turn + 1) * LANES]


def project(f, mixed, tokens, w, first, count, after):
    size = count * SQUARE * ALL
    parts = call(
        functools.partial(project_kernel, first, count),
        "project",
        [jax.ShapeDtypeStruct((SQUARE, LANES), BF16)] * (RANKS * count),
        [SMEM] + [VMEM] * 3 + [ANY] * len(after),
        [VMEM] * (RANKS * count),
        [],
        flops=size * 1024,
        moved=size * 6,
        exps=size,
        grant=SMALL,
    )(f, mixed, tokens, w, *after)
    return [parts[RANKS * quad : RANKS * (quad + 1)] for quad in range(count)]


def merge_kernel(first_row, f_ref, *rest):
    part_refs, (out_ref, done_ref, order_ref, held_v, out_sem) = rest[:RANKS], rest[-5:]
    count = part_refs[0].shape[0] // SQUARE
    done_ref[...] = jnp.zeros_like(done_ref)
    order_ref[...] = ones_where(place_of(iota((WIDE, WIDE), 1), f_ref[0]) == iota((WIDE, WIDE), 0))
    leaving = []
    for quad in range(count):
        for step in range(4):
            blocks = []
            for one in range(4):
                start = quad * SQUARE + step * 256 + one * 64
                rows = [ref[start : start + 64, :] for ref in part_refs]
                blocks.append(jnp.concatenate(rows, axis=0))
            held = jnp.concatenate(blocks, axis=1)
            moved = jnp.dot(order_ref[...], held, preferred_element_type=F32).astype(BF16)
            for p in range(4):
                for one in range(4):
                    block = moved[p * 64 : p * 64 + 64, one * LANES : (one + 1) * LANES]
                    start = p * SQUARE + step * 256 + one * 64
                    held_v[quad, start : start + 64, :] = block
                rows = pl.ds(p * SQUARE + step * 256, 256)
                target = out_ref.at[pl.ds(first_row + (quad * 4 + p) * SQUARE + step * 256, 256), :]
                leaving += started(
                    [pltpu.make_async_copy(held_v.at[quad, rows, :], target, out_sem.at[quad, step * 4 + p])]
                )
    finish(leaving)


def merge(f, parts, total, first_quad, base, after):
    rows = parts[0].shape[0]
    count = rows // SQUARE
    extra = [] if base is None else [base]
    return call(
        functools.partial(merge_kernel, first_quad * 4 * SQUARE),
        "merge",
        (jax.ShapeDtypeStruct((total, LANES), BF16), DONE),
        [SMEM] + [VMEM] * RANKS + [ANY] * (len(extra) + len(after)),
        (ANY, VMEM),
        [
            pltpu.VMEM((WIDE, WIDE), BF16),
            pltpu.VMEM((count, 4 * SQUARE, LANES), BF16),
            pltpu.SemaphoreType.DMA((count, 16)),
        ],
        flops=rows * 4 * WIDE * LANES * 2,
        moved=rows * LANES * 16,
        aliases={5: 0} if extra else None,
        grant=SMALL,
    )(f, *parts, *extra, *after)


TURNS = [[(rank, rank ^ turn) for rank in range(RANKS)] for turn in range(RANKS)]


def swap(parts):
    return [parts[0]] + [lax.ppermute(parts[turn], "fsdp", TURNS[turn]) for turn in (2, 1, 3)]


def in_turn(got):
    return [got[0], got[2], got[1], got[3]]


def hold_kernel(x_ref, after_ref, out_ref):
    pass


def hold(x, after):
    return call(
        hold_kernel,
        "hold",
        jax.ShapeDtypeStruct(x.shape, x.dtype),
        [ANY, ANY],
        ANY,
        [],
        flops=0,
        moved=0,
        aliases={0: 0},
        grant=SMALL,
    )(x, after)


def share(x):
    chip = lax.ppermute(x, "fsdp", TURNS[2])
    core = lax.ppermute(x, "fsdp", TURNS[1])
    far = lax.ppermute(chip, "fsdp", TURNS[1])
    return [x, core, chip, far]


def body(tokens, factor_d, factor_c, factor_b, factor_a, w_proj):
    local_rows = tokens.shape[0]
    f = lax.axis_index("fsdp").astype(jnp.int32).reshape(1)

    raw = lambda factor: factor.transpose(1, 2, 0).reshape(SQUARE, LANES)

    own = (raw(factor_d), raw(factor_c))
    core = [lax.ppermute(x, "fsdp", TURNS[1]) for x in own]
    chip = [lax.ppermute(x, "fsdp", TURNS[2]) for x in own]
    second, _ = local_steps(f, tokens, *own, None)
    second, done = local_steps(f ^ 1, tokens, *core, second)
    chip = [hold(x, done) for x in chip]
    far = [lax.ppermute(x, "fsdp", TURNS[1]) for x in chip]
    second, _ = local_steps(f ^ 2, tokens, *chip, second)
    second, _ = local_steps(f ^ 3, tokens, *far, second)
    token_parts, w = split(f, tokens, w_proj, second)
    w = share(w)
    token_parts = [in_turn(swap(quad)) for quad in token_parts]
    arrived = lax.all_to_all(
        second.reshape(64 * RANKS, 64, LANES), ("ctx", "fsdp"), split_axis=0, concat_axis=0, tiled=True
    )
    ready = weights(raw(factor_b), raw(factor_a), second)
    early = [part for quad in token_parts[:3] for part in quad[1:]]
    third, first_sent = middle(
        arrived.reshape(BLK, 2, RANKS, 64, LANES), raw(factor_b), ready, RETURN_QUADS[0], early + w[1:]
    )

    out, first_quad, after = None, 0, []
    gathered = [gather(f, token_parts[:2], w), gather(f, token_parts[2:], w)]
    for k, count in enumerate(RETURN_QUADS):
        sent = step_a(third, raw(factor_a), first_quad, count, token_parts[3][1:] + [gathered[0][1]]) if k else first_sent
        mixed = lax.all_to_all(
            sent.reshape(64, count * 16, ALL), "ctx", split_axis=0, concat_axis=0, tiled=True
        ).reshape(64, count, 16, ALL)
        tokens_here, w_here = gathered[k]
        parts, size = [], 1 if k else count
        for slot in range(0, count, size):
            here = project(f, mixed, tokens_here, w_here, slot, size, after)
            parts += [in_turn(swap(part)) for part in here]
        ends = []
        for part in parts:
            out, done = merge(f, part, local_rows, first_quad, out, [] if first_quad else [gathered[1][1]])
            first_quad += 1
            ends.append(done)
        after = ends[:1]
    return out


def solution(mesh):
    in_specs = (
        P("ctx", "fsdp"),
        P(("ctx", "fsdp"), None, None),
        P(("ctx", "fsdp"), None, None),
        P(("ctx", "fsdp"), None, None),
        P(("ctx", "fsdp"), None, None),
        P(None, "fsdp"),
    )
    out_specs = P("ctx", "fsdp")
    return jax.shard_map(body, mesh=mesh, in_specs=in_specs, out_specs=out_specs, check_vma=False)
```

```python
import functools

import jax
import jax.numpy as jnp
from jax import lax
from jax.experimental import pallas as pl
from jax.experimental.pallas import tpu as pltpu
from jax.sharding import PartitionSpec as P

BLK = 32
LANES = 128
SUB = 8
WIDE = SUB * BLK
PACK = LANES // BLK
SQUARE = BLK * BLK
RANKS = 4
ALL = RANKS * LANES
BF16 = jnp.bfloat16
F32 = jnp.float32
MIB = 1024 * 1024
LARGE, MEDIUM, SMALL = 60 * MIB, 53 * MIB, 24 * MIB
RETURN_QUADS = (2, 2)

VMEM = pl.BlockSpec(memory_space=pltpu.VMEM)
SMEM = pl.BlockSpec(memory_space=pltpu.SMEM)
ANY = pl.BlockSpec(memory_space=pl.ANY)
FACTOR = pltpu.VMEM((LANES, SQUARE), BF16)
DONE = jax.ShapeDtypeStruct((SUB, LANES), F32)
RAW = pltpu.VMEM((SQUARE, LANES), BF16)
WIDE_SHAPE = pltpu.VMEM((4, SUB, BLK, WIDE), BF16)
SPREAD_SHAPE = pltpu.VMEM((PACK, LANES, WIDE), BF16)


def call(kernel, name, out_shape, in_specs, out_specs, scratch, flops, moved, exps=0, aliases=None, grant=LARGE):
    return pl.pallas_call(
        kernel,
        name=name,
        out_shape=out_shape,
        in_specs=in_specs,
        out_specs=out_specs,
        scratch_shapes=scratch,
        input_output_aliases=aliases or {},
        compiler_params=pltpu.CompilerParams(vmem_limit_bytes=grant),
        cost_estimate=pl.CostEstimate(flops=flops, bytes_accessed=moved, transcendentals=exps),
    )


def aligned(start, size):
    return pl.ds(pl.multiple_of(start, size), size)


def started(copies):
    for copy in copies:
        copy.start()
    return copies


def finish(copies):
    for copy in copies:
        copy.wait()


def iota(shape, axis):
    return lax.broadcasted_iota(jnp.int32, shape, axis)


def ones_where(condition):
    return jnp.where(condition, 1.0, 0.0).astype(BF16)


def take(raw, factor_ref, source_of):
    shape = (LANES, LANES)
    order = ones_where(source_of(iota(shape, 0)) == iota(shape, 1))
    factor = lax.dot_general(order, raw, (((1,), (1,)), ((), ())), preferred_element_type=F32)
    factor_ref[...] = factor.astype(BF16)


def widen_major(factor, wide_ref):
    rows = factor.astype(F32)
    block, row = iota((BLK, LANES), 1) // BLK, iota((BLK, LANES), 0) % SUB
    keeps = (block == row, block == row - PACK)
    for m in range(SUB):
        turned = rows[:, m * LANES : (m + 1) * LANES]
        rolled = [pltpu.roll(turned, turn * BLK, 1) for turn in range(1, PACK)]
        for turn in range(1, PACK):
            turned = jnp.where(row % PACK == turn, rolled[turn - 1], turned)
        for half in range(PACK // 2):
            parts = []
            for q in (2 * half, 2 * half + 1):
                here = turned if q == 0 else pltpu.roll(turned, LANES - q * BLK, 1)
                both = jnp.concatenate([jnp.where(keep, here, 0.0) for keep in keeps], axis=1)
                parts.append(both.reshape(4, SUB, WIDE))
            wide_ref[:, m, half * 16 : half * 16 + 16, :] = jnp.concatenate(parts, axis=1).astype(BF16)


def fill_spread(spread_ref):
    row, want = iota((LANES, WIDE), 0), iota((LANES, WIDE), 1) // 4 % BLK
    for q in range(PACK):
        spread_ref[q] = ones_where(row == want + q * BLK)


def widen_minor(factor, spread_ref, wide_ref):
    rows = factor.astype(F32).reshape(4, SUB, SQUARE)
    tiles = [rows[:, :, m * LANES : (m + 1) * LANES] for m in range(SUB)]
    left = jnp.stack(tiles, axis=1).reshape(WIDE, LANES).astype(BF16)
    shape = (1, SUB, WIDE)
    keep = iota(shape, 1) == iota(shape, 2) // LANES * 4 + iota(shape, 2) % 4
    for half in range(PACK // 2):
        parts = []
        for q in (2 * half, 2 * half + 1):
            part = jnp.dot(left, spread_ref[q], preferred_element_type=F32)
            parts.append(jnp.where(keep, part.reshape(BLK, SUB, WIDE), 0.0))
        both = jnp.concatenate(parts, axis=1).astype(BF16)
        wide_ref[:, :, half * 16 : half * 16 + 16, :] = both.reshape(4, SUB, 16, WIDE)


def apply(wide_ref, group, data):
    left = wide_ref[group].reshape(WIDE, WIDE)
    return jnp.dot(left, data, preferred_element_type=F32).reshape(BLK, SUB, data.shape[1])


def local_kernel(fetch, where_ref, tokens_ref, fd_ref, fc_ref, *rest):
    out_ref, done_ref, tokens_v, fd_v, fc_v, wide_ref, first_ref, out_v, sem, out_sem = rest[-10 - 2 * fetch :][:10]
    fetched = []
    if fetch:
        fetched = started(
            [pltpu.make_async_copy(ref, rest[n - 2], sem.at[4 + n]) for n, ref in enumerate((fd_ref, fc_ref))]
        )
        fd_ref, fc_ref = rest[-2:]
    done_ref[...] = jnp.zeros_like(done_ref)
    quarter = where_ref[0]
    arriving = started(
        [
            pltpu.make_async_copy(tokens_ref.at[aligned((quarter * 4 + p) * SQUARE, SQUARE), :], tokens_v.at[p], sem.at[p])
            for p in range(4)
        ]
    )
    finish(fetched)
    take(fd_ref[...], fd_v, lambda r: r)
    take(fc_ref[...], fc_v, lambda r: r // 4 % 4 * BLK + r // 16 * 4 + r % 4)
    for p in range(4):
        widen_major(fd_v[p * BLK : (p + 1) * BLK, :], wide_ref)
        arriving[p].wait()
        for pair in range(2):
            halves = [
                apply(wide_ref, group, tokens_v[p, group * WIDE : (group + 1) * WIDE, :])
                for group in (2 * pair, 2 * pair + 1)
            ]
            first_ref[p, :, pair * 16 : pair * 16 + 16, :] = jnp.concatenate(halves, axis=1).astype(BF16)
    leaving = []
    for step in range(4):
        widen_major(fc_v[step * BLK : (step + 1) * BLK, :], wide_ref)
        for one in range(2):
            quad = 2 * step + one
            halves = []
            for pair in range(2):
                held = first_ref[2 * pair : 2 * pair + 2, 4 * quad : 4 * quad + 4]
                halves.append(apply(wide_ref, 2 * one + pair, held.reshape(WIDE, LANES)))
            out_v[quad] = jnp.concatenate(halves, axis=1).astype(BF16)
            target = out_ref.at[:, quad // 4, quad % 4, quarter]
            leaving += started([pltpu.make_async_copy(out_v.at[quad], target, out_sem.at[quad])])
    finish(leaving)


def local_steps(where, tokens, factor_d, factor_c, base):
    extra = [] if base is None else [base]
    fetch = base is None
    place = ANY if fetch else VMEM
    return call(
        functools.partial(local_kernel, fetch),
        "steps_d_c",
        (jax.ShapeDtypeStruct((BLK, 2, RANKS, RANKS, 16, LANES), BF16), DONE),
        [SMEM, ANY, place, place] + [ANY] * len(extra),
        (ANY, VMEM),
        [
            pltpu.VMEM((4, SQUARE, LANES), BF16),
            FACTOR,
            FACTOR,
            WIDE_SHAPE,
            pltpu.VMEM((4, BLK, BLK, LANES), BF16),
            pltpu.VMEM((SUB, BLK, 16, LANES), BF16),
            pltpu.SemaphoreType.DMA((6,)),
            pltpu.SemaphoreType.DMA((SUB,)),
        ]
        + [RAW, RAW] * fetch,
        flops=2**31,
        moved=3 * 2**20,
        aliases={4: 0} if extra else None,
        grant=LARGE if fetch else MEDIUM,
    )(where, tokens, factor_d, factor_c, *extra)


def d_lo_minor(row):
    return row % 4 * BLK + row // 4


def quad_rows(factor_ref, quad):
    rows = [factor_ref[high * 64 + quad * 16 : high * 64 + quad * 16 + 16, :] for high in range(2)]
    return jnp.concatenate(rows, axis=0)


READY = jax.ShapeDtypeStruct((4, 4, SUB, BLK, WIDE), BF16)


def weights_kernel(fb_ref, fa_ref, after_ref, out_ref, fb_raw, fa_raw, factor_ref, spread_ref, wide_v, sem, out_sem):
    arriving = started(
        [
            pltpu.make_async_copy(ref, raw, sem.at[n])
            for n, (ref, raw) in enumerate(((fb_ref, fb_raw), (fa_ref, fa_raw)))
        ]
    )
    fill_spread(spread_ref)
    leaving = []
    for n, raw in enumerate((fb_raw, fa_raw)):
        arriving[n].wait()
        take(raw[...], factor_ref, d_lo_minor)
        for step in range(2):
            slot = 2 * n + step
            rows = quad_rows(factor_ref, step) if n else factor_ref[(2 + step) * BLK : (3 + step) * BLK, :]
            widen_minor(rows, spread_ref, wide_v.at[slot])
            leaving += started([pltpu.make_async_copy(wide_v.at[slot], out_ref.at[slot], out_sem.at[slot])])
    finish(leaving)


def weights(factor_b, factor_a, after):
    return call(
        weights_kernel,
        "weights",
        READY,
        [ANY, ANY, ANY],
        ANY,
        [
            RAW,
            RAW,
            FACTOR,
            SPREAD_SHAPE,
            pltpu.VMEM(READY.shape, BF16),
            pltpu.SemaphoreType.DMA((2,)),
            pltpu.SemaphoreType.DMA((4,)),
        ],
        flops=2**30,
        moved=3 * 2**20,
    )(factor_b, factor_a, after)


def step_a_quad(slot, factor, third_ref, row_of, spread_ref, wide_ref, sent_v):
    if factor is not None:
        widen_minor(factor, spread_ref, wide_ref)
    for high in range(2):
        halves = []
        for pair in range(2):
            first = row_of(high) + 2 * pair
            data = third_ref[first : first + 2].reshape(WIDE, ALL)
            halves.append(apply(wide_ref, 2 * high + pair, data))
        sent_v[slot, :, high] = jnp.concatenate(halves, axis=1).astype(BF16)


def middle_kernel(count, held_ref, fb_ref, ready_ref, *rest):
    third_ref, sent_ref, held_v, fb_raw, fb_v, wide_b, wide_a = rest[-12:-5]
    spread_ref, third_v, sent_v, sem, out_sem = rest[-5:]
    factor = started([pltpu.make_async_copy(fb_ref, fb_raw, sem.at[4])])
    rows = [pl.ds(8 * step, 8) for step in range(4)]
    arriving = [pltpu.make_async_copy(held_ref.at[rows[n]], held_v.at[rows[n]], sem.at[n]) for n in range(4)]
    ready_b = pltpu.make_async_copy(ready_ref.at[pl.ds(0, 2)], wide_b.at[pl.ds(2, 2)], sem.at[5])
    ready_a = pltpu.make_async_copy(ready_ref.at[pl.ds(2, 2)], wide_a, sem.at[6])
    started(arriving[:2] + [ready_b] + arriving[2:] + [ready_a])
    fill_spread(spread_ref)
    finish(factor)
    take(fb_raw[...], fb_v, d_lo_minor)
    leaving = []
    later = 16 - 4 * count
    for step in range(4):
        if step < 2:
            widen_minor(fb_v[step * BLK : (step + 1) * BLK, :], spread_ref, wide_b.at[step])
        elif step == 2:
            ready_b.wait()
        arriving[step].wait()
        for quad in range(2):
            halves = []
            for pair in range(2):
                a = 8 * step + 4 * quad + 2 * pair
                data = [held_v[a : a + 2, :, rank].reshape(WIDE, LANES) for rank in range(RANKS)]
                halves.append(apply(wide_b.at[step], 2 * quad + pair, jnp.concatenate(data, axis=1)))
            first = step * BLK + quad * 16
            third_v[:, first : first + 16, :] = jnp.concatenate(halves, axis=1).astype(BF16)
        for high in range(2):
            block = (pl.ds(high * 16 + 4 * count, later), pl.ds(step * BLK, BLK))
            leaving += started(
                [pltpu.make_async_copy(third_v.at[block], third_ref.at[block], out_sem.at[step, high])]
            )
    ready_a.wait()
    for quad in range(count):
        row_of = lambda high: high * 16 + quad * 4
        step_a_quad(quad, None, third_v, row_of, None, wide_a.at[quad], sent_v)
        leaving += started([pltpu.make_async_copy(sent_v.at[quad], sent_ref.at[:, :, quad], out_sem.at[4, quad])])
    finish(leaving)


def sent_shape(count):
    return jax.ShapeDtypeStruct((BLK, 2, count, 16, ALL), BF16)


def middle(held, factor_b, ready, count, after):
    return call(
        functools.partial(middle_kernel, count),
        "steps_b_a",
        (jax.ShapeDtypeStruct((BLK, LANES, ALL), BF16), sent_shape(count)),
        [ANY] * (3 + len(after)),
        (ANY, ANY),
        [
            pltpu.VMEM(held.shape, BF16),
            RAW,
            FACTOR,
            pltpu.VMEM((4, 4, SUB, BLK, WIDE), BF16),
            pltpu.VMEM((count, 4, SUB, BLK, WIDE), BF16),
            SPREAD_SHAPE,
            pltpu.VMEM((BLK, LANES, ALL), BF16),
            pltpu.VMEM((count, BLK, 2, 16, ALL), BF16),
            pltpu.SemaphoreType.DMA((7,)),
            pltpu.SemaphoreType.DMA((5, max(2, count))),
        ],
        flops=2**32,
        moved=9 * 2**20,
    )(held, factor_b, ready, *after)


def step_a_kernel(first_quad, count, third_ref, fa_ref, *rest):
    sent_ref, third_v, fa_raw, fa_v, wide_ref, spread_ref, sent_v, sem, out_sem = rest[-9:]
    arriving = started(
        [pltpu.make_async_copy(fa_ref, fa_raw, sem.at[2])]
        + [
            pltpu.make_async_copy(
                third_ref.at[pl.ds(high * 16 + 4 * first_quad, 4 * count)],
                third_v.at[pl.ds(high * 4 * count, 4 * count)],
                sem.at[high],
            )
            for high in range(2)
        ]
    )
    fill_spread(spread_ref)
    finish(arriving)
    take(fa_raw[...], fa_v, d_lo_minor)
    leaving = []
    for slot in range(count):
        row_of = lambda high: (high * count + slot) * 4
        step_a_quad(slot, quad_rows(fa_v, first_quad + slot), third_v, row_of, spread_ref, wide_ref, sent_v)
        leaving += started([pltpu.make_async_copy(sent_v.at[slot], sent_ref.at[:, :, slot], out_sem.at[slot])])
    finish(leaving)


def step_a(third, factor_a, first_quad, count, after):
    return call(
        functools.partial(step_a_kernel, first_quad, count),
        "step_a",
        sent_shape(count),
        [ANY] * (2 + len(after)),
        ANY,
        [
            pltpu.VMEM((8 * count, LANES, ALL), BF16),
            RAW,
            FACTOR,
            WIDE_SHAPE,
            SPREAD_SHAPE,
            pltpu.VMEM((count, BLK, 2, 16, ALL), BF16),
            pltpu.SemaphoreType.DMA((3,)),
            pltpu.SemaphoreType.DMA((count,)),
        ],
        flops=2**29 * count,
        moved=2**21 * count,
        grant=SMALL,
    )(third, factor_a, *after)


def place_of(row, f):
    turn, s, p, low = row // 64, row // 16 % 4, row // 4 % 4, row % 4
    return p * 64 + s * 16 + (turn ^ f) * 4 + low


def split_kernel(f_ref, tokens_ref, w_ref, after_ref, *rest):
    out_refs, w_out_ref = rest[: 4 * RANKS], rest[4 * RANKS]
    order_ref, tokens_v, out_v, sem, out_sem = rest[4 * RANKS + 1 :]
    leaving = started([pltpu.make_async_copy(w_ref, w_out_ref, sem.at[4])])
    size = 4 * SQUARE
    arriving = started(
        [
            pltpu.make_async_copy(tokens_ref.at[pl.ds(quad * size, size), :], tokens_v.at[quad], sem.at[quad])
            for quad in range(4)
        ]
    )
    order_ref[...] = ones_where(place_of(iota((WIDE, WIDE), 0), f_ref[0]) == iota((WIDE, WIDE), 1))
    for quad in range(4):
        arriving[quad].wait()

        for step in range(4):
            blocks = []
            for one in range(4):
                start = step * 256 + one * 64
                rows = [tokens_v[quad, p * SQUARE + start : p * SQUARE + start + 64, :] for p in range(4)]
                blocks.append(jnp.concatenate(rows, axis=0))
            held = jnp.concatenate(blocks, axis=1)
            moved = jnp.dot(order_ref[...], held, preferred_element_type=F32).astype(BF16)
            for turn in range(RANKS):
                for one in range(4):
                    block = moved[turn * 64 : turn * 64 + 64, one * LANES : (one + 1) * LANES]
                    start = step * 256 + one * 64
                    out_v[turn, quad, start : start + 64, :] = block

        leaving += started(
            [
                pltpu.make_async_copy(out_v.at[turn, quad], out_refs[quad * RANKS + turn], out_sem.at[turn, quad])
                for turn in range(RANKS)
            ]
        )
    finish(leaving)


def split(f, tokens, w, after):
    *parts, w = call(
        split_kernel,
        "split",
        [jax.ShapeDtypeStruct((SQUARE, LANES), BF16)] * (4 * RANKS) + [jax.ShapeDtypeStruct(w.shape, BF16)],
        [SMEM, ANY, ANY, ANY],
        [ANY] * (4 * RANKS + 1),
        [
            pltpu.VMEM((WIDE, WIDE), BF16),
            pltpu.VMEM((4, 4 * SQUARE, LANES), BF16),
            pltpu.VMEM((RANKS, 4, SQUARE, LANES), BF16),
            pltpu.SemaphoreType.DMA((5,)),
            pltpu.SemaphoreType.DMA((RANKS, 4)),
        ],
        flops=2**30,
        moved=8 * 2**20,
    )(f, tokens, w, after)
    return [parts[RANKS * quad : RANKS * (quad + 1)] for quad in range(4)], w


def gather_kernel(count, f_ref, *rest):
    token_refs, w_refs = rest[: RANKS * count], rest[RANKS * count : RANKS * (count + 1)]
    out_refs, (w_ref, w_v, sem) = rest[-3 - count : -3], rest[-3:]
    f = f_ref[0]
    weights = started([pltpu.make_async_copy(w_refs[turn], w_v.at[turn], sem.at[turn]) for turn in range(RANKS)])
    arriving = started(
        [
            pltpu.make_async_copy(ref, out_refs[n // RANKS].at[n % RANKS], sem.at[RANKS + n])
            for n, ref in enumerate(token_refs)
        ]
    )
    finish(weights)
    for row in range(RANKS):
        for column in range(RANKS):
            block = w_v[column, aligned((f ^ row) * LANES, LANES), :]
            w_ref[row * LANES : (row + 1) * LANES, column * LANES : (column + 1) * LANES] = block
    finish(arriving)


def gather(f, tokens, w):
    count = len(tokens)
    *parts, w = call(
        functools.partial(gather_kernel, count),
        "gather",
        [jax.ShapeDtypeStruct((RANKS, SQUARE, LANES), BF16)] * count + [jax.ShapeDtypeStruct((ALL, ALL), BF16)],
        [SMEM] + [ANY] * (RANKS * (count + 1)),
        [VMEM] * (count + 1),
        [pltpu.VMEM((RANKS, ALL, LANES), BF16), pltpu.SemaphoreType.DMA((RANKS * (count + 1),))],
        flops=0,
        moved=count * 2**21 + 2**20,
        grant=SMALL,
    )(f, *sum(tokens, []), *w)
    return parts, w


def project_kernel(first, count, f_ref, mixed_ref, w_ref, *rest):
    token_refs, out_refs = rest[:count], rest[-RANKS * count :]
    f = f_ref[0]
    tile = SQUARE // 2
    for quad in range(count):
        for half in range(2):
            rows, blocks = slice(half * tile, (half + 1) * tile), slice(half * 32, (half + 1) * 32)
            gated = []
            for turn in range(RANKS):
                mixed = mixed_ref[blocks, first + quad, :, aligned((f ^ turn) * LANES, LANES)].reshape(tile, LANES)
                value = token_refs[quad][turn, rows, :].astype(F32)
                gated.append((mixed.astype(F32) * (value / (1.0 + jnp.exp(-value)))).astype(BF16))
            result = jnp.dot(jnp.concatenate(gated, axis=1), w_ref[...], preferred_element_type=F32).astype(BF16)
            for turn in range(RANKS):
                out_refs[RANKS * quad + turn][rows, :] = result[:, turn * LANES : (turn + 1) * LANES]


def project(f, mixed, tokens, w, first, count, after):
    size = count * SQUARE * ALL
    parts = call(
        functools.partial(project_kernel, first, count),
        "project",
        [jax.ShapeDtypeStruct((SQUARE, LANES), BF16)] * (RANKS * count),
        [SMEM] + [VMEM] * (2 + count) + [ANY] * len(after),
        [VMEM] * (RANKS * count),
        [],
        flops=size * 1024,
        moved=size * 6,
        exps=size,
        grant=SMALL,
    )(f, mixed, w, *tokens[first : first + count], *after)
    return [parts[RANKS * quad : RANKS * (quad + 1)] for quad in range(count)]


def merge_kernel(first_row, f_ref, *rest):
    part_refs, (out_ref, done_ref, order_ref, held_v, out_sem) = rest[:RANKS], rest[-5:]
    count = part_refs[0].shape[0] // SQUARE
    done_ref[...] = jnp.zeros_like(done_ref)
    order_ref[...] = ones_where(place_of(iota((WIDE, WIDE), 1), f_ref[0]) == iota((WIDE, WIDE), 0))
    leaving = []
    for quad in range(count):
        for step in range(4):
            blocks = []
            for one in range(4):
                start = quad * SQUARE + step * 256 + one * 64
                rows = [ref[start : start + 64, :] for ref in part_refs]
                blocks.append(jnp.concatenate(rows, axis=0))
            held = jnp.concatenate(blocks, axis=1)
            moved = jnp.dot(order_ref[...], held, preferred_element_type=F32).astype(BF16)
            for p in range(4):
                for one in range(4):
                    block = moved[p * 64 : p * 64 + 64, one * LANES : (one + 1) * LANES]
                    start = p * SQUARE + step * 256 + one * 64
                    held_v[quad, start : start + 64, :] = block
                rows = pl.ds(p * SQUARE + step * 256, 256)
                target = out_ref.at[pl.ds(first_row + (quad * 4 + p) * SQUARE + step * 256, 256), :]
                leaving += started(
                    [pltpu.make_async_copy(held_v.at[quad, rows, :], target, out_sem.at[quad, step * 4 + p])]
                )
    finish(leaving)


def merge(f, parts, total, first_quad, base, after):
    rows = parts[0].shape[0]
    count = rows // SQUARE
    extra = [] if base is None else [base]
    return call(
        functools.partial(merge_kernel, first_quad * 4 * SQUARE),
        "merge",
        (jax.ShapeDtypeStruct((total, LANES), BF16), DONE),
        [SMEM] + [VMEM] * RANKS + [ANY] * (len(extra) + len(after)),
        (ANY, VMEM),
        [
            pltpu.VMEM((WIDE, WIDE), BF16),
            pltpu.VMEM((count, 4 * SQUARE, LANES), BF16),
            pltpu.SemaphoreType.DMA((count, 16)),
        ],
        flops=rows * 4 * WIDE * LANES * 2,
        moved=rows * LANES * 16,
        aliases={5: 0} if extra else None,
        grant=SMALL,
    )(f, *parts, *extra, *after)


TURNS = [[(rank, rank ^ turn) for rank in range(RANKS)] for turn in range(RANKS)]


def swap(parts):
    return [parts[0]] + [lax.ppermute(parts[turn], "fsdp", TURNS[turn]) for turn in (2, 1, 3)]


def in_turn(got):
    return [got[0], got[2], got[1], got[3]]


def hold_kernel(x_ref, after_ref, out_ref):
    pass


def hold(x, after):
    return call(
        hold_kernel,
        "hold",
        jax.ShapeDtypeStruct(x.shape, x.dtype),
        [ANY, ANY],
        ANY,
        [],
        flops=0,
        moved=0,
        aliases={0: 0},
        grant=SMALL,
    )(x, after)


def share(x):
    chip = lax.ppermute(x, "fsdp", TURNS[2])
    core = lax.ppermute(x, "fsdp", TURNS[1])
    far = lax.ppermute(chip, "fsdp", TURNS[1])
    return [x, core, chip, far]


def body(tokens, factor_d, factor_c, factor_b, factor_a, w_proj):
    local_rows = tokens.shape[0]
    f = lax.axis_index("fsdp").astype(jnp.int32).reshape(1)

    raw = lambda factor: factor.transpose(1, 2, 0).reshape(SQUARE, LANES)

    own = (raw(factor_d), raw(factor_c))
    core = [lax.ppermute(x, "fsdp", TURNS[1]) for x in own]
    chip = [lax.ppermute(x, "fsdp", TURNS[2]) for x in own]
    second, _ = local_steps(f, tokens, *own, None)
    second, done = local_steps(f ^ 1, tokens, *core, second)
    chip = [hold(x, done) for x in chip]
    far = [lax.ppermute(x, "fsdp", TURNS[1]) for x in chip]
    second, _ = local_steps(f ^ 2, tokens, *chip, second)
    second, _ = local_steps(f ^ 3, tokens, *far, second)
    token_parts, w = split(f, tokens, w_proj, second)
    w = share(w)
    token_parts = [in_turn(swap(quad)) for quad in token_parts]
    arrived = lax.all_to_all(
        second.reshape(64 * RANKS, 64, LANES), ("ctx", "fsdp"), split_axis=0, concat_axis=0, tiled=True
    )
    ready = weights(raw(factor_b), raw(factor_a), second)
    early = [part for quad in token_parts[:3] for part in quad[1:]]
    third, first_sent = middle(
        arrived.reshape(BLK, 2, RANKS, 64, LANES), raw(factor_b), ready, RETURN_QUADS[0], early + w[1:]
    )

    out, first_quad, after = None, 0, []
    gathered = [gather(f, token_parts[:2], w), gather(f, token_parts[2:], w)]
    for k, count in enumerate(RETURN_QUADS):
        sent = step_a(third, raw(factor_a), first_quad, count, token_parts[3][1:] + [gathered[0][1]]) if k else first_sent
        mixed = lax.all_to_all(
            sent.reshape(64, count * 16, ALL), "ctx", split_axis=0, concat_axis=0, tiled=True
        ).reshape(64, count, 16, ALL)
        tokens_here, w_here = gathered[k]
        parts, size = [], 1 if k else count
        for slot in range(0, count, size):
            here = project(f, mixed, tokens_here, w_here, slot, size, after)
            parts += [in_turn(swap(part)) for part in here]
        ends = []
        for part in parts:
            out, done = merge(f, part, local_rows, first_quad, out, [] if first_quad else [gathered[1][1]])
            first_quad += 1
            ends.append(done)
        after = ends[:1]
    return out


def solution(mesh):
    in_specs = (
        P("ctx", "fsdp"),
        P(("ctx", "fsdp"), None, None),
        P(("ctx", "fsdp"), None, None),
        P(("ctx", "fsdp"), None, None),
        P(("ctx", "fsdp"), None, None),
        P(None, "fsdp"),
    )
    out_specs = P("ctx", "fsdp")
    return jax.shard_map(body, mesh=mesh, in_specs=in_specs, out_specs=out_specs, check_vma=False)
```

```python
import functools

import jax
import jax.numpy as jnp
from jax import lax
from jax.experimental import pallas as pl
from jax.experimental.pallas import tpu as pltpu
from jax.sharding import PartitionSpec as P

BLK = 32
LANES = 128
SUB = 8
WIDE = SUB * BLK
PACK = LANES // BLK
SQUARE = BLK * BLK
RANKS = 4
ALL = RANKS * LANES
BF16 = jnp.bfloat16
F32 = jnp.float32
MIB = 1024 * 1024
LARGE, MEDIUM, SMALL = 60 * MIB, 53 * MIB, 24 * MIB
RETURN_QUADS = (2, 2)

VMEM = pl.BlockSpec(memory_space=pltpu.VMEM)
SMEM = pl.BlockSpec(memory_space=pltpu.SMEM)
ANY = pl.BlockSpec(memory_space=pl.ANY)
FACTOR = pltpu.VMEM((LANES, SQUARE), BF16)
DONE = jax.ShapeDtypeStruct((SUB, LANES), F32)
RAW = pltpu.VMEM((SQUARE, LANES), BF16)
WIDE_SHAPE = pltpu.VMEM((4, SUB, BLK, WIDE), BF16)
SPREAD_SHAPE = pltpu.VMEM((PACK, LANES, WIDE), BF16)


def call(kernel, name, out_shape, in_specs, out_specs, scratch, flops, moved, exps=0, aliases=None, grant=LARGE):
    return pl.pallas_call(
        kernel,
        name=name,
        out_shape=out_shape,
        in_specs=in_specs,
        out_specs=out_specs,
        scratch_shapes=scratch,
        input_output_aliases=aliases or {},
        compiler_params=pltpu.CompilerParams(vmem_limit_bytes=grant),
        cost_estimate=pl.CostEstimate(flops=flops, bytes_accessed=moved, transcendentals=exps),
    )


def aligned(start, size):
    return pl.ds(pl.multiple_of(start, size), size)


def started(copies):
    for copy in copies:
        copy.start()
    return copies


def finish(copies):
    for copy in copies:
        copy.wait()


def iota(shape, axis):
    return lax.broadcasted_iota(jnp.int32, shape, axis)


def ones_where(condition):
    return jnp.where(condition, 1.0, 0.0).astype(BF16)


def take(raw, factor_ref, source_of):
    shape = (LANES, LANES)
    order = ones_where(source_of(iota(shape, 0)) == iota(shape, 1))
    factor = lax.dot_general(order, raw, (((1,), (1,)), ((), ())), preferred_element_type=F32)
    factor_ref[...] = factor.astype(BF16)


def widen_major(factor, wide_ref):
    rows = factor.astype(F32)
    block, row = iota((BLK, LANES), 1) // BLK, iota((BLK, LANES), 0) % SUB
    keeps = (block == row, block == row - PACK)
    for m in range(SUB):
        turned = rows[:, m * LANES : (m + 1) * LANES]
        rolled = [pltpu.roll(turned, turn * BLK, 1) for turn in range(1, PACK)]
        for turn in range(1, PACK):
            turned = jnp.where(row % PACK == turn, rolled[turn - 1], turned)
        for half in range(PACK // 2):
            parts = []
            for q in (2 * half, 2 * half + 1):
                here = turned if q == 0 else pltpu.roll(turned, LANES - q * BLK, 1)
                both = jnp.concatenate([jnp.where(keep, here, 0.0) for keep in keeps], axis=1)
                parts.append(both.reshape(4, SUB, WIDE))
            wide_ref[:, m, half * 16 : half * 16 + 16, :] = jnp.concatenate(parts, axis=1).astype(BF16)


def fill_spread(spread_ref):
    row, want = iota((LANES, WIDE), 0), iota((LANES, WIDE), 1) // 4 % BLK
    for q in range(PACK):
        spread_ref[q] = ones_where(row == want + q * BLK)


def widen_minor(factor, spread_ref, wide_ref):
    rows = factor.astype(F32).reshape(4, SUB, SQUARE)
    tiles = [rows[:, :, m * LANES : (m + 1) * LANES] for m in range(SUB)]
    left = jnp.stack(tiles, axis=1).reshape(WIDE, LANES).astype(BF16)
    shape = (1, SUB, WIDE)
    keep = iota(shape, 1) == iota(shape, 2) // LANES * 4 + iota(shape, 2) % 4
    for half in range(PACK // 2):
        parts = []
        for q in (2 * half, 2 * half + 1):
            part = jnp.dot(left, spread_ref[q], preferred_element_type=F32)
            parts.append(jnp.where(keep, part.reshape(BLK, SUB, WIDE), 0.0))
        both = jnp.concatenate(parts, axis=1).astype(BF16)
        wide_ref[:, :, half * 16 : half * 16 + 16, :] = both.reshape(4, SUB, 16, WIDE)


def apply(wide_ref, group, data):
    left = wide_ref[group].reshape(WIDE, WIDE)
    return jnp.dot(left, data, preferred_element_type=F32).reshape(BLK, SUB, data.shape[1])


def local_kernel(fetch, where_ref, tokens_ref, fd_ref, fc_ref, *rest):
    out_ref, done_ref, tokens_v, fd_v, fc_v, wide_ref, first_ref, out_v, sem, out_sem = rest[-10 - 2 * fetch :][:10]
    fetched = []
    if fetch:
        fetched = started(
            [pltpu.make_async_copy(ref, rest[n - 2], sem.at[4 + n]) for n, ref in enumerate((fd_ref, fc_ref))]
        )
        fd_ref, fc_ref = rest[-2:]
    done_ref[...] = jnp.zeros_like(done_ref)
    quarter = where_ref[0]
    arriving = started(
        [
            pltpu.make_async_copy(tokens_ref.at[aligned((quarter * 4 + p) * SQUARE, SQUARE), :], tokens_v.at[p], sem.at[p])
            for p in range(4)
        ]
    )
    finish(fetched)
    take(fd_ref[...], fd_v, lambda r: r)
    take(fc_ref[...], fc_v, lambda r: r // 4 % 4 * BLK + r // 16 * 4 + r % 4)
    for p in range(4):
        widen_major(fd_v[p * BLK : (p + 1) * BLK, :], wide_ref)
        arriving[p].wait()
        for pair in range(2):
            halves = [
                apply(wide_ref, group, tokens_v[p, group * WIDE : (group + 1) * WIDE, :])
                for group in (2 * pair, 2 * pair + 1)
            ]
            first_ref[p, :, pair * 16 : pair * 16 + 16, :] = jnp.concatenate(halves, axis=1).astype(BF16)
    leaving = []
    for step in range(4):
        widen_major(fc_v[step * BLK : (step + 1) * BLK, :], wide_ref)
        for one in range(2):
            quad = 2 * step + one
            halves = []
            for pair in range(2):
                held = first_ref[2 * pair : 2 * pair + 2, 4 * quad : 4 * quad + 4]
                halves.append(apply(wide_ref, 2 * one + pair, held.reshape(WIDE, LANES)))
            out_v[quad] = jnp.concatenate(halves, axis=1).astype(BF16)
            target = out_ref.at[:, quad // 4, quad % 4, quarter]
            leaving += started([pltpu.make_async_copy(out_v.at[quad], target, out_sem.at[quad])])
    finish(leaving)


def local_steps(where, tokens, factor_d, factor_c, base):
    extra = [] if base is None else [base]
    fetch = base is None
    place = ANY if fetch else VMEM
    return call(
        functools.partial(local_kernel, fetch),
        "steps_d_c",
        (jax.ShapeDtypeStruct((BLK, 2, RANKS, RANKS, 16, LANES), BF16), DONE),
        [SMEM, ANY, place, place] + [ANY] * len(extra),
        (ANY, VMEM),
        [
            pltpu.VMEM((4, SQUARE, LANES), BF16),
            FACTOR,
            FACTOR,
            WIDE_SHAPE,
            pltpu.VMEM((4, BLK, BLK, LANES), BF16),
            pltpu.VMEM((SUB, BLK, 16, LANES), BF16),
            pltpu.SemaphoreType.DMA((6,)),
            pltpu.SemaphoreType.DMA((SUB,)),
        ]
        + [RAW, RAW] * fetch,
        flops=2**31,
        moved=3 * 2**20,
        aliases={4: 0} if extra else None,
        grant=LARGE if fetch else MEDIUM,
    )(where, tokens, factor_d, factor_c, *extra)


def d_lo_minor(row):
    return row % 4 * BLK + row // 4


def quad_rows(factor_ref, quad):
    rows = [factor_ref[high * 64 + quad * 16 : high * 64 + quad * 16 + 16, :] for high in range(2)]
    return jnp.concatenate(rows, axis=0)


READY = jax.ShapeDtypeStruct((4, 4, SUB, BLK, WIDE), BF16)


def weights_kernel(fb_ref, fa_ref, after_ref, out_ref, fb_raw, fa_raw, factor_ref, spread_ref, wide_v, sem, out_sem):
    arriving = started(
        [
            pltpu.make_async_copy(ref, raw, sem.at[n])
            for n, (ref, raw) in enumerate(((fb_ref, fb_raw), (fa_ref, fa_raw)))
        ]
    )
    fill_spread(spread_ref)
    leaving = []
    for n, raw in enumerate((fb_raw, fa_raw)):
        arriving[n].wait()
        take(raw[...], factor_ref, d_lo_minor)
        for step in range(2):
            slot = 2 * n + step
            rows = quad_rows(factor_ref, step) if n else factor_ref[(2 + step) * BLK : (3 + step) * BLK, :]
            widen_minor(rows, spread_ref, wide_v.at[slot])
            leaving += started([pltpu.make_async_copy(wide_v.at[slot], out_ref.at[slot], out_sem.at[slot])])
    finish(leaving)


def weights(factor_b, factor_a, after):
    return call(
        weights_kernel,
        "weights",
        READY,
        [ANY, ANY, ANY],
        ANY,
        [
            RAW,
            RAW,
            FACTOR,
            SPREAD_SHAPE,
            pltpu.VMEM(READY.shape, BF16),
            pltpu.SemaphoreType.DMA((2,)),
            pltpu.SemaphoreType.DMA((4,)),
        ],
        flops=2**30,
        moved=3 * 2**20,
    )(factor_b, factor_a, after)


def step_a_quad(slot, factor, third_ref, row_of, spread_ref, wide_ref, sent_v):
    if factor is not None:
        widen_minor(factor, spread_ref, wide_ref)
    for high in range(2):
        halves = []
        for pair in range(2):
            first = row_of(high) + 2 * pair
            data = third_ref[first : first + 2].reshape(WIDE, ALL)
            halves.append(apply(wide_ref, 2 * high + pair, data))
        sent_v[slot, :, high] = jnp.concatenate(halves, axis=1).astype(BF16)


def middle_kernel(count, held_ref, fb_ref, ready_ref, *rest):
    third_ref, sent_ref, held_v, fb_raw, fb_v, wide_b, wide_a = rest[-12:-5]
    spread_ref, third_v, sent_v, sem, out_sem = rest[-5:]
    factor = started([pltpu.make_async_copy(fb_ref, fb_raw, sem.at[4])])
    rows = [pl.ds(8 * step, 8) for step in range(4)]
    arriving = [pltpu.make_async_copy(held_ref.at[rows[n]], held_v.at[rows[n]], sem.at[n]) for n in range(4)]
    ready_b = pltpu.make_async_copy(ready_ref.at[pl.ds(0, 2)], wide_b.at[pl.ds(2, 2)], sem.at[5])
    ready_a = pltpu.make_async_copy(ready_ref.at[pl.ds(2, 2)], wide_a, sem.at[6])
    started(arriving[:2] + [ready_b] + arriving[2:] + [ready_a])
    fill_spread(spread_ref)
    finish(factor)
    take(fb_raw[...], fb_v, d_lo_minor)
    leaving = []
    later = 16 - 4 * count
    for step in range(4):
        if step < 2:
            widen_minor(fb_v[step * BLK : (step + 1) * BLK, :], spread_ref, wide_b.at[step])
        elif step == 2:
            ready_b.wait()
        arriving[step].wait()
        for quad in range(2):
            halves = []
            for pair in range(2):
                a = 8 * step + 4 * quad + 2 * pair
                data = [held_v[a : a + 2, :, rank].reshape(WIDE, LANES) for rank in range(RANKS)]
                halves.append(apply(wide_b.at[step], 2 * quad + pair, jnp.concatenate(data, axis=1)))
            first = step * BLK + quad * 16
            third_v[:, first : first + 16, :] = jnp.concatenate(halves, axis=1).astype(BF16)
        for high in range(2):
            block = (pl.ds(high * 16 + 4 * count, later), pl.ds(step * BLK, BLK))
            leaving += started(
                [pltpu.make_async_copy(third_v.at[block], third_ref.at[block], out_sem.at[step, high])]
            )
    ready_a.wait()
    for quad in range(count):
        row_of = lambda high: high * 16 + quad * 4
        step_a_quad(quad, None, third_v, row_of, None, wide_a.at[quad], sent_v)
        leaving += started([pltpu.make_async_copy(sent_v.at[quad], sent_ref.at[:, :, quad], out_sem.at[4, quad])])
    finish(leaving)


def sent_shape(count):
    return jax.ShapeDtypeStruct((BLK, 2, count, 16, ALL), BF16)


def middle(held, factor_b, ready, count, after):
    return call(
        functools.partial(middle_kernel, count),
        "steps_b_a",
        (jax.ShapeDtypeStruct((BLK, LANES, ALL), BF16), sent_shape(count)),
        [ANY] * (3 + len(after)),
        (ANY, ANY),
        [
            pltpu.VMEM(held.shape, BF16),
            RAW,
            FACTOR,
            pltpu.VMEM((4, 4, SUB, BLK, WIDE), BF16),
            pltpu.VMEM((count, 4, SUB, BLK, WIDE), BF16),
            SPREAD_SHAPE,
            pltpu.VMEM((BLK, LANES, ALL), BF16),
            pltpu.VMEM((count, BLK, 2, 16, ALL), BF16),
            pltpu.SemaphoreType.DMA((7,)),
            pltpu.SemaphoreType.DMA((5, max(2, count))),
        ],
        flops=2**32,
        moved=9 * 2**20,
    )(held, factor_b, ready, *after)


def step_a_kernel(first_quad, count, third_ref, fa_ref, *rest):
    sent_ref, third_v, fa_raw, fa_v, wide_ref, spread_ref, sent_v, sem, out_sem = rest[-9:]
    arriving = started(
        [pltpu.make_async_copy(fa_ref, fa_raw, sem.at[2])]
        + [
            pltpu.make_async_copy(
                third_ref.at[pl.ds(high * 16 + 4 * first_quad, 4 * count)],
                third_v.at[pl.ds(high * 4 * count, 4 * count)],
                sem.at[high],
            )
            for high in range(2)
        ]
    )
    fill_spread(spread_ref)
    finish(arriving)
    take(fa_raw[...], fa_v, d_lo_minor)
    leaving = []
    for slot in range(count):
        row_of = lambda high: (high * count + slot) * 4
        step_a_quad(slot, quad_rows(fa_v, first_quad + slot), third_v, row_of, spread_ref, wide_ref, sent_v)
        leaving += started([pltpu.make_async_copy(sent_v.at[slot], sent_ref.at[:, :, slot], out_sem.at[slot])])
    finish(leaving)


def step_a(third, factor_a, first_quad, count, after):
    return call(
        functools.partial(step_a_kernel, first_quad, count),
        "step_a",
        sent_shape(count),
        [ANY] * (2 + len(after)),
        ANY,
        [
            pltpu.VMEM((8 * count, LANES, ALL), BF16),
            RAW,
            FACTOR,
            WIDE_SHAPE,
            SPREAD_SHAPE,
            pltpu.VMEM((count, BLK, 2, 16, ALL), BF16),
            pltpu.SemaphoreType.DMA((3,)),
            pltpu.SemaphoreType.DMA((count,)),
        ],
        flops=2**29 * count,
        moved=2**21 * count,
        grant=SMALL,
    )(third, factor_a, *after)


def place_of(row, f):
    turn, s, p, low = row // 64, row // 16 % 4, row // 4 % 4, row % 4
    return p * 64 + s * 16 + (turn ^ f) * 4 + low


def split_kernel(f_ref, tokens_ref, w_ref, after_ref, *rest):
    out_refs, w_out_ref = rest[: 4 * RANKS], rest[4 * RANKS]
    order_ref, tokens_v, out_v, sem, out_sem = rest[4 * RANKS + 1 :]
    leaving = started([pltpu.make_async_copy(w_ref, w_out_ref, sem.at[4])])
    size = 4 * SQUARE
    arriving = started(
        [
            pltpu.make_async_copy(tokens_ref.at[pl.ds(quad * size, size), :], tokens_v.at[quad], sem.at[quad])
            for quad in range(4)
        ]
    )
    order_ref[...] = ones_where(place_of(iota((WIDE, WIDE), 0), f_ref[0]) == iota((WIDE, WIDE), 1))
    for quad in range(4):
        arriving[quad].wait()

        for step in range(4):
            blocks = []
            for one in range(4):
                start = step * 256 + one * 64
                rows = [tokens_v[quad, p * SQUARE + start : p * SQUARE + start + 64, :] for p in range(4)]
                blocks.append(jnp.concatenate(rows, axis=0))
            held = jnp.concatenate(blocks, axis=1)
            moved = jnp.dot(order_ref[...], held, preferred_element_type=F32).astype(BF16)
            for turn in range(RANKS):
                for one in range(4):
                    block = moved[turn * 64 : turn * 64 + 64, one * LANES : (one + 1) * LANES]
                    start = step * 256 + one * 64
                    out_v[turn, quad, start : start + 64, :] = block

        leaving += started(
            [
                pltpu.make_async_copy(out_v.at[turn, quad], out_refs[quad * RANKS + turn], out_sem.at[turn, quad])
                for turn in range(RANKS)
            ]
        )
    finish(leaving)


def split(f, tokens, w, after):
    *parts, w = call(
        split_kernel,
        "split",
        [jax.ShapeDtypeStruct((SQUARE, LANES), BF16)] * (4 * RANKS) + [jax.ShapeDtypeStruct(w.shape, BF16)],
        [SMEM, ANY, ANY, ANY],
        [ANY] * (4 * RANKS + 1),
        [
            pltpu.VMEM((WIDE, WIDE), BF16),
            pltpu.VMEM((4, 4 * SQUARE, LANES), BF16),
            pltpu.VMEM((RANKS, 4, SQUARE, LANES), BF16),
            pltpu.SemaphoreType.DMA((5,)),
            pltpu.SemaphoreType.DMA((RANKS, 4)),
        ],
        flops=2**30,
        moved=8 * 2**20,
    )(f, tokens, w, after)
    return [parts[RANKS * quad : RANKS * (quad + 1)] for quad in range(4)], w


def gather_kernel(count, f_ref, *rest):
    token_refs, w_refs = rest[: RANKS * count], rest[RANKS * count : RANKS * (count + 1)]
    out_refs, (w_ref, w_v, sem) = rest[-3 - count : -3], rest[-3:]
    f = f_ref[0]
    weights = started([pltpu.make_async_copy(w_refs[turn], w_v.at[turn], sem.at[turn]) for turn in range(RANKS)])
    arriving = started(
        [
            pltpu.make_async_copy(ref, out_refs[n // RANKS].at[n % RANKS], sem.at[RANKS + n])
            for n, ref in enumerate(token_refs)
        ]
    )
    finish(weights)
    for row in range(RANKS):
        for column in range(RANKS):
            block = w_v[column, aligned((f ^ row) * LANES, LANES), :]
            w_ref[row * LANES : (row + 1) * LANES, column * LANES : (column + 1) * LANES] = block
    finish(arriving)


def gather(f, tokens, w):
    count = len(tokens)
    *parts, w = call(
        functools.partial(gather_kernel, count),
        "gather",
        [jax.ShapeDtypeStruct((RANKS, SQUARE, LANES), BF16)] * count + [jax.ShapeDtypeStruct((ALL, ALL), BF16)],
        [SMEM] + [ANY] * (RANKS * (count + 1)),
        [VMEM] * (count + 1),
        [pltpu.VMEM((RANKS, ALL, LANES), BF16), pltpu.SemaphoreType.DMA((RANKS * (count + 1),))],
        flops=0,
        moved=count * 2**21 + 2**20,
        grant=SMALL,
    )(f, *sum(tokens, []), *w)
    return parts, w


def project_kernel(first, count, f_ref, mixed_ref, w_ref, *rest):
    token_refs, out_refs = rest[:count], rest[-RANKS * count :]
    f = f_ref[0]
    tile = SQUARE // 2
    for quad in range(count):
        for half in range(2):
            rows, blocks = slice(half * tile, (half + 1) * tile), slice(half * 32, (half + 1) * 32)
            gated = []
            for turn in range(RANKS):
                mixed = mixed_ref[blocks, first + quad, :, aligned((f ^ turn) * LANES, LANES)].reshape(tile, LANES)
                value = token_refs[quad][turn, rows, :].astype(F32)
                gated.append((mixed.astype(F32) * (value / (1.0 + jnp.exp(-value)))).astype(BF16))
            result = jnp.dot(jnp.concatenate(gated, axis=1), w_ref[...], preferred_element_type=F32).astype(BF16)
            for turn in range(RANKS):
                out_refs[RANKS * quad + turn][rows, :] = result[:, turn * LANES : (turn + 1) * LANES]


def project(f, mixed, tokens, w, first, count, after):
    size = count * SQUARE * ALL
    parts = call(
        functools.partial(project_kernel, first, count),
        "project",
        [jax.ShapeDtypeStruct((SQUARE, LANES), BF16)] * (RANKS * count),
        [SMEM] + [VMEM] * (2 + count) + [ANY] * len(after),
        [VMEM] * (RANKS * count),
        [],
        flops=size * 1024,
        moved=size * 6,
        exps=size,
        grant=SMALL,
    )(f, mixed, w, *tokens[first : first + count], *after)
    return [parts[RANKS * quad : RANKS * (quad + 1)] for quad in range(count)]


def merge_kernel(first_row, f_ref, *rest):
    part_refs, (out_ref, done_ref, order_ref, held_v, out_sem) = rest[:RANKS], rest[-5:]
    count = part_refs[0].shape[0] // SQUARE
    done_ref[...] = jnp.zeros_like(done_ref)
    order_ref[...] = ones_where(place_of(iota((WIDE, WIDE), 1), f_ref[0]) == iota((WIDE, WIDE), 0))
    leaving = []
    for quad in range(count):
        for step in range(4):
            blocks = []
            for one in range(4):
                start = quad * SQUARE + step * 256 + one * 64
                rows = [ref[start : start + 64, :] for ref in part_refs]
                blocks.append(jnp.concatenate(rows, axis=0))
            held = jnp.concatenate(blocks, axis=1)
            moved = jnp.dot(order_ref[...], held, preferred_element_type=F32).astype(BF16)
            for p in range(4):
                for one in range(4):
                    block = moved[p * 64 : p * 64 + 64, one * LANES : (one + 1) * LANES]
                    start = p * SQUARE + step * 256 + one * 64
                    held_v[quad, start : start + 64, :] = block
                rows = pl.ds(p * SQUARE + step * 256, 256)
                target = out_ref.at[pl.ds(first_row + (quad * 4 + p) * SQUARE + step * 256, 256), :]
                leaving += started(
                    [pltpu.make_async_copy(held_v.at[quad, rows, :], target, out_sem.at[quad, step * 4 + p])]
                )
    finish(leaving)


def merge(f, parts, total, first_quad, base, after):
    rows = parts[0].shape[0]
    count = rows // SQUARE
    extra = [] if base is None else [base]
    return call(
        functools.partial(merge_kernel, first_quad * 4 * SQUARE),
        "merge",
        (jax.ShapeDtypeStruct((total, LANES), BF16), DONE),
        [SMEM] + [VMEM] * RANKS + [ANY] * (len(extra) + len(after)),
        (ANY, VMEM),
        [
            pltpu.VMEM((WIDE, WIDE), BF16),
            pltpu.VMEM((count, 4 * SQUARE, LANES), BF16),
            pltpu.SemaphoreType.DMA((count, 16)),
        ],
        flops=rows * 4 * WIDE * LANES * 2,
        moved=rows * LANES * 16,
        aliases={5: 0} if extra else None,
        grant=SMALL,
    )(f, *parts, *extra, *after)


TURNS = [[(rank, rank ^ turn) for rank in range(RANKS)] for turn in range(RANKS)]


def swap(parts):
    return [parts[0]] + [lax.ppermute(parts[turn], "fsdp", TURNS[turn]) for turn in (2, 1, 3)]


def in_turn(got):
    return [got[0], got[2], got[1], got[3]]


def hold_kernel(x_ref, after_ref, out_ref):
    pass


def hold(x, after):
    return call(
        hold_kernel,
        "hold",
        jax.ShapeDtypeStruct(x.shape, x.dtype),
        [ANY, ANY],
        ANY,
        [],
        flops=0,
        moved=0,
        aliases={0: 0},
        grant=SMALL,
    )(x, after)


def share(x):
    chip = lax.ppermute(x, "fsdp", TURNS[2])
    core = lax.ppermute(x, "fsdp", TURNS[1])
    far = lax.ppermute(chip, "fsdp", TURNS[1])
    return [x, core, chip, far]


def body(tokens, factor_d, factor_c, factor_b, factor_a, w_proj):
    local_rows = tokens.shape[0]
    f = lax.axis_index("fsdp").astype(jnp.int32).reshape(1)

    raw = lambda factor: factor.transpose(1, 2, 0).reshape(SQUARE, LANES)

    own = (raw(factor_d), raw(factor_c))
    core = [lax.ppermute(x, "fsdp", TURNS[1]) for x in own]
    chip = [lax.ppermute(x, "fsdp", TURNS[2]) for x in own]
    second, _ = local_steps(f, tokens, *own, None)
    second, done = local_steps(f ^ 1, tokens, *core, second)
    chip = [hold(x, done) for x in chip]
    far = [lax.ppermute(x, "fsdp", TURNS[1]) for x in chip]
    second, _ = local_steps(f ^ 2, tokens, *chip, second)
    second, _ = local_steps(f ^ 3, tokens, *far, second)
    token_parts, w = split(f, tokens, w_proj, second)
    w = share(w)
    token_parts = [in_turn(swap(quad)) for quad in token_parts]
    arrived = lax.all_to_all(
        second.reshape(64 * RANKS, 64, LANES), ("ctx", "fsdp"), split_axis=0, concat_axis=0, tiled=True
    )
    ready = weights(raw(factor_b), raw(factor_a), second)
    early = [part for quad in token_parts[:3] for part in quad[1:]]
    third, first_sent = middle(
        arrived.reshape(BLK, 2, RANKS, 64, LANES), raw(factor_b), ready, RETURN_QUADS[0], early + w[1:]
    )

    out, first_quad, after = None, 0, []
    gathered = [gather(f, token_parts[:2], w), gather(f, token_parts[2:], w)]
    for k, count in enumerate(RETURN_QUADS):
        sent = step_a(third, raw(factor_a), first_quad, count, token_parts[3][1:] + [gathered[0][1]]) if k else first_sent
        mixed = lax.all_to_all(
            sent.reshape(64, count * 16, ALL), "ctx", split_axis=0, concat_axis=0, tiled=True
        ).reshape(64, count, 16, ALL)
        tokens_here, w_here = gathered[k]
        parts, size = [], count
        for slot in range(0, count, size):
            here = project(f, mixed, tokens_here, w_here, slot, size, after)
            parts += [in_turn(swap(part)) for part in here]
        ends = []
        for part in parts:
            out, done = merge(f, part, local_rows, first_quad, out, [] if first_quad else [gathered[1][1]])
            first_quad += 1
            ends.append(done)
        after = ends[:1]
    return out


def solution(mesh):
    in_specs = (
        P("ctx", "fsdp"),
        P(("ctx", "fsdp"), None, None),
        P(("ctx", "fsdp"), None, None),
        P(("ctx", "fsdp"), None, None),
        P(("ctx", "fsdp"), None, None),
        P(None, "fsdp"),
    )
    out_specs = P("ctx", "fsdp")
    return jax.shard_map(body, mesh=mesh, in_specs=in_specs, out_specs=out_specs, check_vma=False)
```
